512 devices in a mesh: tile: 32 (over y_hi, z, core), layer: 16 (over x, y_lo).
Axes of the slice: x: 4, y: 8 (y_hi: 2, y_lo: 4; y = y_hi * 4 + y_lo), z: 8, core: 2. Of those that a mesh axis runs over, the one named last changes fastest.
Arguments:
- pressure: float32 [64, 256, 2048], P('layer', 'tile'), may hold values from -4 to -0.5
- old_pressure: float32 [64, 256, 2048], P('layer', 'tile'), may hold values from -4 to -0.5
- texture: int32 [64, 256, 2048], P('layer', 'tile'), may hold values from 0 to 11
- zones: int32 [256, 2048], P('tile'), may hold values from 0 to 15
- rates: float32 [16], replicated, may hold values from 0.05 to 0.5
- vg_table: float32 [5, 12], replicated, may hold values from 0.03 to 3, as said below
- approx_inverse: float32 [64, 64], replicated, may hold values from -0.2 to 0.36, as said below
Outputs:
- new_pressure: float32 [64, 256, 2048], P('layer', 'tile')
The draws below stay inside these ranges and needn't reach their ends.
Inputs may be any that keep to these rules, and one draw needn't show every extreme that they name: `vg_table`: rows are inverse scale in 0.5 to 3, n in 1.3 to 2.7, residual content in 0.03 to 0.1, saturated content in 0.35 to 0.5, saturated conductivity in 0.05 to 0.5. `approx_inverse`: diagonal in 0.24 to 0.36, off-diagonal entries of deviation 0.02.
All inputs are finite; a program needn't handle non-finite values.
Results may differ from the reference program's by a relative error of at most 0.0001.
Values sent between devices are 32-bit elements; how exact they have to be, the bound alone decides.
A program may use at most 64 MiB of HBM per device.

```python
import jax
import jax.numpy as jnp
from jax import lax

NZ = 64
CLASSES = 12
ZONES = 16
ITERS = 3
SWEEPS = 2
NY = 2048
NX = 256


def draw_vg_table(key, part):
    key = jax.random.fold_in(key, 11)
    lower = jnp.array([0.5, 1.3, 0.03, 0.35, 0.05], jnp.float32)
    upper = jnp.array([3.0, 2.7, 0.1, 0.5, 0.5], jnp.float32)
    unit = jax.random.uniform(key, (5, CLASSES), jnp.float32)
    return lower[:, None] + (upper - lower)[:, None] * unit


def draw_approx_inverse(key, part):
    key = jax.random.fold_in(key, 23)
    first, second = jax.random.split(key)
    diagonal = 0.3 * jax.random.uniform(first, (NZ,), jnp.float32, 0.8, 1.2)
    offdiag = jnp.clip(0.02 * jax.random.normal(second, (NZ, NZ), jnp.float32), -0.2, 0.2)
    return offdiag * (1.0 - jnp.eye(NZ, dtype=jnp.float32)) + jnp.diag(diagonal)


def set_ends(result, stream_key, smallest, largest):
    place = [jax.random.randint(jax.random.fold_in(stream_key, axis), (), 0, length) for axis, length in enumerate(result.shape)]
    widest = result.shape.index(max(result.shape))
    next_to = place[:widest] + [(place[widest] + 1) % result.shape[widest]] + place[widest + 1:]
    return result.at[tuple(place)].set(smallest).at[tuple(next_to)].set(largest)


def steps_of(own_key, dims, cuts, least, high):
    factor_of, own = 1.0, jax.random.fold_in(own_key, 6)
    for position, shards_of in cuts:
        heights = jnp.exp(jax.random.uniform(jax.random.fold_in(own, position), (shards_of,), jnp.float32, least / len(cuts), high / len(cuts)))
        factor_of = factor_of * jnp.repeat(heights, dims[position] // shards_of).reshape([-1 if axis == position else 1 for axis in range(len(dims))])
    return factor_of


def setup_inputs(seed: int = 0) -> dict:
    key_list = jax.random.split(jax.random.key(seed), 8)
    return {
        "pressure": jnp.clip(-4.0 + 3.5 * jax.random.uniform(key_list[0], (NZ, NX, NY), jnp.float32) ** steps_of(key_list[0], (NZ, NX, NY), ((0, 16), (1, 32)), -0.2, 0.2), -4.0, -0.5),
        "old_pressure": jnp.clip(-4.0 + 3.5 * jax.random.uniform(key_list[1], (NZ, NX, NY), jnp.float32) ** steps_of(key_list[1], (NZ, NX, NY), ((0, 16), (1, 32)), -0.2, 0.2), -4.0, -0.5),
        "texture": set_ends(jax.random.randint(key_list[2], (NZ, NX, NY), 0, CLASSES), jax.random.fold_in(key_list[2], 1), 0, CLASSES - 1).astype(jnp.int32),
        "zones": set_ends(jax.random.randint(key_list[3], (NX, NY), 0, ZONES), jax.random.fold_in(key_list[3], 1), 0, ZONES - 1).astype(jnp.int32),
        "rates": jnp.clip(jax.random.uniform(key_list[4], (ZONES,), jnp.float32, 0.05, 0.5), 0.05, 0.5),
        "vg_table": draw_vg_table(jax.random.fold_in(key_list[7], 71), 0),
        "approx_inverse": draw_approx_inverse(jax.random.fold_in(key_list[7], 71), 0),
    }


DT = 1.0
DZ = 1.0
OMEGA = 0.2


def closures(pressure, params):
    inv_scale, exponent, residual_wc, saturated_wc, saturated_k = params
    suction = jax.nn.softplus(-pressure)
    power = 1.0 - 1.0 / exponent
    saturation = (1.0 + (inv_scale * suction) ** exponent) ** (-power)
    moisture = residual_wc + (saturated_wc - residual_wc) * saturation
    conduct = saturated_k * saturation * saturation * saturation
    return moisture, conduct


def misfit_of(pressure, moisture_old, params, inflow):
    moisture, conduct = closures(pressure, params)
    interface = 0.5 * (conduct[:-1] + conduct[1:])
    inner = interface * ((pressure[:-1] - pressure[1:]) / DZ + 1.0)
    fluxes = jnp.concatenate([inflow[None], inner, conduct[-1:]], axis=0)
    return (moisture - moisture_old) / DT + (fluxes[1:] - fluxes[:-1]) / DZ


def lateral(pressure, params):
    moisture, conduct = closures(pressure, params)
    flow_x = 0.5 * (conduct[:, 1:] + conduct[:, :-1]) * (pressure[:, 1:] - pressure[:, :-1])
    change = jnp.pad(flow_x, ((0, 0), (0, 1), (0, 0))) - jnp.pad(flow_x, ((0, 0), (1, 0), (0, 0)))
    flow_y = 0.5 * (conduct[:, :, 1:] + conduct[:, :, :-1]) * (pressure[:, :, 1:] - pressure[:, :, :-1])
    change = change + (jnp.pad(flow_y, ((0, 0), (0, 0), (0, 1))) - jnp.pad(flow_y, ((0, 0), (0, 0), (1, 0))))
    return pressure + OMEGA * change


def reference(pressure, old_pressure, texture, zones, rates, vg_table, approx_inverse):
    params = tuple(vg_table[j][texture] for j in range(5))
    moisture_old, unused = closures(old_pressure, params)
    inflow = rates[zones]
    for newton_index in range(ITERS):
        misfit = misfit_of(pressure, moisture_old, params, inflow)
        update = jnp.dot(approx_inverse, misfit.reshape(NZ, -1), precision=lax.Precision.HIGHEST)
        pressure = pressure - update.reshape(misfit.shape)
    for sweep_index in range(SWEEPS):
        pressure = lateral(pressure, params)
    return pressure
```

```python
import functools

import jax
import jax.numpy as jnp
from jax import lax
from jax.experimental import pallas as pl
from jax.experimental.pallas import tpu as pltpu
from jax.sharding import PartitionSpec as P

ITERS = 3
SWEEPS = 2
OMEGA = 0.2
LOG2E = 1.4426950408889634
MESH = pl.DeviceIdType.MESH
LANES = 128
F32 = jnp.float32


def saturation(head, la, n, negp):
    suction = jnp.log(1.0 + jnp.exp2(jnp.abs(head) * (-LOG2E))) + jnp.maximum(-head, 0.0)
    power = jnp.exp2(n * jnp.log(suction) + la)
    return jnp.exp2(negp * jnp.log(1.0 + power))


def pick(row, index):
    parts = []
    for k in range(index.shape[0] // 8):
        parts.append(
            jnp.take_along_axis(row, index[8 * k : 8 * k + 8], axis=1, mode="promise_in_bounds")
        )
    return parts[0] if len(parts) == 1 else jnp.concatenate(parts, axis=0)


def pick_wide(row, index):
    parts = []
    for k in range(index.shape[1] // LANES):
        parts.append(
            jnp.take_along_axis(
                row, index[:, k * LANES : (k + 1) * LANES], axis=1, mode="promise_in_bounds"
            )
        )
    return parts[0] if len(parts) == 1 else jnp.concatenate(parts, axis=1)


def kernel(
    count,
    tiles,
    press,
    old,
    tex,
    zones,
    rates,
    table,
    inverse,
    out,
    old_v,
    tex_v,
    mold_v,
    own,
    halo,
    own2,
    halo2,
    tex_h,
    cond_o,
    cond_h,
    par_o,
    par_h,
    pack_ts,
    pack_tr,
    pack_hs,
    pack_hr,
    col_h,
    col_t,
    col_m,
    par_c,
    cond_c,
    flux_c,
    mis_c,
    zone_v,
    rate_v,
    table_v,
    tab,
    inv_v,
    loc_sem,
    own_sem,
    send_sem,
    recv_sem,
    hsend_sem,
    hrecv_sem,
):
    me = lax.axis_index("layer")
    tile = lax.axis_index("tile")
    rows = press.shape[0]
    width = press.shape[1]
    layers = count * rows // 8
    own_rows = rows // 8
    down = lax.rem(tile + tiles - 1, tiles)
    up = lax.rem(tile + 1, tiles)

    def peer_of(k):
        return lax.rem(me + k, count)

    barrier = pltpu.get_barrier_semaphore()

    def greet(k, carry):
        pl.semaphore_signal(
            barrier, inc=1, device_id={"layer": peer_of(k)}, device_id_type=MESH
        )
        return carry

    lax.fori_loop(1, count, greet, 0)
    pl.semaphore_signal(barrier, inc=1, device_id={"tile": down}, device_id_type=MESH)
    pl.semaphore_signal(barrier, inc=1, device_id={"tile": up}, device_id_type=MESH)

    my_cols = pl.ds(pl.multiple_of(me * LANES, LANES), LANES)
    my_rows = pl.ds(pl.multiple_of(me * rows, rows), rows)
    loads = [
        pltpu.make_async_copy(old, old_v, loc_sem.at[0]),
        pltpu.make_async_copy(tex, tex_v, loc_sem.at[1]),
        pltpu.make_async_copy(table, table_v, loc_sem.at[2]),
        pltpu.make_async_copy(inverse, inv_v, loc_sem.at[3]),
        pltpu.make_async_copy(zones.at[:, my_cols], zone_v, loc_sem.at[4]),
        pltpu.make_async_copy(rates, rate_v, loc_sem.at[5]),
    ]
    for load in loads:
        load.start()
    own_h = pltpu.make_async_copy(press.at[:, my_cols], col_h.at[my_rows], own_sem.at[0])
    own_t = pltpu.make_async_copy(tex.at[:, my_cols], col_t.at[my_rows], own_sem.at[1])
    own_h.start()
    own_t.start()

    def scatter(src, dst, slot):
        def send(k, carry):
            peer = peer_of(k)
            cols = pl.ds(pl.multiple_of(peer * LANES, LANES), LANES)
            pltpu.make_async_remote_copy(
                src_ref=src.at[:, cols],
                dst_ref=dst.at[my_rows],
                send_sem=send_sem.at[slot],
                recv_sem=recv_sem.at[slot],
                device_id={"layer": peer},
                device_id_type=MESH,
            ).start()
            return carry

        lax.fori_loop(1, count, send, 0)

    def arrived(dst, slot):
        part = dst.at[pl.ds(0, (count - 1) * rows)]
        pltpu.make_async_copy(part, part, recv_sem.at[slot]).wait()

    def sent(dst, slot):
        part = dst.at[pl.ds(0, (count - 1) * rows)]
        pltpu.make_async_copy(part, part, send_sem.at[slot]).wait()

    pl.semaphore_wait(barrier, count - 1 + 2)
    scatter(press, col_h, 0)
    scatter(tex, col_t, 1)

    loads[2].wait()
    tab[...] = jnp.ones(tab.shape, F32)
    tab[0:5, 0 : table.shape[1]] = table_v[...]
    t_a, t_n, t_r, t_s, t_k = (tab[j : j + 1, :] for j in range(5))

    def full(row):
        return jnp.broadcast_to(row, (8, LANES))

    tab_la = full(t_n * jnp.log(t_a) * LOG2E)
    tab_n = full(t_n * LOG2E)
    tab_p = full((1.0 / t_n - 1.0) * LOG2E)
    tab_r = full(t_r)
    tab_d = full(t_s - t_r)
    tab_k = full(t_k)

    loads[1].wait()
    for l in range(own_rows):
        pack_ts[0, 2 * l : 2 * l + 2, :] = tex_v[8 * l : 8 * l + 2, :]
        pack_ts[1, 2 * l : 2 * l + 2, :] = tex_v[8 * l + 6 : 8 * l + 8, :]

    def halo_copies(src, dst, slot):
        copies = []
        for side, device in ((0, down), (1, up)):
            copies.append(
                pltpu.make_async_remote_copy(
                    src_ref=src.at[side],
                    dst_ref=dst.at[side],
                    send_sem=hsend_sem.at[slot, side],
                    recv_sem=hrecv_sem.at[slot, side],
                    device_id={"tile": device},
                    device_id_type=MESH,
                )
            )
        return copies

    tex_copies = halo_copies(pack_ts, pack_tr, 0)
    for copy in tex_copies:
        copy.start()

    loads[0].wait()
    chunk = 512
    per_row = width // chunk

    def old_step(i, carry):
        r = pl.ds(pl.multiple_of(lax.div(i, per_row) * 8, 8), 8)
        c = pl.ds(pl.multiple_of(lax.rem(i, per_row) * chunk, chunk), chunk)
        index = tex_v[r, c]
        la, n, negp = pick_wide(tab_la, index), pick_wide(tab_n, index), pick_wide(tab_p, index)
        sat = saturation(old_v[r, c], la, n, negp)
        mold_v[r, c] = pick_wide(tab_r, index) + pick_wide(tab_d, index) * sat
        par_o[0, r, c] = la
        par_o[1, r, c] = n
        par_o[2, r, c] = negp
        par_o[3, r, c] = pick_wide(tab_k, index)
        return carry

    lax.fori_loop(0, own_rows * per_row, old_step, 0)
    scatter(mold_v, col_m, 2)
    own_m = pltpu.make_async_copy(mold_v.at[:, my_cols], col_m.at[my_rows], own_sem.at[2])
    own_m.start()

    for copy in tex_copies:
        copy.wait()
    tex_h[...] = jnp.zeros(tex_h.shape, jnp.int32)
    halo[...] = jnp.zeros(halo.shape, F32)
    for l in range(own_rows):
        tex_h[8 * l : 8 * l + 2, :] = pack_tr[0, 2 * l : 2 * l + 2, :]
        tex_h[8 * l + 6 : 8 * l + 8, :] = pack_tr[1, 2 * l : 2 * l + 2, :]

    def halo_step(i, carry):
        r = pl.ds(pl.multiple_of(lax.div(i, per_row) * 8, 8), 8)
        c = pl.ds(pl.multiple_of(lax.rem(i, per_row) * chunk, chunk), chunk)
        index = tex_h[r, c]
        for j, row in enumerate((tab_la, tab_n, tab_p, tab_k)):
            par_h[j, r, c] = pick_wide(row, index)
        return carry

    lax.fori_loop(0, own_rows * per_row, halo_step, 0)

    block = 64
    blocks = layers * 8 // block
    own_t.wait()
    arrived(col_t, 1)

    def par_step(i, carry):
        r = pl.ds(pl.multiple_of(i * block, block), block)
        index = col_t[r, :]
        for j, row in enumerate((tab_la, tab_n, tab_p, tab_k, tab_r, tab_d)):
            par_c[j, r, :] = pick(row, index)
        return carry

    lax.fori_loop(0, blocks, par_step, 0)
    loads[4].wait()
    loads[5].wait()
    tab[0:1, 0 : rates.shape[1]] = rate_v[...]
    flux_c[0:8, :] = pick(full(tab[0:1, :]), zone_v[...])
    loads[3].wait()
    inv = inv_v[...]
    inv_hi = inv.astype(jnp.bfloat16)
    inv_lo = (inv - inv_hi.astype(F32)).astype(jnp.bfloat16)
    inv_all = jnp.concatenate([inv_hi, inv_lo, inv_hi, inv_lo], axis=1)
    own_h.wait()
    arrived(col_h, 0)

    def closure_step(i, carry):
        r = pl.ds(pl.multiple_of(i * block, block), block)
        sat = saturation(col_h[r, :], par_c[0, r, :], par_c[1, r, :], par_c[2, r, :])
        cond_c[r, :] = par_c[3, r, :] * (sat * sat * sat)
        mis_c[r, :] = sat
        return carry

    def newton(first):
        lax.fori_loop(0, blocks, closure_step, 0)
        if first:
            own_m.wait()
            arrived(col_m, 2)

            def mold_step(i, carry):
                r = pl.ds(pl.multiple_of(i * block, block), block)
                col_m[r, :] = col_m[r, :] - par_c[4, r, :]
                return carry

            lax.fori_loop(0, blocks, mold_step, 0)
        last = layers * 8
        cond_c[last : last + 8, :] = cond_c[last - 8 : last, :]
        col_h[last : last + 8, :] = col_h[last - 8 : last, :]

        def flux_step(i, carry):
            start = pl.multiple_of(i * block, block)
            r = pl.ds(start, block)
            b = pl.ds(pl.multiple_of(start + 8, 8), block)
            below = (0.5 * (cond_c[r, :] + cond_c[b, :])) * (col_h[r, :] - col_h[b, :] + 1.0)
            flux_c[b, :] = below
            above = jnp.concatenate([flux_c[pl.ds(start, 8), :], below[: block - 8]], axis=0)
            moist = par_c[5, r, :] * mis_c[r, :] - col_m[r, :]
            mis_c[r, :] = moist + (below - above)
            return carry

        lax.fori_loop(0, blocks, flux_step, 0)
        for y in range(0, 8, 2):
            x = jnp.concatenate(
                [mis_c[pl.ds(y + j, layers, stride=8), :] for j in range(2)], axis=1
            )
            hi = x.astype(jnp.bfloat16)
            lo = (x - hi.astype(F32)).astype(jnp.bfloat16)
            stacked = jnp.concatenate([hi, hi, lo, lo], axis=0)
            update = jnp.dot(inv_all, stacked, preferred_element_type=F32)
            for j in range(2):
                at = pl.ds(y + j, layers, stride=8)
                col_h[at, :] = col_h[at, :] - update[:, j * LANES : (j + 1) * LANES]

    newton(True)

    def again(i, carry):
        newton(False)
        return carry

    lax.fori_loop(1, ITERS, again, 0)

    own_b = pltpu.make_async_copy(col_h.at[my_rows], own.at[:, my_cols], own_sem.at[3])
    own_b.start()

    def send_back(k, carry):
        peer = peer_of(k)
        pltpu.make_async_remote_copy(
            src_ref=col_h.at[pl.ds(pl.multiple_of(peer * rows, rows), rows)],
            dst_ref=own.at[:, my_cols],
            send_sem=send_sem.at[3],
            recv_sem=recv_sem.at[3],
            device_id={"layer": peer},
            device_id_type=MESH,
        ).start()
        return carry

    lax.fori_loop(1, count, send_back, 0)
    own_b.wait()
    part = own.at[:, pl.ds(0, (count - 1) * LANES)]
    pltpu.make_async_copy(part, part, recv_sem.at[3]).wait()

    for l in range(own_rows):
        pack_hs[0, 2 * l : 2 * l + 2, :] = own[8 * l : 8 * l + 2, :]
        pack_hs[1, 2 * l : 2 * l + 2, :] = own[8 * l + 6 : 8 * l + 8, :]
    head_copies = halo_copies(pack_hs, pack_hr, 1)
    for copy in head_copies:
        copy.start()

    def cond_pass(src, par, dst):
        def step(i, carry):
            r = pl.ds(pl.multiple_of(lax.div(i, per_row) * 8, 8), 8)
            c = pl.ds(pl.multiple_of(lax.rem(i, per_row) * chunk, chunk), chunk)
            sat = saturation(src[r, c], par[0, r, c], par[1, r, c], par[2, r, c])
            dst[r, c] = par[3, r, c] * (sat * sat * sat)
            return carry

        lax.fori_loop(0, own_rows * per_row, step, 0)

    cond_pass(own, par_o, cond_o)
    for copy in head_copies:
        copy.wait()
    for l in range(own_rows):
        halo[8 * l : 8 * l + 2, :] = pack_hr[0, 2 * l : 2 * l + 2, :]
        halo[8 * l + 6 : 8 * l + 8, :] = pack_hr[1, 2 * l : 2 * l + 2, :]

    sub = lax.broadcasted_iota(jnp.int32, (8, width), 0)
    lane = lax.broadcasted_iota(jnp.int32, (8, width), 1)
    right_end = lane == width - 1
    cut_top = jnp.logical_and(sub == 7, tile == tiles - 1)
    cut_bottom = jnp.logical_and(sub == 7, tile == 0)

    def flow(h, c, hn, cn):
        return (0.5 * (c + cn)) * (hn - h)

    def sweep(src_o, src_h, dst_o, dst_h):
        cond_pass(src_h, par_h, cond_h)
        if dst_h is None:
            cond_pass(src_o, par_o, cond_o)

        def step(l, carry):
            r = pl.ds(pl.multiple_of(l * 8, 8), 8)
            h, c, g, e = src_o[r, :], cond_o[r, :], src_h[r, :], cond_h[r, :]

            def next_row(a, b):
                return pltpu.roll(jnp.where(sub == 0, b, a), 7, 0)

            f = jnp.where(cut_top, 0.0, flow(h, c, next_row(h, g), next_row(c, e)))
            fh = jnp.where(cut_bottom, 0.0, flow(g, e, next_row(g, h), next_row(e, c)))

            def across(a, k):
                x = flow(a, k, pltpu.roll(a, width - 1, 1), pltpu.roll(k, width - 1, 1))
                x = jnp.where(right_end, 0.0, x)
                return x - pltpu.roll(x, 1, 1)

            change = f - pltpu.roll(jnp.where(sub == 7, fh, f), 1, 0) + across(h, c)
            dst_o[r, :] = h + OMEGA * change
            if dst_h is not None:
                change = fh - pltpu.roll(jnp.where(sub == 7, f, fh), 1, 0) + across(g, e)
                dst_h[r, :] = g + OMEGA * change
            return carry

        lax.fori_loop(0, own_rows, step, 0)

    sweep(own, halo, own2, halo2)
    sweep(own2, halo2, own, None)
    store = pltpu.make_async_copy(own, out, own_sem.at[4])
    store.start()
    sent(col_h, 0)
    sent(col_t, 1)
    sent(col_m, 2)
    sent(col_h, 3)
    store.wait()


def body(pressure, old_pressure, texture, zones, rates, vg_table, approx_inverse):
    count = lax.axis_size("layer")
    tiles = lax.axis_size("tile")
    depth, tall, width = pressure.shape
    rows = depth * tall
    total = rows * count
    flat = (rows, width)

    def vmem(*shape, dtype=F32):
        return pltpu.VMEM(shape, dtype)

    result = pl.pallas_call(
        functools.partial(kernel, count, tiles),
        out_shape=jax.ShapeDtypeStruct(flat, F32),
        in_specs=[pl.BlockSpec(memory_space=pl.ANY)] * 7,
        out_specs=pl.BlockSpec(memory_space=pl.ANY),
        scratch_shapes=[
            vmem(*flat),
            vmem(*flat, dtype=jnp.int32),
            vmem(*flat),
            vmem(*flat),
            vmem(*flat),
            vmem(*flat),
            vmem(*flat),
            vmem(*flat, dtype=jnp.int32),
            vmem(*flat),
            vmem(*flat),
            vmem(4, *flat),
            vmem(4, *flat),
            vmem(2, 2 * depth, width, dtype=jnp.int32),
            vmem(2, 2 * depth, width, dtype=jnp.int32),
            vmem(2, 2 * depth, width),
            vmem(2, 2 * depth, width),
            vmem(total + 8, LANES),
            vmem(total, LANES, dtype=jnp.int32),
            vmem(total, LANES),
            vmem(6, total, LANES),
            vmem(total + 8, LANES),
            vmem(total + 8, LANES),
            vmem(total, LANES),
            vmem(tall, LANES, dtype=jnp.int32),
            vmem(1, rates.shape[0]),
            vmem(*vg_table.shape),
            vmem(8, LANES),
            vmem(*approx_inverse.shape),
            pltpu.SemaphoreType.DMA((6,)),
            pltpu.SemaphoreType.DMA((5,)),
            pltpu.SemaphoreType.DMA((4,)),
            pltpu.SemaphoreType.DMA((4,)),
            pltpu.SemaphoreType.DMA((2, 2)),
            pltpu.SemaphoreType.DMA((2, 2)),
        ],
        compiler_params=pltpu.CompilerParams(
            collective_id=0, has_side_effects=True, vmem_limit_bytes=48 * 1024 * 1024
        ),
    )(
        pressure.reshape(flat),
        old_pressure.reshape(flat),
        texture.reshape(flat),
        zones,
        rates.reshape(1, -1),
        vg_table,
        approx_inverse,
    )
    return result.reshape(pressure.shape)


def solution(mesh):
    placed = (
        P("layer", "tile", None),
        P("layer", "tile", None),
        P("layer", "tile", None),
        P("tile", None),
        P(),
        P(),
        P(),
    )
    return jax.shard_map(
        body, mesh=mesh, in_specs=placed, out_specs=P("layer", "tile", None), check_vma=False
    )
```

```python
import functools

import jax
import jax.numpy as jnp
from jax import lax
from jax.experimental import pallas as pl
from jax.experimental.pallas import tpu as pltpu
from jax.sharding import PartitionSpec as P

ITERS = 3
OMEGA = 0.2
LOG2E = 1.4426950408889634
MESH = pl.DeviceIdType.MESH
LANES = 128
CHUNKS = 4
FIELDS = 3
F32 = jnp.float32


def saturation(head, la, n, negp):
    suction = jnp.log(1.0 + jnp.exp2(jnp.abs(head) * (-LOG2E))) + jnp.maximum(-head, 0.0)
    power = jnp.exp2(n * jnp.log(suction) + la)
    return jnp.exp2(negp * jnp.log(1.0 + power))


def exchange(tiles):
    sub = lax.broadcasted_iota(jnp.int32, tiles[0].shape, 0)
    low, even = sub < 4, (sub & 2) == 0
    a, b, c, d = tiles

    def halves(p, q):
        r = pltpu.roll(jnp.where(low, q, p), 4, 0)
        return jnp.where(low, p, r), jnp.where(low, r, q)

    def pairs(p, q):
        return (
            jnp.where(even, p, pltpu.roll(q, 2, 0)),
            jnp.where(even, pltpu.roll(p, 6, 0), q),
        )

    a, c = halves(a, c)
    b, d = halves(b, d)
    a, b = pairs(a, b)
    c, d = pairs(c, d)
    return a, b, c, d


def lookup(splat, classes, row, index, masks):
    def constant(k):
        tile = splat[row, min(k, classes - 1)]
        if len(index.shape) == 2:
            return jnp.concatenate([tile] * (index.shape[1] // LANES), axis=1)
        return jnp.broadcast_to(tile[None], index.shape)

    level = [constant(k) for k in range(classes)]
    for mask in masks:
        level = [
            jnp.where(mask, level[k + 1], level[k]) if k + 1 < len(level) else level[k]
            for k in range(0, len(level), 2)
        ]
    return level[0]


def bits(index, classes):
    return [(index & (1 << b)) != 0 for b in range((classes - 1).bit_length())]


def kernel(
    count,
    tiles,
    press,
    old,
    tex,
    zones,
    rates,
    table,
    inverse,
    out,
    nat_h,
    nat_o,
    nat_t,
    stage,
    colb,
    hcur,
    par_c,
    mold_c,
    mis_c,
    upd_c,
    ghost,
    lay,
    lay2,
    cond,
    swap_h,
    swap_c,
    par_l,
    tex_h,
    fin,
    zone_v,
    rate_v,
    table_v,
    tab,
    splat,
    inv_v,
    load_sem,
    in_send,
    in_recv,
    back_send,
    back_recv,
    halo_send,
    halo_recv,
    tex_send,
    tex_recv,
):
    me = lax.axis_index("layer")
    tile = lax.axis_index("tile")
    width = press.shape[1]
    depth = press.shape[0] // 8
    classes = table.shape[1]
    layers = count * depth
    down = lax.rem(tile + tiles - 1, tiles)
    up = lax.rem(tile + 1, tiles)
    wide = 512
    blocks = width // wide

    def peer_of(k):
        return lax.rem(me + k, count)

    def greet(k, carry):
        pl.semaphore_signal(
            pltpu.get_barrier_semaphore(),
            inc=1,
            device_id={"layer": peer_of(k)},
            device_id_type=MESH,
        )
        return carry

    def greet_down(k, carry):
        pl.semaphore_signal(
            pltpu.get_barrier_semaphore(),
            inc=1,
            device_id={"tile": down, "layer": peer_of(k)},
            device_id_type=MESH,
        )
        return carry

    lax.fori_loop(1, count, greet, 0)
    lax.fori_loop(0, count, greet_down, 0)

    my_cols = pl.ds(pl.multiple_of(me * LANES, LANES), LANES)
    loads = [
        pltpu.make_async_copy(table, table_v, load_sem.at[0]),
        pltpu.make_async_copy(press, nat_h, load_sem.at[1]),
        pltpu.make_async_copy(old, nat_o, load_sem.at[2]),
        pltpu.make_async_copy(tex, nat_t, load_sem.at[3]),
        pltpu.make_async_copy(inverse, inv_v, load_sem.at[4]),
        pltpu.make_async_copy(zones.at[:, my_cols], zone_v, load_sem.at[5]),
        pltpu.make_async_copy(rates, rate_v, load_sem.at[6]),
    ]
    for load in loads:
        load.start()

    loads[0].wait()
    tab[...] = jnp.ones(tab.shape, F32)
    tab[0:5, 0:classes] = table_v[...]
    t_a, t_n, t_r, t_s, t_k = (tab[j : j + 1, :] for j in range(5))
    derived = (
        t_n * jnp.log(t_a) * LOG2E,
        t_n * LOG2E,
        (1.0 / t_n - 1.0) * LOG2E,
        t_k,
        t_r,
        t_s - t_r,
    )
    for j, row in enumerate(derived):
        for k in range(classes):
            splat[j, k] = jnp.broadcast_to(row[:, k : k + 1], (8, LANES))

    for load in loads[1:4]:
        load.wait()

    def pack(b, carry):
        cols = pl.ds(pl.multiple_of(b * wide, wide), wide)
        for f, nat in enumerate((nat_h, nat_o, nat_t)):
            rows = [nat[8 * l : 8 * l + 8, cols] for l in range(depth)]
            if f == 2:
                rows = [r.astype(F32) for r in rows]
            for c, packed in enumerate(exchange(rows)):
                stage[c, 8 * f : 8 * f + 8, cols] = packed
        return carry

    lax.fori_loop(0, blocks, pack, 0)

    def params_of(texture, slot):
        def step(b, carry):
            cols = pl.ds(pl.multiple_of(b * wide, wide), wide)
            index = texture(cols).astype(jnp.int32)
            masks = bits(index, classes)
            for j in range(4):
                par_l[j, slot, :, cols] = lookup(splat, classes, j, index, masks)
            return carry

        lax.fori_loop(0, blocks, step, 0)

    for c in range(CHUNKS):
        params_of(lambda cols, c=c: stage[c, 16:24, cols], c + 1)

    pl.semaphore_wait(pltpu.get_barrier_semaphore(), count - 1 + count)

    order = (3, 0, 1, 2)
    for c in order:

        def send(k, carry, c=c):
            peer = peer_of(k)
            pltpu.make_async_remote_copy(
                src_ref=stage.at[c, :, pl.ds(pl.multiple_of(peer * LANES, LANES), LANES)],
                dst_ref=colb.at[c, me],
                send_sem=in_send.at[c],
                recv_sem=in_recv.at[c],
                device_id={"layer": peer},
                device_id_type=MESH,
            ).start()
            return carry

        lax.fori_loop(1, count, send, 0)
        if c == 3:
            tex_up = pltpu.make_async_remote_copy(
                src_ref=stage.at[3, pl.ds(16, 8)],
                dst_ref=tex_h.at[0],
                send_sem=tex_send.at[0],
                recv_sem=tex_recv.at[0],
                device_id={"tile": up},
                device_id_type=MESH,
            )
            tex_up.start()
        colb[c, me] = stage[c, :, my_cols]

    loads[5].wait()
    loads[6].wait()
    tab[0:1, 0 : rates.shape[1]] = rate_v[...]
    inflow = jnp.take_along_axis(
        jnp.broadcast_to(tab[0:1, :], (8, LANES)), zone_v[...], axis=1, mode="promise_in_bounds"
    )
    for c in range(CHUNKS):
        ghost[c] = pltpu.roll(inflow, (6 - 2 * c) % 8, 0)

    loads[4].wait()
    inv = inv_v[...]
    inv_hi = inv.astype(jnp.bfloat16)
    inv_lo = (inv - inv_hi.astype(F32)).astype(jnp.bfloat16)
    inv_all = jnp.concatenate([inv_hi, inv_lo, inv_hi], axis=1)

    shape = (count, 8, LANES)
    sub3 = lax.broadcasted_iota(jnp.int32, shape, 1)

    def below(x):
        last = pltpu.roll(x[count - 1 :], 2, 1)
        return pltpu.roll(jnp.where(sub3 < 2, jnp.concatenate([x[1:], last], axis=0), x), 6, 1)

    def newton(c):
        group = 4

        def params(g, carry):
            at = pl.ds(g * group, group)
            index = colb[c, at, 16:24, :].astype(jnp.int32)
            masks = bits(index, classes)
            values = [lookup(splat, classes, j, index, masks) for j in range(6)]
            for j in range(6):
                par_c[j, at] = values[j]
            sat = saturation(colb[c, at, 8:16, :], values[0], values[1], values[2])
            mold_c[at] = values[4] + values[5] * sat
            return carry

        lax.fori_loop(0, count // group, params, 0)
        hcur[c] = colb[c, :, 0:8, :].reshape(count * 8, LANES)

        def step(i, carry):
            h = hcur[c].reshape(shape)
            sat = saturation(h, par_c[0], par_c[1], par_c[2])
            k = par_c[3] * (sat * sat * sat)
            flux = (0.5 * (k + below(k))) * (h - below(h) + 1.0)
            shifted = jnp.concatenate([ghost[c][None], flux[:-1]], axis=0)
            above = pltpu.roll(jnp.where(sub3 >= 6, shifted, flux), 2, 1)
            moisture = par_c[4] + par_c[5] * sat
            misfit = (moisture - mold_c[...]) + (flux - above)
            mis_c[...] = misfit.reshape(count * 8, LANES)
            x = jnp.concatenate(
                [mis_c[pl.ds(y, layers, stride=2), :] for y in range(2)], axis=1
            )
            hi = x.astype(jnp.bfloat16)
            lo = (x - hi.astype(F32)).astype(jnp.bfloat16)
            stacked = jnp.concatenate([hi, hi, lo], axis=0)
            update = jnp.dot(inv_all, stacked, preferred_element_type=F32)
            for y in range(2):
                upd_c[pl.ds(y, layers, stride=2), :] = update[:, y * LANES : (y + 1) * LANES]
            hcur[c] = hcur[c] - upd_c[...]
            return carry

        lax.fori_loop(0, ITERS, step, 0)

    def tile_rows(peer):
        return pl.ds(pl.multiple_of(peer * 8, 8), 8)

    def send_halo(c, slot, side, device):
        def send(k, carry):
            peer = peer_of(k)
            pltpu.make_async_remote_copy(
                src_ref=hcur.at[c, tile_rows(peer)],
                dst_ref=lay.at[slot, :, my_cols],
                send_sem=halo_send.at[side],
                recv_sem=halo_recv.at[side],
                device_id={"tile": device, "layer": peer},
                device_id_type=MESH,
            ).start()
            return carry

        lax.fori_loop(0, count, send, 0)

    def send_back(c):
        def send(k, carry):
            peer = peer_of(k)
            pltpu.make_async_remote_copy(
                src_ref=hcur.at[c, tile_rows(peer)],
                dst_ref=lay.at[c + 1, :, my_cols],
                send_sem=back_send.at[c],
                recv_sem=back_recv.at[c],
                device_id={"layer": peer},
                device_id_type=MESH,
            ).start()
            return carry

        lax.fori_loop(1, count, send, 0)
        lay[c + 1, :, my_cols] = hcur[c, tile_rows(me), :]

    for c in order:
        part = colb.at[c, pl.ds(0, count - 1)]
        pltpu.make_async_copy(part, part, in_recv.at[c]).wait()
        newton(c)
        if c == 3:
            send_halo(3, 0, 0, up)
        send_back(c)

    tex_up.wait_recv()
    tex_down = pltpu.make_async_remote_copy(
        src_ref=stage.at[0, pl.ds(16, 8)],
        dst_ref=tex_h.at[1],
        send_sem=tex_send.at[1],
        recv_sem=tex_recv.at[1],
        device_id={"tile": down},
        device_id_type=MESH,
    )
    tex_down.start()
    send_halo(0, 5, 1, down)
    params_of(lambda cols: tex_h[0, :, cols], 0)

    def odd_rows(shape):
        return (lax.broadcasted_iota(jnp.int32, shape, 0) & 1) == 1

    def prepare(src, s):
        def step(b, carry):
            cols = pl.ds(pl.multiple_of(b * wide, wide), wide)
            h = src[s, :, cols]
            sat = saturation(h, par_l[0, s, :, cols], par_l[1, s, :, cols], par_l[2, s, :, cols])
            k = par_l[3, s, :, cols] * (sat * sat * sat)
            odd = odd_rows(h.shape)
            cond[s, :, cols] = k
            swap_h[s, :, cols] = jnp.where(odd, pltpu.roll(h, 1, 0), pltpu.roll(h, 7, 0))
            swap_c[s, :, cols] = jnp.where(odd, pltpu.roll(k, 1, 0), pltpu.roll(k, 7, 0))
            return carry

        lax.fori_loop(0, blocks, step, 0)

    def advance(src, dst, s):
        h, k = src[s], cond[s]
        lane = lax.broadcasted_iota(jnp.int32, h.shape, 1)
        flow = (k + pltpu.roll(k, width - 1, 1)) * (pltpu.roll(h, width - 1, 1) - h)
        flow = jnp.where(lane == width - 1, 0.0, flow)
        change = flow - pltpu.roll(flow, 1, 1)
        change = change + (k + swap_c[s]) * (swap_h[s] - h)
        odd = odd_rows(h.shape)
        after, before = min(s + 1, CHUNKS + 1), max(s - 1, 0)
        side_h = jnp.where(odd, swap_h[after], swap_h[before])
        side_c = jnp.where(odd, swap_c[after], swap_c[before])
        side = (k + side_c) * (side_h - h)
        if s == 1:
            side = jnp.where(jnp.logical_and(tile == 0, jnp.logical_not(odd)), 0.0, side)
        if s == CHUNKS:
            side = jnp.where(jnp.logical_and(tile == tiles - 1, odd), 0.0, side)
        dst[s] = h + (0.5 * OMEGA) * (change + side)

    for c in order:
        part = lay.at[c + 1, :, pl.ds(0, (count - 1) * LANES)]
        pltpu.make_async_copy(part, part, back_recv.at[c]).wait()
        prepare(lay, c + 1)
    tex_down.wait_recv()
    params_of(lambda cols: tex_h[1, :, cols], 5)
    pltpu.make_async_copy(lay.at[5], lay.at[5], halo_recv.at[1]).wait()
    prepare(lay, 5)
    for s in (2, 3, 4, 5):
        advance(lay, lay2, s)
    pltpu.make_async_copy(lay.at[0], lay.at[0], halo_recv.at[0]).wait()
    prepare(lay, 0)
    for s in (0, 1):
        advance(lay, lay2, s)
    for s in range(6):
        prepare(lay2, s)
    for s in (1, 2, 3, 4):
        advance(lay2, fin, s)

    def unpack(b, carry):
        cols = pl.ds(pl.multiple_of(b * wide, wide), wide)
        for l, rows in enumerate(exchange([fin[c + 1, :, cols] for c in range(CHUNKS)])):
            nat_h[8 * l : 8 * l + 8, cols] = rows
        return carry

    lax.fori_loop(0, blocks, unpack, 0)
    store = pltpu.make_async_copy(nat_h, out, load_sem.at[7])
    store.start()
    for c in range(CHUNKS):
        part = colb.at[c, pl.ds(0, count - 1)]
        pltpu.make_async_copy(part, part, in_send.at[c]).wait()
        part = hcur.at[c, pl.ds(0, (count - 1) * 8)]
        pltpu.make_async_copy(part, part, back_send.at[c]).wait()
    pltpu.make_async_copy(hcur.at[3], hcur.at[3], halo_send.at[0]).wait()
    pltpu.make_async_copy(hcur.at[0], hcur.at[0], halo_send.at[1]).wait()
    tex_up.wait_send()
    tex_down.wait_send()
    store.wait()


def body(pressure, old_pressure, texture, zones, rates, vg_table, approx_inverse):
    count = lax.axis_size("layer")
    tiles = lax.axis_size("tile")
    depth, tall, width = pressure.shape
    rows = depth * tall
    flat = (rows, width)
    slots = (CHUNKS + 2, 2 * depth, width)
    column = (count, 2 * depth, LANES)
    classes = vg_table.shape[1]

    def vmem(*shape, dtype=F32):
        return pltpu.VMEM(shape, dtype)

    result = pl.pallas_call(
        functools.partial(kernel, count, tiles),
        out_shape=jax.ShapeDtypeStruct(flat, F32),
        in_specs=[pl.BlockSpec(memory_space=pltpu.HBM)] * 7,
        out_specs=pl.BlockSpec(memory_space=pltpu.HBM),
        scratch_shapes=[
            vmem(*flat),
            vmem(*flat),
            vmem(*flat, dtype=jnp.int32),
            vmem(CHUNKS, FIELDS * 2 * depth, width),
            vmem(CHUNKS, count, FIELDS * 2 * depth, LANES),
            vmem(CHUNKS, count * 2 * depth, LANES),
            vmem(6, *column),
            vmem(*column),
            vmem(count * 2 * depth, LANES),
            vmem(count * 2 * depth, LANES),
            vmem(CHUNKS, 8, LANES),
            vmem(*slots),
            vmem(*slots),
            vmem(*slots),
            vmem(*slots),
            vmem(*slots),
            vmem(4, *slots),
            vmem(2, 2 * depth, width),
            vmem(*slots),
            vmem(tall, LANES, dtype=jnp.int32),
            vmem(1, rates.shape[0]),
            vmem(*vg_table.shape),
            vmem(8, LANES),
            vmem(6, classes, 8, LANES),
            vmem(*approx_inverse.shape),
            pltpu.SemaphoreType.DMA((8,)),
            pltpu.SemaphoreType.DMA((CHUNKS,)),
            pltpu.SemaphoreType.DMA((CHUNKS,)),
            pltpu.SemaphoreType.DMA((CHUNKS,)),
            pltpu.SemaphoreType.DMA((CHUNKS,)),
            pltpu.SemaphoreType.DMA((2,)),
            pltpu.SemaphoreType.DMA((2,)),
            pltpu.SemaphoreType.DMA((2,)),
            pltpu.SemaphoreType.DMA((2,)),
        ],
        compiler_params=pltpu.CompilerParams(
            collective_id=0, has_side_effects=True, vmem_limit_bytes=56 * 1024 * 1024
        ),
    )(
        pressure.reshape(flat),
        old_pressure.reshape(flat),
        texture.reshape(flat),
        zones,
        rates.reshape(1, -1),
        vg_table,
        approx_inverse,
    )
    return result.reshape(pressure.shape)


def solution(mesh):
    placed = (
        P("layer", "tile", None),
        P("layer", "tile", None),
        P("layer", "tile", None),
        P("tile", None),
        P(),
        P(),
        P(),
    )
    return jax.shard_map(
        body, mesh=mesh, in_specs=placed, out_specs=P("layer", "tile", None), check_vma=False
    )
```

```python
import functools

import jax
import jax.numpy as jnp
from jax import lax
from jax.experimental import pallas as pl
from jax.experimental.pallas import tpu as pltpu
from jax.sharding import PartitionSpec as P

ITERS = 3
OMEGA = 0.2
LOG2E = 1.4426950408889634
MESH = pl.DeviceIdType.MESH
LANES = 128
CHUNKS = 4
FIELDS = 3
GROUPS = ((3, 0), (1, 2))
ORDER = sum(GROUPS, ())
F32 = jnp.float32


def saturation(head, la, n, negp):
    suction = jnp.log(1.0 + jnp.exp2(jnp.abs(head) * (-LOG2E))) + jnp.maximum(-head, 0.0)
    power = jnp.exp2(n * jnp.log(suction) + la)
    return jnp.exp2(negp * jnp.log(1.0 + power))


def exchange(tiles):
    sub = lax.broadcasted_iota(jnp.int32, tiles[0].shape, 0)
    low, even = sub < 4, (sub & 2) == 0
    a, b, c, d = tiles

    def halves(p, q):
        r = pltpu.roll(jnp.where(low, q, p), 4, 0)
        return jnp.where(low, p, r), jnp.where(low, r, q)

    def pairs(p, q):
        return (
            jnp.where(even, p, pltpu.roll(q, 2, 0)),
            jnp.where(even, pltpu.roll(p, 6, 0), q),
        )

    a, c = halves(a, c)
    b, d = halves(b, d)
    a, b = pairs(a, b)
    c, d = pairs(c, d)
    return a, b, c, d


def lookup(splat, classes, row, index, masks):
    def constant(k):
        tile = splat[row, min(k, classes - 1)]
        if len(index.shape) == 2:
            return jnp.concatenate([tile] * (index.shape[1] // LANES), axis=1)
        return jnp.broadcast_to(tile[None], index.shape)

    level = [constant(k) for k in range(classes)]
    for mask in masks:
        level = [
            jnp.where(mask, level[k + 1], level[k]) if k + 1 < len(level) else level[k]
            for k in range(0, len(level), 2)
        ]
    return level[0]


def bits(index, classes):
    return [(index & (1 << b)) != 0 for b in range((classes - 1).bit_length())]


def kernel(
    count,
    tiles,
    press,
    old,
    tex,
    zones,
    rates,
    table,
    inverse,
    out,
    nat_h,
    nat_o,
    nat_t,
    stage,
    colb_a,
    colb_b,
    hcur,
    par_c,
    mold_c,
    mis_c,
    upd_c,
    ghost,
    lay,
    lay2,
    ready,
    ready2,
    par_l,
    tex_h,
    fin,
    zone_v,
    rate_v,
    table_v,
    tab,
    splat,
    inv_v,
    load_sem,
    in_send,
    in_recv,
    back_send,
    back_recv,
    halo_send,
    halo_recv,
    tex_send,
    tex_recv,
):
    colb = (colb_a, colb_b)
    me = lax.axis_index("layer")
    tile = lax.axis_index("tile")
    width = press.shape[1]
    depth = press.shape[0] // 8
    classes = table.shape[1]
    layers = count * depth
    down = lax.rem(tile + tiles - 1, tiles)
    up = lax.rem(tile + 1, tiles)
    wide = 512
    blocks = width // wide

    def peer_of(k):
        return lax.rem(me + k, count)

    run = tiles // 2
    above, beneath = tile != tiles - 1, tile != 0
    last, first = tile == run - 1, tile == run
    greets_up = jnp.logical_and(above, jnp.logical_not(last))
    greeted_below = jnp.logical_and(beneath, jnp.logical_not(first))

    def hello(device):
        pl.semaphore_signal(
            pltpu.get_barrier_semaphore(), inc=1, device_id=device, device_id_type=MESH
        )

    def greet(k, carry):
        hello({"layer": peer_of(k)})
        return carry

    lax.fori_loop(1, count, greet, 0)

    @pl.when(greets_up)
    def _():
        hello({"tile": up})

    @pl.when(first)
    def _():
        hello({"tile": down})

    my_cols = pl.ds(pl.multiple_of(me * LANES, LANES), LANES)
    loads = [
        pltpu.make_async_copy(table, table_v, load_sem.at[0]),
        pltpu.make_async_copy(press, nat_h, load_sem.at[1]),
        pltpu.make_async_copy(old, nat_o, load_sem.at[2]),
        pltpu.make_async_copy(tex, nat_t, load_sem.at[3]),
        pltpu.make_async_copy(inverse, inv_v, load_sem.at[4]),
        pltpu.make_async_copy(zones.at[:, my_cols], zone_v, load_sem.at[5]),
        pltpu.make_async_copy(rates, rate_v, load_sem.at[6]),
    ]
    for load in loads:
        load.start()

    loads[0].wait()
    tab[...] = jnp.ones(tab.shape, F32)
    tab[0:5, 0:classes] = table_v[...]
    t_a, t_n, t_r, t_s, t_k = (tab[j : j + 1, :] for j in range(5))
    derived = (
        t_n * jnp.log(t_a) * LOG2E,
        t_n * LOG2E,
        (1.0 / t_n - 1.0) * LOG2E,
        t_k,
        t_r,
        t_s - t_r,
    )
    for j, row in enumerate(derived):
        for k in range(classes):
            splat[j, k] = jnp.broadcast_to(row[:, k : k + 1], (8, LANES))

    for load in loads[1:4]:
        load.wait()

    def pack(b, carry):
        cols = pl.ds(pl.multiple_of(b * wide, wide), wide)
        for f, nat in enumerate((nat_h, nat_o, nat_t)):
            rows = [nat[8 * l : 8 * l + 8, cols] for l in range(depth)]
            if f == 2:
                rows = [r.astype(F32) for r in rows]
            for c, packed in enumerate(exchange(rows)):
                stage[pl.ds(ORDER.index(c) * FIELDS * 8 + 8 * f, 8), cols] = packed
        return carry

    lax.fori_loop(0, blocks, pack, 0)

    def at_stage(c):
        return ORDER.index(c) * FIELDS * 8

    def params_of(texture, slot):
        def step(b, carry):
            cols = pl.ds(pl.multiple_of(b * wide, wide), wide)
            index = texture(cols).astype(jnp.int32)
            masks = bits(index, classes)
            for j in range(4):
                par_l[j, slot, :, cols] = lookup(splat, classes, j, index, masks)
            return carry

        lax.fori_loop(0, blocks, step, 0)

    for c in range(CHUNKS):
        params_of(lambda cols, c=c: stage[pl.ds(at_stage(c) + 16, 8), cols], c + 1)

    greeted = count - 1 + jnp.where(greeted_below, 1, 0) + jnp.where(last, 1, 0)
    pl.semaphore_wait(pltpu.get_barrier_semaphore(), greeted)

    def beside(side):
        return pltpu.make_async_remote_copy(
            src_ref=stage.at[pl.ds(at_stage(3 if side == 0 else 0) + 16, 8)],
            dst_ref=tex_h.at[side],
            send_sem=tex_send.at[side],
            recv_sem=tex_recv.at[side],
            device_id={"tile": up if side == 0 else down},
            device_id_type=MESH,
        )

    @pl.when(greeted_below)
    def _():
        beside(1).start()

    @pl.when(last)
    def _():
        beside(0).start()

    for g, chunks in enumerate(GROUPS):
        rows = pl.ds(at_stage(chunks[0]), len(chunks) * FIELDS * 8)

        def send_in(k, carry, g=g, rows=rows):
            peer = peer_of(k)
            pltpu.make_async_remote_copy(
                src_ref=stage.at[rows, pl.ds(pl.multiple_of(peer * LANES, LANES), LANES)],
                dst_ref=colb[g].at[me],
                send_sem=in_send.at[g],
                recv_sem=in_recv.at[g],
                device_id={"layer": peer},
                device_id_type=MESH,
            ).start()
            return carry

        lax.fori_loop(1, count, send_in, 0)
        colb[g][me] = stage[rows, my_cols]

    loads[5].wait()
    loads[6].wait()
    tab[0:1, 0 : rates.shape[1]] = rate_v[...]
    inflow = jnp.take_along_axis(
        jnp.broadcast_to(tab[0:1, :], (8, LANES)), zone_v[...], axis=1, mode="promise_in_bounds"
    )
    for c in range(CHUNKS):
        ghost[c] = pltpu.roll(inflow, (6 - 2 * c) % 8, 0)

    loads[4].wait()
    inv = inv_v[...]
    inv_hi = inv.astype(jnp.bfloat16)
    inv_lo = (inv - inv_hi.astype(F32)).astype(jnp.bfloat16)
    inv_all = jnp.concatenate([inv_hi, inv_lo, inv_hi], axis=1)

    shape = (count, 8, LANES)
    sub3 = lax.broadcasted_iota(jnp.int32, shape, 1)

    def below(x):
        last = pltpu.roll(x[count - 1 :], 2, 1)
        return pltpu.roll(jnp.where(sub3 < 2, jnp.concatenate([x[1:], last], axis=0), x), 6, 1)

    def newton(c):
        group = 4
        g = [c in chunks for chunks in GROUPS].index(True)
        base = GROUPS[g].index(c) * FIELDS * 8

        def field(f, at):
            return colb[g][at, base + 8 * f : base + 8 * f + 8, :]

        def params(i, carry):
            at = pl.ds(i * group, group)
            index = field(2, at).astype(jnp.int32)
            masks = bits(index, classes)
            values = [lookup(splat, classes, j, index, masks) for j in range(6)]
            for j in range(6):
                par_c[j, at] = values[j]
            sat = saturation(field(1, at), values[0], values[1], values[2])
            mold_c[at] = values[4] + values[5] * sat
            return carry

        lax.fori_loop(0, count // group, params, 0)
        hcur[c] = field(0, slice(None)).reshape(count * 8, LANES)

        def step(i, carry):
            h = hcur[c].reshape(shape)
            sat = saturation(h, par_c[0], par_c[1], par_c[2])
            k = par_c[3] * (sat * sat * sat)
            flux = (0.5 * (k + below(k))) * (h - below(h) + 1.0)
            shifted = jnp.concatenate([ghost[c][None], flux[:-1]], axis=0)
            above = pltpu.roll(jnp.where(sub3 >= 6, shifted, flux), 2, 1)
            moisture = par_c[4] + par_c[5] * sat
            misfit = (moisture - mold_c[...]) + (flux - above)
            mis_c[...] = misfit.reshape(count * 8, LANES)
            x = jnp.concatenate(
                [mis_c[pl.ds(y, layers, stride=2), :] for y in range(2)], axis=1
            )
            hi = x.astype(jnp.bfloat16)
            lo = (x - hi.astype(F32)).astype(jnp.bfloat16)
            stacked = jnp.concatenate([hi, hi, lo], axis=0)
            update = jnp.dot(inv_all, stacked, preferred_element_type=F32)
            for y in range(2):
                upd_c[pl.ds(y, layers, stride=2), :] = update[:, y * LANES : (y + 1) * LANES]
            hcur[c] = hcur[c] - upd_c[...]
            return carry

        lax.fori_loop(0, ITERS, step, 0)

    def tile_rows(peer):
        return pl.ds(pl.multiple_of(peer * 8, 8), 8)

    def send_back(c):
        def send(k, carry):
            peer = peer_of(k)
            pltpu.make_async_remote_copy(
                src_ref=hcur.at[c, tile_rows(peer)],
                dst_ref=lay.at[c + 1, :, my_cols],
                send_sem=back_send.at[c],
                recv_sem=back_recv.at[c],
                device_id={"layer": peer},
                device_id_type=MESH,
            ).start()
            return carry

        lax.fori_loop(1, count, send, 0)
        lay[c + 1, :, my_cols] = hcur[c, tile_rows(me), :]

    def landed(c):
        part = lay.at[c + 1, :, pl.ds(0, (count - 1) * LANES)]
        pltpu.make_async_copy(part, part, back_recv.at[c]).wait()

    def forward(c, slot, side):
        return pltpu.make_async_remote_copy(
            src_ref=lay.at[c + 1],
            dst_ref=lay.at[slot],
            send_sem=halo_send.at[side],
            recv_sem=halo_recv.at[side],
            device_id={"tile": up if side == 0 else down},
            device_id_type=MESH,
        )

    heads_up, heads_down = forward(3, 0, 0), forward(0, CHUNKS + 1, 1)
    for g, chunks in enumerate(GROUPS):
        part = colb[g].at[pl.ds(0, count - 1)]
        pltpu.make_async_copy(part, part, in_recv.at[g]).wait()
        for c in chunks:
            newton(c)
            send_back(c)
        if 3 in chunks:

            @pl.when(greets_up)
            def _():
                beside(1).wait_recv()
                beside(0).start()

            landed(3)

            @pl.when(above)
            def _():
                heads_up.start()

    @pl.when(first)
    def _():
        beside(0).wait_recv()
        beside(1).start()

    landed(0)

    @pl.when(beneath)
    def _():
        heads_down.start()


    @pl.when(jnp.logical_not(beneath))
    def _():
        tex_h[0] = jnp.zeros(tex_h.shape[1:], F32)
        lay[0] = lay[1]

    @pl.when(jnp.logical_not(above))
    def _():
        tex_h[1] = jnp.zeros(tex_h.shape[1:], F32)
        lay[CHUNKS + 1] = lay[CHUNKS]

    def odd_rows(shape):
        return (lax.broadcasted_iota(jnp.int32, shape, 0) & 1) == 1

    def prepare(src, dst, s):
        h = src[s]
        sat = saturation(h, par_l[0, s], par_l[1, s], par_l[2, s])
        k = par_l[3, s] * (sat * sat * sat)
        odd = odd_rows(h.shape)
        dst[0, s] = k
        dst[1, s] = jnp.where(odd, pltpu.roll(h, 1, 0), pltpu.roll(h, 7, 0))
        dst[2, s] = jnp.where(odd, pltpu.roll(k, 1, 0), pltpu.roll(k, 7, 0))

    def advance(src, by, dst, s):
        h, k = src[s], by[0, s]
        lane = lax.broadcasted_iota(jnp.int32, h.shape, 1)
        flow = (k + pltpu.roll(k, width - 1, 1)) * (pltpu.roll(h, width - 1, 1) - h)
        flow = jnp.where(lane == width - 1, 0.0, flow)
        change = flow - pltpu.roll(flow, 1, 1)
        change = change + (k + by[2, s]) * (by[1, s] - h)
        odd = odd_rows(h.shape)
        after, before = min(s + 1, CHUNKS + 1), max(s - 1, 0)
        side_h = jnp.where(odd, by[1, after], by[1, before])
        side_c = jnp.where(odd, by[2, after], by[2, before])
        side = (k + side_c) * (side_h - h)
        if s == 1:
            side = jnp.where(jnp.logical_and(tile == 0, jnp.logical_not(odd)), 0.0, side)
        if s == CHUNKS:
            side = jnp.where(jnp.logical_and(tile == tiles - 1, odd), 0.0, side)
        dst[s] = h + (0.5 * OMEGA) * (change + side)

    prepare(lay, ready, 4)
    prepare(lay, ready, 1)
    landed(1)
    prepare(lay, ready, 2)

    @pl.when(last)
    def _():
        beside(1).wait_recv()

    params_of(lambda cols: tex_h[1, :, cols], 5)

    def low_side():
        @pl.when(greeted_below)
        def _():
            beside(0).wait_recv()

        params_of(lambda cols: tex_h[0, :, cols], 0)

        @pl.when(beneath)
        def _():
            heads_up.wait_recv()

        prepare(lay, ready, 0)
        for s in (0, 1):
            advance(lay, ready, lay2, s)
            prepare(lay2, ready2, s)

    pl.when(jnp.logical_not(first))(low_side)

    @pl.when(above)
    def _():
        heads_down.wait_recv()

    prepare(lay, ready, 5)
    advance(lay, ready, lay2, 5)
    prepare(lay2, ready2, 5)
    landed(2)
    prepare(lay, ready, 3)
    for s in (2, 3, 4):
        advance(lay, ready, lay2, s)
        prepare(lay2, ready2, s)
    pl.when(first)(low_side)
    for s in (1, 2, 3, 4):
        advance(lay2, ready2, fin, s)

    def unpack(b, carry):
        cols = pl.ds(pl.multiple_of(b * wide, wide), wide)
        for l, rows in enumerate(exchange([fin[c + 1, :, cols] for c in range(CHUNKS)])):
            nat_h[8 * l : 8 * l + 8, cols] = rows
        pltpu.make_async_copy(nat_h.at[:, cols], out.at[:, cols], load_sem.at[7]).start()
        return carry

    lax.fori_loop(0, blocks, unpack, 0)
    for g in range(len(GROUPS)):
        part = colb[g].at[pl.ds(0, count - 1)]
        pltpu.make_async_copy(part, part, in_send.at[g]).wait()
    for c in range(CHUNKS):
        part = hcur.at[c, pl.ds(0, (count - 1) * 8)]
        pltpu.make_async_copy(part, part, back_send.at[c]).wait()

    @pl.when(above)
    def _():
        heads_up.wait_send()
        beside(0).wait_send()

    @pl.when(beneath)
    def _():
        heads_down.wait_send()
        beside(1).wait_send()

    pltpu.make_async_copy(nat_h, out, load_sem.at[7]).wait()


def body(pressure, old_pressure, texture, zones, rates, vg_table, approx_inverse):
    count = lax.axis_size("layer")
    tiles = lax.axis_size("tile")
    depth, tall, width = pressure.shape
    rows = depth * tall
    flat = (rows, width)
    slots = (CHUNKS + 2, 2 * depth, width)
    column = (count, 2 * depth, LANES)
    classes = vg_table.shape[1]

    def vmem(*shape, dtype=F32):
        return pltpu.VMEM(shape, dtype)

    result = pl.pallas_call(
        functools.partial(kernel, count, tiles),
        out_shape=jax.ShapeDtypeStruct(flat, F32),
        in_specs=[pl.BlockSpec(memory_space=pltpu.HBM)] * 7,
        out_specs=pl.BlockSpec(memory_space=pltpu.HBM),
        scratch_shapes=[
            vmem(*flat),
            vmem(*flat),
            vmem(*flat, dtype=jnp.int32),
            vmem(CHUNKS * FIELDS * 2 * depth, width),
            *(vmem(count, len(g) * FIELDS * 2 * depth, LANES) for g in GROUPS),
            vmem(CHUNKS, count * 2 * depth, LANES),
            vmem(6, *column),
            vmem(*column),
            vmem(count * 2 * depth, LANES),
            vmem(count * 2 * depth, LANES),
            vmem(CHUNKS, 8, LANES),
            vmem(*slots),
            vmem(*slots),
            vmem(3, *slots),
            vmem(3, *slots),
            vmem(4, *slots),
            vmem(2, 2 * depth, width),
            vmem(*slots),
            vmem(tall, LANES, dtype=jnp.int32),
            vmem(1, rates.shape[0]),
            vmem(*vg_table.shape),
            vmem(8, LANES),
            vmem(6, classes, 8, LANES),
            vmem(*approx_inverse.shape),
            pltpu.SemaphoreType.DMA((8,)),
            pltpu.SemaphoreType.DMA((len(GROUPS),)),
            pltpu.SemaphoreType.DMA((len(GROUPS),)),
            pltpu.SemaphoreType.DMA((CHUNKS,)),
            pltpu.SemaphoreType.DMA((CHUNKS,)),
            pltpu.SemaphoreType.DMA((2,)),
            pltpu.SemaphoreType.DMA((2,)),
            pltpu.SemaphoreType.DMA((2,)),
            pltpu.SemaphoreType.DMA((2,)),
        ],
        compiler_params=pltpu.CompilerParams(
            collective_id=0, has_side_effects=True, vmem_limit_bytes=56 * 1024 * 1024
        ),
    )(
        pressure.reshape(flat),
        old_pressure.reshape(flat),
        texture.reshape(flat),
        zones,
        rates.reshape(1, -1),
        vg_table,
        approx_inverse,
    )
    return result.reshape(pressure.shape)


def solution(mesh):
    placed = (
        P("layer", "tile", None),
        P("layer", "tile", None),
        P("layer", "tile", None),
        P("tile", None),
        P(),
        P(),
        P(),
    )
    return jax.shard_map(
        body, mesh=mesh, in_specs=placed, out_specs=P("layer", "tile", None), check_vma=False
    )
```

```python
import functools

import jax
import jax.numpy as jnp
from jax import lax
from jax.experimental import pallas as pl
from jax.experimental.pallas import tpu as pltpu
from jax.sharding import PartitionSpec as P

ITERS = 3
OMEGA = 0.2
LOG2E = 1.4426950408889634
MESH = pl.DeviceIdType.MESH
LANES = 128
CHUNKS = 4
FIELDS = 3
HEAD, OLD, TEXTURE = range(FIELDS)
GROUPS = (
    tuple((c, f) for c in (3, 0) for f in range(FIELDS)),
    tuple((c, f) for c in (1, 2) for f in (TEXTURE, OLD)),
    tuple((c, HEAD) for c in (1, 2)),
)
TILES = sum(GROUPS, ())
SIDE = 4
TURNS = sorted(
    range(1, SIDE * SIDE),
    key=lambda v: (not v & 2, -(v % SIDE) - min(v // SIDE, SIDE - v // SIDE)),
)
F32 = jnp.float32


def words(values):
    packed = [sum(v << (4 * i) for i, v in enumerate(values[j : j + 8])) for j in (0, 8)]
    return [w - (1 << 32) if w >= 1 << 31 else w for w in packed]


TURN_WORDS = words(TURNS)


def turn(k):
    word = jnp.where(k < 8, jnp.int32(TURN_WORDS[0]), jnp.int32(TURN_WORDS[1]))
    return lax.shift_right_logical(word, 4 * lax.rem(k, 8)) & (SIDE * SIDE - 1)


def saturation(head, la, n, negp):
    suction = jnp.log(1.0 + jnp.exp2(jnp.abs(head) * (-LOG2E))) + jnp.maximum(-head, 0.0)
    power = jnp.exp2(n * jnp.log(suction) + la)
    return jnp.exp2(negp * jnp.log(1.0 + power))


def exchange(tiles):
    sub = lax.broadcasted_iota(jnp.int32, tiles[0].shape, 0)
    low, even = sub < 4, (sub & 2) == 0
    a, b, c, d = tiles

    def halves(p, q):
        r = pltpu.roll(jnp.where(low, q, p), 4, 0)
        return jnp.where(low, p, r), jnp.where(low, r, q)

    def pairs(p, q):
        return (
            jnp.where(even, p, pltpu.roll(q, 2, 0)),
            jnp.where(even, pltpu.roll(p, 6, 0), q),
        )

    a, c = halves(a, c)
    b, d = halves(b, d)
    a, b = pairs(a, b)
    c, d = pairs(c, d)
    return a, b, c, d


def lookup(splat, classes, row, index, masks):
    def constant(k):
        tile = splat[row, min(k, classes - 1)]
        if len(index.shape) == 2:
            return jnp.concatenate([tile] * (index.shape[1] // LANES), axis=1)
        return jnp.broadcast_to(tile[None], index.shape)

    level = [constant(k) for k in range(classes)]
    for mask in masks:
        level = [
            jnp.where(mask, level[k + 1], level[k]) if k + 1 < len(level) else level[k]
            for k in range(0, len(level), 2)
        ]
    return level[0]


def bits(index, classes):
    return [(index & (1 << b)) != 0 for b in range((classes - 1).bit_length())]


def kernel(
    count,
    tiles,
    press,
    old,
    tex,
    zones,
    rates,
    table,
    inverse,
    out,
    nat_h,
    nat_o,
    nat_t,
    stage,
    colb_a,
    colb_b,
    colb_c,
    hcur,
    par_c,
    mold_c,
    mis_c,
    upd_c,
    ghost,
    lay,
    lay2,
    ready,
    ready2,
    par_l,
    tex_h,
    zone_v,
    rate_v,
    table_v,
    tab,
    splat,
    inv_v,
    load_sem,
    in_send,
    in_recv,
    back_send,
    back_recv,
    halo_send,
    halo_recv,
    tex_send,
    tex_recv,
):
    colb = (colb_a, colb_b, colb_c)
    me = lax.axis_index("layer")
    tile = lax.axis_index("tile")
    width = press.shape[1]
    depth = press.shape[0] // 8
    classes = table.shape[1]
    layers = count * depth
    down = lax.rem(tile + tiles - 1, tiles)
    up = lax.rem(tile + 1, tiles)
    wide = 512
    blocks = width // wide

    def peer_of(k):
        return jnp.bitwise_xor(me, turn(k))

    run = tiles // 2
    my_cols = pl.ds(pl.multiple_of(me * LANES, LANES), LANES)
    loads = [
        pltpu.make_async_copy(table, table_v, load_sem.at[0]),
        pltpu.make_async_copy(press, nat_h, load_sem.at[1]),
        pltpu.make_async_copy(old, nat_o, load_sem.at[2]),
        pltpu.make_async_copy(tex, nat_t, load_sem.at[3]),
        pltpu.make_async_copy(inverse, inv_v, load_sem.at[4]),
        pltpu.make_async_copy(zones.at[:, my_cols], zone_v, load_sem.at[5]),
        pltpu.make_async_copy(rates, rate_v, load_sem.at[6]),
    ]
    for load in loads:
        load.start()

    above, beneath = tile != tiles - 1, tile != 0
    last, first = tile == run - 1, tile == run
    greets_up = jnp.logical_and(above, jnp.logical_not(last))
    greeted_below = jnp.logical_and(beneath, jnp.logical_not(first))

    def hello(device):
        pl.semaphore_signal(
            pltpu.get_barrier_semaphore(), inc=1, device_id=device, device_id_type=MESH
        )

    def greet(k, carry):
        hello({"layer": peer_of(k)})
        return carry

    lax.fori_loop(0, count - 1, greet, 0)

    @pl.when(greets_up)
    def _():
        hello({"tile": up})

    @pl.when(first)
    def _():
        hello({"tile": down})

    loads[0].wait()
    tab[...] = jnp.ones(tab.shape, F32)
    tab[0:5, 0:classes] = table_v[...]
    t_a, t_n, t_r, t_s, t_k = (tab[j : j + 1, :] for j in range(5))
    derived = (
        t_n * jnp.log(t_a) * LOG2E,
        t_n * LOG2E,
        (1.0 / t_n - 1.0) * LOG2E,
        t_k,
        t_r,
        t_s - t_r,
    )
    for j, row in enumerate(derived):
        for k in range(classes):
            splat[j, k] = jnp.broadcast_to(row[:, k : k + 1], (8, LANES))

    def staged(c, f):
        return pl.ds(8 * TILES.index((c, f)), 8)

    for load in loads[1:4]:
        load.wait()

    def pack(b, carry):
        cols = pl.ds(pl.multiple_of(b * wide, wide), wide)
        for f, nat in enumerate((nat_h, nat_o, nat_t)):
            rows = [nat[8 * l : 8 * l + 8, cols] for l in range(depth)]
            if f == 2:
                rows = [r.astype(F32) for r in rows]
            for c, packed in enumerate(exchange(rows)):
                stage[staged(c, f), cols] = packed
        return carry

    lax.fori_loop(0, blocks, pack, 0)

    def params_of(texture, slot):
        def step(b, carry):
            cols = pl.ds(pl.multiple_of(b * wide, wide), wide)
            index = texture(cols).astype(jnp.int32)
            masks = bits(index, classes)
            for j in range(4):
                par_l[j, slot, :, cols] = lookup(splat, classes, j, index, masks)
            return carry

        lax.fori_loop(0, blocks, step, 0)

    greeted = count - 1 + jnp.where(greeted_below, 1, 0) + jnp.where(last, 1, 0)
    pl.semaphore_wait(pltpu.get_barrier_semaphore(), greeted)

    def beside(side):
        return pltpu.make_async_remote_copy(
            src_ref=stage.at[staged(3 if side == 0 else 0, TEXTURE)],
            dst_ref=tex_h.at[side],
            send_sem=tex_send.at[side],
            recv_sem=tex_recv.at[side],
            device_id={"tile": up if side == 0 else down},
            device_id_type=MESH,
        )

    @pl.when(greeted_below)
    def _():
        beside(1).start()

    @pl.when(last)
    def _():
        beside(0).start()

    start = 0
    for g, members in enumerate(GROUPS):
        rows = pl.ds(8 * start, 8 * len(members))
        start += len(members)

        def send_in(k, carry, g=g, rows=rows):
            peer = peer_of(k)
            pltpu.make_async_remote_copy(
                src_ref=stage.at[rows, pl.ds(pl.multiple_of(peer * LANES, LANES), LANES)],
                dst_ref=colb[g].at[me],
                send_sem=in_send.at[g],
                recv_sem=in_recv.at[g],
                device_id={"layer": peer},
                device_id_type=MESH,
            ).start()
            return carry

        lax.fori_loop(0, count - 1, send_in, 0)
        colb[g][me] = stage[rows, my_cols]

    for c in range(CHUNKS):
        params_of(lambda cols, c=c: stage[staged(c, TEXTURE), cols], c + 1)

    loads[5].wait()
    loads[6].wait()
    tab[0:1, 0 : rates.shape[1]] = rate_v[...]
    inflow = jnp.take_along_axis(
        jnp.broadcast_to(tab[0:1, :], (8, LANES)), zone_v[...], axis=1, mode="promise_in_bounds"
    )
    for c in range(CHUNKS):
        ghost[c] = pltpu.roll(inflow, (6 - 2 * c) % 8, 0)

    loads[4].wait()
    inv = inv_v[...]
    inv_hi = inv.astype(jnp.bfloat16)
    inv_lo = (inv - inv_hi.astype(F32)).astype(jnp.bfloat16)
    inv_all = jnp.concatenate([inv_hi, inv_lo, inv_hi], axis=1)

    shape = (count, 8, LANES)
    sub3 = lax.broadcasted_iota(jnp.int32, shape, 1)

    def below(x):
        last = pltpu.roll(x[count - 1 :], 2, 1)
        return pltpu.roll(jnp.where(sub3 < 2, jnp.concatenate([x[1:], last], axis=0), x), 6, 1)

    def field(c, f, at):
        g = [(c, f) in members for members in GROUPS].index(True)
        row = 8 * GROUPS[g].index((c, f))
        return colb[g][at, row : row + 8, :]

    def column_params(c):
        group = 4

        def step(i, carry):
            at = pl.ds(i * group, group)
            index = field(c, TEXTURE, at).astype(jnp.int32)
            masks = bits(index, classes)
            values = [lookup(splat, classes, j, index, masks) for j in range(6)]
            for j in range(6):
                par_c[c, j, at] = values[j]
            sat = saturation(field(c, OLD, at), values[0], values[1], values[2])
            mold_c[c, at] = values[4] + values[5] * sat
            return carry

        lax.fori_loop(0, count // group, step, 0)

    def newton(c):
        hcur[c] = field(c, HEAD, slice(None)).reshape(count * 8, LANES)

        def step(i, carry):
            h = hcur[c].reshape(shape)
            sat = saturation(h, par_c[c, 0], par_c[c, 1], par_c[c, 2])
            k = par_c[c, 3] * (sat * sat * sat)
            flux = (0.5 * (k + below(k))) * (h - below(h) + 1.0)
            shifted = jnp.concatenate([ghost[c][None], flux[:-1]], axis=0)
            above = pltpu.roll(jnp.where(sub3 >= 6, shifted, flux), 2, 1)
            moisture = par_c[c, 4] + par_c[c, 5] * sat
            misfit = (moisture - mold_c[c]) + (flux - above)
            mis_c[...] = misfit.reshape(count * 8, LANES)
            x = jnp.concatenate(
                [mis_c[pl.ds(y, layers, stride=2), :] for y in range(2)], axis=1
            )
            hi = x.astype(jnp.bfloat16)
            lo = (x - hi.astype(F32)).astype(jnp.bfloat16)
            stacked = jnp.concatenate([hi, hi, lo], axis=0)
            update = jnp.dot(inv_all, stacked, preferred_element_type=F32)
            for y in range(2):
                upd_c[pl.ds(y, layers, stride=2), :] = update[:, y * LANES : (y + 1) * LANES]
            hcur[c] = hcur[c] - upd_c[...]
            return carry

        lax.fori_loop(0, ITERS, step, 0)

    def tile_rows(peer):
        return pl.ds(pl.multiple_of(peer * 8, 8), 8)

    def send_back(c):
        def send(k, carry):
            peer = peer_of(k)
            pltpu.make_async_remote_copy(
                src_ref=hcur.at[c, tile_rows(peer)],
                dst_ref=lay.at[c + 1, :, my_cols],
                send_sem=back_send.at[c],
                recv_sem=back_recv.at[c],
                device_id={"layer": peer},
                device_id_type=MESH,
            ).start()
            return carry

        lax.fori_loop(0, count - 1, send, 0)
        lay[c + 1, :, my_cols] = hcur[c, tile_rows(me), :]

    def landed(c):
        part = lay.at[c + 1, :, pl.ds(0, (count - 1) * LANES)]
        pltpu.make_async_copy(part, part, back_recv.at[c]).wait()

    def forward(c, slot, side):
        return pltpu.make_async_remote_copy(
            src_ref=lay.at[c + 1],
            dst_ref=lay.at[slot],
            send_sem=halo_send.at[side],
            recv_sem=halo_recv.at[side],
            device_id={"tile": up if side == 0 else down},
            device_id_type=MESH,
        )

    heads_up, heads_down = forward(3, 0, 0), forward(0, CHUNKS + 1, 1)
    def arrived(g):
        part = colb[g].at[pl.ds(0, count - 1)]
        pltpu.make_async_copy(part, part, in_recv.at[g]).wait()

    arrived(0)
    for c in (3, 0):
        column_params(c)
        newton(c)
        send_back(c)

    @pl.when(greets_up)
    def _():
        beside(1).wait_recv()
        beside(0).start()

    landed(3)

    @pl.when(above)
    def _():
        heads_up.start()

    arrived(1)
    for c in (1, 2):
        column_params(c)

    @pl.when(first)
    def _():
        beside(0).wait_recv()
        beside(1).start()

    landed(0)

    @pl.when(beneath)
    def _():
        heads_down.start()

    arrived(2)
    for c in (1, 2):
        newton(c)
        send_back(c)

    @pl.when(jnp.logical_not(beneath))
    def _():
        tex_h[0] = jnp.zeros(tex_h.shape[1:], F32)
        lay[0] = lay[1]

    @pl.when(jnp.logical_not(above))
    def _():
        tex_h[1] = jnp.zeros(tex_h.shape[1:], F32)
        lay[CHUNKS + 1] = lay[CHUNKS]

    def odd_rows(shape):
        return (lax.broadcasted_iota(jnp.int32, shape, 0) & 1) == 1

    def prepare(src, dst, s):
        h = src[s]
        sat = saturation(h, par_l[0, s], par_l[1, s], par_l[2, s])
        k = par_l[3, s] * (sat * sat * sat)
        odd = odd_rows(h.shape)
        other_h = jnp.where(odd, pltpu.roll(h, 1, 0), pltpu.roll(h, 7, 0))
        other_k = jnp.where(odd, pltpu.roll(k, 1, 0), pltpu.roll(k, 7, 0))
        dst[0, s] = k
        dst[1, s] = other_h
        dst[2, s] = other_k
        lane = lax.broadcasted_iota(jnp.int32, h.shape, 1)
        flow = (k + pltpu.roll(k, width - 1, 1)) * (pltpu.roll(h, width - 1, 1) - h)
        flow = jnp.where(lane == width - 1, 0.0, flow)
        dst[3, s] = flow - pltpu.roll(flow, 1, 1) + (k + other_k) * (other_h - h)

    def advanced(src, by, s, cols):
        h, k = src[s, :, cols], by[0, s, :, cols]
        odd = odd_rows(h.shape)
        after, before = min(s + 1, CHUNKS + 1), max(s - 1, 0)
        side_h = jnp.where(odd, by[1, after, :, cols], by[1, before, :, cols])
        side_k = jnp.where(odd, by[2, after, :, cols], by[2, before, :, cols])
        side = (k + side_k) * (side_h - h)
        if s == 1:
            side = jnp.where(jnp.logical_and(tile == 0, jnp.logical_not(odd)), 0.0, side)
        if s == CHUNKS:
            side = jnp.where(jnp.logical_and(tile == tiles - 1, odd), 0.0, side)
        return h + (0.5 * OMEGA) * (by[3, s, :, cols] + side)

    def advance(src, by, dst, s):
        dst[s] = advanced(src, by, s, slice(None))

    prepare(lay, ready, 4)
    prepare(lay, ready, 1)
    landed(1)
    prepare(lay, ready, 2)

    @pl.when(last)
    def _():
        beside(1).wait_recv()

    params_of(lambda cols: tex_h[1, :, cols], 5)

    def low_side():
        @pl.when(greeted_below)
        def _():
            beside(0).wait_recv()

        params_of(lambda cols: tex_h[0, :, cols], 0)

        @pl.when(beneath)
        def _():
            heads_up.wait_recv()

        prepare(lay, ready, 0)
        for s in (0, 1):
            advance(lay, ready, lay2, s)
            prepare(lay2, ready2, s)

    pl.when(jnp.logical_not(first))(low_side)

    @pl.when(above)
    def _():
        heads_down.wait_recv()

    prepare(lay, ready, 5)
    advance(lay, ready, lay2, 5)
    prepare(lay2, ready2, 5)
    landed(2)
    prepare(lay, ready, 3)
    for s in (2, 3, 4):
        advance(lay, ready, lay2, s)
        prepare(lay2, ready2, s)
    pl.when(first)(low_side)
    def finish(b, carry):
        cols = pl.ds(pl.multiple_of(b * wide, wide), wide)
        tops = [advanced(lay2, ready2, c + 1, cols) for c in range(CHUNKS)]
        for l, rows in enumerate(exchange(tops)):
            nat_h[8 * l : 8 * l + 8, cols] = rows
        pltpu.make_async_copy(nat_h.at[:, cols], out.at[:, cols], load_sem.at[7]).start()
        return carry

    lax.fori_loop(0, blocks, finish, 0)
    for g in range(len(GROUPS)):
        part = colb[g].at[pl.ds(0, count - 1)]
        pltpu.make_async_copy(part, part, in_send.at[g]).wait()
    for c in range(CHUNKS):
        part = hcur.at[c, pl.ds(0, (count - 1) * 8)]
        pltpu.make_async_copy(part, part, back_send.at[c]).wait()

    @pl.when(above)
    def _():
        heads_up.wait_send()
        beside(0).wait_send()

    @pl.when(beneath)
    def _():
        heads_down.wait_send()
        beside(1).wait_send()

    pltpu.make_async_copy(nat_h, out, load_sem.at[7]).wait()


def body(pressure, old_pressure, texture, zones, rates, vg_table, approx_inverse):
    count = lax.axis_size("layer")
    tiles = lax.axis_size("tile")
    depth, tall, width = pressure.shape
    rows = depth * tall
    flat = (rows, width)
    slots = (CHUNKS + 2, 2 * depth, width)
    column = (count, 2 * depth, LANES)
    classes = vg_table.shape[1]

    def vmem(*shape, dtype=F32):
        return pltpu.VMEM(shape, dtype)

    result = pl.pallas_call(
        functools.partial(kernel, count, tiles),
        out_shape=jax.ShapeDtypeStruct(flat, F32),
        in_specs=[pl.BlockSpec(memory_space=pltpu.HBM)] * 7,
        out_specs=pl.BlockSpec(memory_space=pltpu.HBM),
        scratch_shapes=[
            vmem(*flat),
            vmem(*flat),
            vmem(*flat, dtype=jnp.int32),
            vmem(CHUNKS * FIELDS * 2 * depth, width),
            *(vmem(count, len(g) * 2 * depth, LANES) for g in GROUPS),
            vmem(CHUNKS, count * 2 * depth, LANES),
            vmem(CHUNKS, 6, *column),
            vmem(CHUNKS, *column),
            vmem(count * 2 * depth, LANES),
            vmem(count * 2 * depth, LANES),
            vmem(CHUNKS, 8, LANES),
            vmem(*slots),
            vmem(*slots),
            vmem(4, *slots),
            vmem(4, *slots),
            vmem(4, *slots),
            vmem(2, 2 * depth, width),
            vmem(tall, LANES, dtype=jnp.int32),
            vmem(1, rates.shape[0]),
            vmem(*vg_table.shape),
            vmem(8, LANES),
            vmem(6, classes, 8, LANES),
            vmem(*approx_inverse.shape),
            pltpu.SemaphoreType.DMA((8,)),
            pltpu.SemaphoreType.DMA((len(GROUPS),)),
            pltpu.SemaphoreType.DMA((len(GROUPS),)),
            pltpu.SemaphoreType.DMA((CHUNKS,)),
            pltpu.SemaphoreType.DMA((CHUNKS,)),
            pltpu.SemaphoreType.DMA((2,)),
            pltpu.SemaphoreType.DMA((2,)),
            pltpu.SemaphoreType.DMA((2,)),
            pltpu.SemaphoreType.DMA((2,)),
        ],
        compiler_params=pltpu.CompilerParams(
            collective_id=0, has_side_effects=True, vmem_limit_bytes=56 * 1024 * 1024
        ),
    )(
        pressure.reshape(flat),
        old_pressure.reshape(flat),
        texture.reshape(flat),
        zones,
        rates.reshape(1, -1),
        vg_table,
        approx_inverse,
    )
    return result.reshape(pressure.shape)


def solution(mesh):
    placed = (
        P("layer", "tile", None),
        P("layer", "tile", None),
        P("layer", "tile", None),
        P("tile", None),
        P(),
        P(),
        P(),
    )
    return jax.shard_map(
        body, mesh=mesh, in_specs=placed, out_specs=P("layer", "tile", None), check_vma=False
    )
```

```python
import functools

import jax
import jax.numpy as jnp
from jax import lax
from jax.experimental import pallas as pl
from jax.experimental.pallas import tpu as pltpu
from jax.sharding import PartitionSpec as P

ITERS = 3
OMEGA = 0.2
LOG2E = 1.4426950408889634
MESH = pl.DeviceIdType.MESH
LANES = 128
CHUNKS = 4
FIELDS = 3
HEAD, OLD, TEXTURE = range(FIELDS)
GROUPS = (
    tuple((c, f) for c in (3, 0) for f in range(FIELDS)),
    tuple((c, f) for c in (1, 2) for f in range(FIELDS)),
)
TILES = sum(GROUPS, ())
PAIRS = ((3, 0), (1, 2))
PLACES = (0, 4, 1, 2, 3, 5)
SIDE = 4
TURNS = sorted(
    range(1, SIDE * SIDE),
    key=lambda v: (not v & 2, -(v % SIDE) - min(v // SIDE, SIDE - v // SIDE)),
)
F32 = jnp.float32


def words(values):
    packed = [sum(v << (4 * i) for i, v in enumerate(values[j : j + 8])) for j in (0, 8)]
    return [w - (1 << 32) if w >= 1 << 31 else w for w in packed]


TURN_WORDS = words(TURNS + [0])


def turn(k):
    word = jnp.where(k < 8, jnp.int32(TURN_WORDS[0]), jnp.int32(TURN_WORDS[1]))
    return lax.shift_right_logical(word, 4 * lax.rem(k, 8)) & (SIDE * SIDE - 1)


def saturation(head, la, n, negp):
    suction = jnp.log(1.0 + jnp.exp2(jnp.abs(head) * (-LOG2E))) + jnp.maximum(-head, 0.0)
    power = jnp.exp2(n * jnp.log(suction) + la)
    return jnp.exp2(negp * jnp.log(1.0 + power))


def exchange(tiles):
    sub = lax.broadcasted_iota(jnp.int32, tiles[0].shape, 0)
    low, even = sub < 4, (sub & 2) == 0
    a, b, c, d = tiles

    def halves(p, q):
        r = pltpu.roll(jnp.where(low, q, p), 4, 0)
        return jnp.where(low, p, r), jnp.where(low, r, q)

    def pairs(p, q):
        return (
            jnp.where(even, p, pltpu.roll(q, 2, 0)),
            jnp.where(even, pltpu.roll(p, 6, 0), q),
        )

    a, c = halves(a, c)
    b, d = halves(b, d)
    a, b = pairs(a, b)
    c, d = pairs(c, d)
    return a, b, c, d


def lookup(splat, classes, row, index, masks):
    def constant(k):
        tile = splat[row, min(k, classes - 1)]
        if len(index.shape) == 2:
            return jnp.concatenate([tile] * (index.shape[1] // LANES), axis=1)
        return jnp.broadcast_to(tile[None], index.shape)

    level = [constant(k) for k in range(classes)]
    for mask in masks:
        level = [
            jnp.where(mask, level[k + 1], level[k]) if k + 1 < len(level) else level[k]
            for k in range(0, len(level), 2)
        ]
    return level[0]


def bits(index, classes):
    return [(index & (1 << b)) != 0 for b in range((classes - 1).bit_length())]


def kernel(
    count,
    tiles,
    press,
    old,
    tex,
    zones,
    rates,
    table,
    inverse,
    out,
    nat_h,
    nat_o,
    nat_t,
    stage,
    colb_a,
    colb_b,
    hcur,
    par_c,
    mold_c,
    mis_c,
    upd_c,
    ghost,
    lay,
    lay2,
    ready,
    ready2,
    par_l,
    tex_h,
    zone_v,
    rate_v,
    table_v,
    tab,
    splat,
    inv_v,
    load_sem,
    in_send,
    in_recv,
    back_send,
    back_recv,
    halo_send,
    halo_recv,
    tex_send,
    tex_recv,
):
    colb = (colb_a, colb_b)
    me = lax.axis_index("layer")
    tile = lax.axis_index("tile")
    width = press.shape[1]
    depth = press.shape[0] // 8
    classes = table.shape[1]
    layers = count * depth
    down = lax.rem(tile + tiles - 1, tiles)
    up = lax.rem(tile + 1, tiles)
    wide = 512
    blocks = width // wide

    def peer_of(k):
        return jnp.bitwise_xor(me, turn(k))

    run = tiles // 2
    my_cols = pl.ds(pl.multiple_of(me * LANES, LANES), LANES)
    loads = [
        pltpu.make_async_copy(table, table_v, load_sem.at[0]),
        pltpu.make_async_copy(press, nat_h, load_sem.at[1]),
        pltpu.make_async_copy(old, nat_o, load_sem.at[2]),
        pltpu.make_async_copy(tex, nat_t, load_sem.at[3]),
        pltpu.make_async_copy(inverse, inv_v, load_sem.at[4]),
        pltpu.make_async_copy(zones.at[:, my_cols], zone_v, load_sem.at[5]),
        pltpu.make_async_copy(rates, rate_v, load_sem.at[6]),
    ]
    for load in loads:
        load.start()

    above, beneath = tile != tiles - 1, tile != 0
    last, first = tile == run - 1, tile == run
    greets_up = jnp.logical_and(above, jnp.logical_not(last))
    greeted_below = jnp.logical_and(beneath, jnp.logical_not(first))

    def hello(device):
        pl.semaphore_signal(
            pltpu.get_barrier_semaphore(), inc=1, device_id=device, device_id_type=MESH
        )

    def greet(k, carry):
        hello({"layer": peer_of(k)})
        return carry

    lax.fori_loop(0, count - 1, greet, 0)

    @pl.when(greets_up)
    def _():
        hello({"tile": up})

    def greet_below(k, carry):
        hello({"tile": down, "layer": peer_of(k)})
        return carry

    @pl.when(first)
    def _():
        lax.fori_loop(0, count, greet_below, 0)


    loads[0].wait()
    tab[...] = jnp.ones(tab.shape, F32)
    tab[0:5, 0:classes] = table_v[...]
    t_a, t_n, t_r, t_s, t_k = (tab[j : j + 1, :] for j in range(5))
    derived = (
        t_n * jnp.log(t_a) * LOG2E,
        t_n * LOG2E,
        (1.0 / t_n - 1.0) * LOG2E,
        t_k,
        t_r,
        t_s - t_r,
    )
    for j, row in enumerate(derived):
        for k in range(classes):
            splat[j, k] = jnp.broadcast_to(row[:, k : k + 1], (8, LANES))

    def staged(c, f):
        return pl.ds(8 * TILES.index((c, f)), 8)

    for load in loads[1:4]:
        load.wait()

    def pack(b, carry):
        cols = pl.ds(pl.multiple_of(b * wide, wide), wide)
        for f, nat in enumerate((nat_h, nat_o, nat_t)):
            rows = [nat[8 * l : 8 * l + 8, cols] for l in range(depth)]
            if f == 2:
                rows = [r.astype(F32) for r in rows]
            for c, packed in enumerate(exchange(rows)):
                stage[staged(c, f), cols] = packed
        return carry

    lax.fori_loop(0, blocks, pack, 0)

    def params_of(texture, slot):
        def step(b, carry):
            cols = pl.ds(pl.multiple_of(b * wide, wide), wide)
            index = texture(cols).astype(jnp.int32)
            masks = bits(index, classes)
            for j in range(4):
                par_l[j, slot, :, cols] = lookup(splat, classes, j, index, masks)
            return carry

        lax.fori_loop(0, blocks, step, 0)

    greeted = count - 1 + jnp.where(greeted_below, 1, 0) + jnp.where(last, count, 0)
    pl.semaphore_wait(pltpu.get_barrier_semaphore(), greeted)

    def beside(side):
        return pltpu.make_async_remote_copy(
            src_ref=stage.at[staged(3 if side == 0 else 0, TEXTURE)],
            dst_ref=tex_h.at[side],
            send_sem=tex_send.at[side],
            recv_sem=tex_recv.at[side],
            device_id={"tile": up if side == 0 else down},
            device_id_type=MESH,
        )

    @pl.when(greeted_below)
    def _():
        beside(1).start()

    @pl.when(last)
    def _():
        beside(0).start()

    start = 0
    for g, members in enumerate(GROUPS):
        rows = pl.ds(8 * start, 8 * len(members))
        start += len(members)

        def send_in(k, carry, g=g, rows=rows):
            peer = peer_of(k)
            pltpu.make_async_remote_copy(
                src_ref=stage.at[rows, pl.ds(pl.multiple_of(peer * LANES, LANES), LANES)],
                dst_ref=colb[g].at[me],
                send_sem=in_send.at[g],
                recv_sem=in_recv.at[g],
                device_id={"layer": peer},
                device_id_type=MESH,
            ).start()
            return carry

        lax.fori_loop(0, count - 1, send_in, 0)
        colb[g][me] = stage[rows, my_cols]

    for c in range(CHUNKS):
        params_of(lambda cols, c=c: stage[staged(c, TEXTURE), cols], c + 1)

    loads[5].wait()
    loads[6].wait()
    tab[0:1, 0 : rates.shape[1]] = rate_v[...]
    inflow = jnp.take_along_axis(
        jnp.broadcast_to(tab[0:1, :], (8, LANES)), zone_v[...], axis=1, mode="promise_in_bounds"
    )
    for c in range(CHUNKS):
        ghost[c] = pltpu.roll(inflow, (6 - 2 * c) % 8, 0)

    loads[4].wait()
    inv = inv_v[...]
    inv_hi = inv.astype(jnp.bfloat16)
    inv_lo = (inv - inv_hi.astype(F32)).astype(jnp.bfloat16)
    inv_all = jnp.concatenate([inv_hi, inv_lo, inv_hi], axis=1)

    shape = (count, 8, LANES)
    sub3 = lax.broadcasted_iota(jnp.int32, shape, 1)

    def below(x):
        last = pltpu.roll(x[count - 1 :], 2, 1)
        return pltpu.roll(jnp.where(sub3 < 2, jnp.concatenate([x[1:], last], axis=0), x), 6, 1)

    def field(c, f, at):
        g = [(c, f) in members for members in GROUPS].index(True)
        row = 8 * GROUPS[g].index((c, f))
        return colb[g][at, row : row + 8, :]

    def column_params(c):
        group = 4

        def step(i, carry):
            at = pl.ds(i * group, group)
            index = field(c, TEXTURE, at).astype(jnp.int32)
            masks = bits(index, classes)
            values = [lookup(splat, classes, j, index, masks) for j in range(6)]
            for j in range(6):
                par_c[c, j, at] = values[j]
            sat = saturation(field(c, OLD, at), values[0], values[1], values[2])
            mold_c[c, at] = values[4] + values[5] * sat
            return carry

        lax.fori_loop(0, count // group, step, 0)

    def newton(p):
        chunks = PAIRS[p]
        for i, c in enumerate(chunks):
            hcur[p, :, 8 * i : 8 * i + 8, :] = field(c, HEAD, slice(None))

        def step(_, carry):
            for i, c in enumerate(chunks):
                h = hcur[p, :, 8 * i : 8 * i + 8, :]
                sat = saturation(h, par_c[c, 0], par_c[c, 1], par_c[c, 2])
                k = par_c[c, 3] * (sat * sat * sat)
                flux = (0.5 * (k + below(k))) * (h - below(h) + 1.0)
                shifted = jnp.concatenate([ghost[c][None], flux[:-1]], axis=0)
                above_it = pltpu.roll(jnp.where(sub3 >= 6, shifted, flux), 2, 1)
                moisture = par_c[c, 4] + par_c[c, 5] * sat
                misfit = (moisture - mold_c[c]) + (flux - above_it)
                mis_c[i] = misfit.reshape(count * 8, LANES)
            parts = [(i, y) for i in range(len(chunks)) for y in range(2)]
            x = jnp.concatenate([mis_c[i, pl.ds(y, layers, stride=2), :] for i, y in parts], axis=1)
            hi = x.astype(jnp.bfloat16)
            lo = (x - hi.astype(F32)).astype(jnp.bfloat16)
            stacked = jnp.concatenate([hi, hi, lo], axis=0)
            update = jnp.dot(inv_all, stacked, preferred_element_type=F32)
            for j, (i, y) in enumerate(parts):
                upd_c[i, pl.ds(y, layers, stride=2), :] = update[:, j * LANES : (j + 1) * LANES]
            for i in range(len(chunks)):
                rows = slice(8 * i, 8 * i + 8)
                hcur[p, :, rows, :] = hcur[p, :, rows, :] - upd_c[i].reshape(shape)
            return carry

        lax.fori_loop(0, ITERS, step, 0)

    def slot_rows(s):
        return pl.ds(8 * PLACES.index(s), 8)

    def pair_rows(p):
        return pl.ds(8 * PLACES.index(PAIRS[p][0] + 1), 16)

    def send_back(p):
        def send(k, carry):
            peer = peer_of(k)
            pltpu.make_async_remote_copy(
                src_ref=hcur.at[p, peer],
                dst_ref=lay.at[pair_rows(p), my_cols],
                send_sem=back_send.at[p],
                recv_sem=back_recv.at[p],
                device_id={"layer": peer},
                device_id_type=MESH,
            ).start()
            return carry

        lax.fori_loop(0, count - 1, send, 0)
        lay[pair_rows(p), my_cols] = hcur[p, me]

    def landed(p):
        part = lay.at[pair_rows(p), pl.ds(0, (count - 1) * LANES)]
        pltpu.make_async_copy(part, part, back_recv.at[p]).wait()

    def forward(c, slot, side):
        return pltpu.make_async_remote_copy(
            src_ref=lay.at[slot_rows(c + 1)],
            dst_ref=lay.at[slot_rows(slot)],
            send_sem=halo_send.at[side],
            recv_sem=halo_recv.at[side],
            device_id={"tile": up if side == 0 else down},
            device_id_type=MESH,
        )

    heads_up, heads_down = forward(3, 0, 0), forward(0, CHUNKS + 1, 1)
    def arrived(g):
        part = colb[g].at[pl.ds(0, count - 1)]
        pltpu.make_async_copy(part, part, in_recv.at[g]).wait()

    arrived(0)
    for c in PAIRS[0]:
        column_params(c)
    newton(0)

    def send_up(k, carry):
        peer = peer_of(k)
        pltpu.make_async_remote_copy(
            src_ref=hcur.at[0, peer, pl.ds(0, 8)],
            dst_ref=lay.at[slot_rows(0), my_cols],
            send_sem=halo_send.at[0],
            recv_sem=halo_recv.at[0],
            device_id={"tile": up, "layer": peer},
            device_id_type=MESH,
        ).start()
        return carry

    @pl.when(last)
    def _():
        lax.fori_loop(0, count, send_up, 0)

    send_back(0)

    @pl.when(greets_up)
    def _():
        beside(1).wait_recv()
        beside(0).start()

    landed(0)

    @pl.when(greets_up)
    def _():
        heads_up.start()


    @pl.when(first)
    def _():
        beside(0).wait_recv()
        beside(1).start()

    @pl.when(beneath)
    def _():
        heads_down.start()

    arrived(1)
    for c in PAIRS[1]:
        column_params(c)
    newton(1)
    send_back(1)

    @pl.when(jnp.logical_not(beneath))
    def _():
        tex_h[0] = jnp.zeros(tex_h.shape[1:], F32)
        lay[slot_rows(0)] = lay[slot_rows(1)]

    @pl.when(jnp.logical_not(above))
    def _():
        tex_h[1] = jnp.zeros(tex_h.shape[1:], F32)
        lay[slot_rows(CHUNKS + 1)] = lay[slot_rows(CHUNKS)]

    def odd_rows(shape):
        return (lax.broadcasted_iota(jnp.int32, shape, 0) & 1) == 1

    def head(src, s, cols):
        return src[slot_rows(s), cols] if src is lay else src[s, :, cols]

    def prepare(src, dst, s):
        h = head(src, s, slice(None))
        sat = saturation(h, par_l[0, s], par_l[1, s], par_l[2, s])
        k = par_l[3, s] * (sat * sat * sat)
        odd = odd_rows(h.shape)
        other_h = jnp.where(odd, pltpu.roll(h, 1, 0), pltpu.roll(h, 7, 0))
        other_k = jnp.where(odd, pltpu.roll(k, 1, 0), pltpu.roll(k, 7, 0))
        dst[0, s] = k
        dst[1, s] = other_h
        dst[2, s] = other_k
        lane = lax.broadcasted_iota(jnp.int32, h.shape, 1)
        flow = (k + pltpu.roll(k, width - 1, 1)) * (pltpu.roll(h, width - 1, 1) - h)
        flow = jnp.where(lane == width - 1, 0.0, flow)
        dst[3, s] = flow - pltpu.roll(flow, 1, 1) + (k + other_k) * (other_h - h)

    def advanced(src, by, s, cols):
        h, k = head(src, s, cols), by[0, s, :, cols]
        odd = odd_rows(h.shape)
        after, before = min(s + 1, CHUNKS + 1), max(s - 1, 0)
        side_h = jnp.where(odd, by[1, after, :, cols], by[1, before, :, cols])
        side_k = jnp.where(odd, by[2, after, :, cols], by[2, before, :, cols])
        side = (k + side_k) * (side_h - h)
        if s == 1:
            side = jnp.where(jnp.logical_and(tile == 0, jnp.logical_not(odd)), 0.0, side)
        if s == CHUNKS:
            side = jnp.where(jnp.logical_and(tile == tiles - 1, odd), 0.0, side)
        return h + (0.5 * OMEGA) * (by[3, s, :, cols] + side)

    def advance(src, by, dst, s):
        dst[s] = advanced(src, by, s, slice(None))

    prepare(lay, ready, 4)
    prepare(lay, ready, 1)

    @pl.when(last)
    def _():
        beside(1).wait_recv()

    params_of(lambda cols: tex_h[1, :, cols], 5)

    def low_side():
        @pl.when(greeted_below)
        def _():
            beside(0).wait_recv()

        params_of(lambda cols: tex_h[0, :, cols], 0)

        @pl.when(beneath)
        def _():
            heads_up.wait_recv()

        prepare(lay, ready, 0)
        advance(lay, ready, lay2, 0)
        prepare(lay2, ready2, 0)

    pl.when(jnp.logical_not(first))(low_side)

    @pl.when(above)
    def _():
        heads_down.wait_recv()

    prepare(lay, ready, 5)
    advance(lay, ready, lay2, 5)
    prepare(lay2, ready2, 5)
    landed(1)
    prepare(lay, ready, 2)
    prepare(lay, ready, 3)
    for s in (2, 3, 4):
        advance(lay, ready, lay2, s)
        prepare(lay2, ready2, s)
    pl.when(first)(low_side)
    advance(lay, ready, lay2, 1)
    prepare(lay2, ready2, 1)
    def finish(b, carry):
        cols = pl.ds(pl.multiple_of(b * wide, wide), wide)
        tops = [advanced(lay2, ready2, c + 1, cols) for c in range(CHUNKS)]
        for l, rows in enumerate(exchange(tops)):
            nat_h[8 * l : 8 * l + 8, cols] = rows
        pltpu.make_async_copy(nat_h.at[:, cols], out.at[:, cols], load_sem.at[7]).start()
        return carry

    lax.fori_loop(0, blocks, finish, 0)
    for g in range(len(GROUPS)):
        part = colb[g].at[pl.ds(0, count - 1)]
        pltpu.make_async_copy(part, part, in_send.at[g]).wait()
    for p in range(len(PAIRS)):
        part = hcur.at[p, pl.ds(0, count - 1)]
        pltpu.make_async_copy(part, part, back_send.at[p]).wait()

    @pl.when(above)
    def _():
        heads_up.wait_send()
        beside(0).wait_send()

    @pl.when(beneath)
    def _():
        heads_down.wait_send()
        beside(1).wait_send()

    pltpu.make_async_copy(nat_h, out, load_sem.at[7]).wait()


def body(pressure, old_pressure, texture, zones, rates, vg_table, approx_inverse):
    count = lax.axis_size("layer")
    tiles = lax.axis_size("tile")
    depth, tall, width = pressure.shape
    rows = depth * tall
    flat = (rows, width)
    slots = (CHUNKS + 2, 2 * depth, width)
    column = (count, 2 * depth, LANES)
    classes = vg_table.shape[1]

    def vmem(*shape, dtype=F32):
        return pltpu.VMEM(shape, dtype)

    result = pl.pallas_call(
        functools.partial(kernel, count, tiles),
        out_shape=jax.ShapeDtypeStruct(flat, F32),
        in_specs=[pl.BlockSpec(memory_space=pltpu.HBM)] * 7,
        out_specs=pl.BlockSpec(memory_space=pltpu.HBM),
        scratch_shapes=[
            vmem(*flat),
            vmem(*flat),
            vmem(*flat, dtype=jnp.int32),
            vmem(CHUNKS * FIELDS * 2 * depth, width),
            *(vmem(count, len(g) * 2 * depth, LANES) for g in GROUPS),
            vmem(len(PAIRS), count, 4 * depth, LANES),
            vmem(CHUNKS, 6, *column),
            vmem(CHUNKS, *column),
            vmem(2, count * 2 * depth, LANES),
            vmem(2, count * 2 * depth, LANES),
            vmem(CHUNKS, 8, LANES),
            vmem((CHUNKS + 2) * 2 * depth, width),
            vmem(*slots),
            vmem(4, *slots),
            vmem(4, *slots),
            vmem(4, *slots),
            vmem(2, 2 * depth, width),
            vmem(tall, LANES, dtype=jnp.int32),
            vmem(1, rates.shape[0]),
            vmem(*vg_table.shape),
            vmem(8, LANES),
            vmem(6, classes, 8, LANES),
            vmem(*approx_inverse.shape),
            pltpu.SemaphoreType.DMA((8,)),
            pltpu.SemaphoreType.DMA((len(GROUPS),)),
            pltpu.SemaphoreType.DMA((len(GROUPS),)),
            pltpu.SemaphoreType.DMA((len(PAIRS),)),
            pltpu.SemaphoreType.DMA((len(PAIRS),)),
            pltpu.SemaphoreType.DMA((2,)),
            pltpu.SemaphoreType.DMA((2,)),
            pltpu.SemaphoreType.DMA((2,)),
            pltpu.SemaphoreType.DMA((2,)),
        ],
        compiler_params=pltpu.CompilerParams(
            collective_id=0, has_side_effects=True, vmem_limit_bytes=56 * 1024 * 1024
        ),
    )(
        pressure.reshape(flat),
        old_pressure.reshape(flat),
        texture.reshape(flat),
        zones,
        rates.reshape(1, -1),
        vg_table,
        approx_inverse,
    )
    return result.reshape(pressure.shape)


def solution(mesh):
    placed = (
        P("layer", "tile", None),
        P("layer", "tile", None),
        P("layer", "tile", None),
        P("tile", None),
        P(),
        P(),
        P(),
    )
    return jax.shard_map(
        body, mesh=mesh, in_specs=placed, out_specs=P("layer", "tile", None), check_vma=False
    )
```

```python
import functools

import jax
import jax.numpy as jnp
from jax import lax
from jax.experimental import pallas as pl
from jax.experimental.pallas import tpu as pltpu
from jax.sharding import PartitionSpec as P

ITERS = 3
OMEGA = 0.2
LOG2E = 1.4426950408889634
MESH = pl.DeviceIdType.MESH
LANES = 128
CHUNKS = 4
FIELDS = 3
HEAD, OLD, TEXTURE = range(FIELDS)
SEGMENTS = (
    tuple((c, f) for c in (1, 2) for f in (TEXTURE, OLD)),
    tuple((c, f) for c in (3, 0) for f in (TEXTURE, OLD)),
    tuple((c, HEAD) for c in (3, 0)),
    tuple((c, HEAD) for c in (1, 2)),
)
TILES = sum(SEGMENTS, ())
USUAL = ((0, 1), (2, 3))
BORDER = ((1, 2), (0,), (3,))
PAIRS = ((3, 0), (1, 2))
PLACES = (0, 4, 1, 2, 3, 5)
SIDE = 4
TURNS = sorted(
    range(1, SIDE * SIDE),
    key=lambda v: (not v & 2, -(v % SIDE) - min(v // SIDE, SIDE - v // SIDE)),
)
F32 = jnp.float32


def words(values):
    packed = [sum(v << (4 * i) for i, v in enumerate(values[j : j + 8])) for j in (0, 8)]
    return [w - (1 << 32) if w >= 1 << 31 else w for w in packed]


TURN_WORDS = words(TURNS + [0])


def turn(k):
    word = jnp.where(k < 8, jnp.int32(TURN_WORDS[0]), jnp.int32(TURN_WORDS[1]))
    return lax.shift_right_logical(word, 4 * lax.rem(k, 8)) & (SIDE * SIDE - 1)


def saturation(head, la, n, negp):
    suction = jnp.log(1.0 + jnp.exp2(jnp.abs(head) * (-LOG2E))) + jnp.maximum(-head, 0.0)
    power = jnp.exp2(n * jnp.log(suction) + la)
    return jnp.exp2(negp * jnp.log(1.0 + power))


def exchange(tiles):
    sub = lax.broadcasted_iota(jnp.int32, tiles[0].shape, 0)
    low, even = sub < 4, (sub & 2) == 0
    a, b, c, d = tiles

    def halves(p, q):
        r = pltpu.roll(jnp.where(low, q, p), 4, 0)
        return jnp.where(low, p, r), jnp.where(low, r, q)

    def pairs(p, q):
        return (
            jnp.where(even, p, pltpu.roll(q, 2, 0)),
            jnp.where(even, pltpu.roll(p, 6, 0), q),
        )

    a, c = halves(a, c)
    b, d = halves(b, d)
    a, b = pairs(a, b)
    c, d = pairs(c, d)
    return a, b, c, d


def lookup(splat, classes, row, index, masks):
    def constant(k):
        tile = splat[row, min(k, classes - 1)]
        if len(index.shape) == 2:
            return jnp.concatenate([tile] * (index.shape[1] // LANES), axis=1)
        return jnp.broadcast_to(tile[None], index.shape)

    level = [constant(k) for k in range(classes)]
    for mask in masks:
        level = [
            jnp.where(mask, level[k + 1], level[k]) if k + 1 < len(level) else level[k]
            for k in range(0, len(level), 2)
        ]
    return level[0]


def bits(index, classes):
    return [(index & (1 << b)) != 0 for b in range((classes - 1).bit_length())]


def kernel(
    count,
    tiles,
    press,
    old,
    tex,
    zones,
    rates,
    table,
    inverse,
    out,
    nat_h,
    nat_o,
    nat_t,
    stage,
    colb,
    hcur,
    par_c,
    mold_c,
    mis_c,
    upd_c,
    ghost,
    lay,
    lay2,
    ready,
    ready2,
    par_l,
    tex_h,
    zone_v,
    rate_v,
    table_v,
    tab,
    splat,
    inv_v,
    load_sem,
    in_send,
    in_recv,
    back_send,
    back_recv,
    halo_send,
    halo_recv,
    tex_send,
    tex_recv,
):
    me = lax.axis_index("layer")
    tile = lax.axis_index("tile")
    width = press.shape[1]
    depth = press.shape[0] // 8
    classes = table.shape[1]
    layers = count * depth
    down = lax.rem(tile + tiles - 1, tiles)
    up = lax.rem(tile + 1, tiles)
    wide = 512
    blocks = width // wide

    def peer_of(k):
        return jnp.bitwise_xor(me, turn(k))

    run = tiles // 2
    my_cols = pl.ds(pl.multiple_of(me * LANES, LANES), LANES)
    loads = [
        pltpu.make_async_copy(table, table_v, load_sem.at[0]),
        pltpu.make_async_copy(press, nat_h, load_sem.at[1]),
        pltpu.make_async_copy(old, nat_o, load_sem.at[2]),
        pltpu.make_async_copy(tex, nat_t, load_sem.at[3]),
        pltpu.make_async_copy(inverse, inv_v, load_sem.at[4]),
        pltpu.make_async_copy(zones.at[:, my_cols], zone_v, load_sem.at[5]),
        pltpu.make_async_copy(rates, rate_v, load_sem.at[6]),
    ]
    for load in loads:
        load.start()

    above, beneath = tile != tiles - 1, tile != 0
    last, first = tile == run - 1, tile == run
    greets_up = jnp.logical_and(above, jnp.logical_not(last))
    greeted_below = jnp.logical_and(beneath, jnp.logical_not(first))
    odd_tile = lax.rem(tile, 2) == 1
    straight_down = jnp.logical_and(greeted_below, jnp.logical_not(odd_tile))
    last_chip = lax.rem(tile, run) >= run - 2

    def hello(device):
        pl.semaphore_signal(
            pltpu.get_barrier_semaphore(), inc=1, device_id=device, device_id_type=MESH
        )

    def greet(k, carry):
        hello({"layer": peer_of(k)})
        return carry

    lax.fori_loop(0, count - 1, greet, 0)

    def greet_above(k, carry):
        hello({"tile": up, "layer": peer_of(k)})
        return carry

    @pl.when(jnp.logical_and(greets_up, odd_tile))
    def _():
        lax.fori_loop(0, count, greet_above, 0)

    @pl.when(jnp.logical_and(greets_up, jnp.logical_not(odd_tile)))
    def _():
        hello({"tile": up})

    def greet_below(k, carry):
        hello({"tile": down, "layer": peer_of(k)})
        return carry

    @pl.when(first)
    def _():
        lax.fori_loop(0, count, greet_below, 0)


    loads[0].wait()
    tab[...] = jnp.ones(tab.shape, F32)
    tab[0:5, 0:classes] = table_v[...]
    t_a, t_n, t_r, t_s, t_k = (tab[j : j + 1, :] for j in range(5))
    derived = (
        t_n * jnp.log(t_a) * LOG2E,
        t_n * LOG2E,
        (1.0 / t_n - 1.0) * LOG2E,
        t_k,
        t_r,
        t_s - t_r,
    )
    for j, row in enumerate(derived):
        for k in range(classes):
            splat[j, k] = jnp.broadcast_to(row[:, k : k + 1], (8, LANES))

    def staged(c, f):
        return pl.ds(8 * TILES.index((c, f)), 8)

    for load in loads[1:4]:
        load.wait()

    def pack(b, carry):
        cols = pl.ds(pl.multiple_of(b * wide, wide), wide)
        for f, nat in enumerate((nat_h, nat_o, nat_t)):
            rows = [nat[8 * l : 8 * l + 8, cols] for l in range(depth)]
            if f == 2:
                rows = [r.astype(F32) for r in rows]
            for c, packed in enumerate(exchange(rows)):
                stage[staged(c, f), cols] = packed
        return carry

    lax.fori_loop(0, blocks, pack, 0)

    def params_of(texture, slot):
        def step(b, carry):
            cols = pl.ds(pl.multiple_of(b * wide, wide), wide)
            index = texture(cols).astype(jnp.int32)
            masks = bits(index, classes)
            for j in range(4):
                par_l[j, slot, :, cols] = lookup(splat, classes, j, index, masks)
            return carry

        lax.fori_loop(0, blocks, step, 0)

    greeted = count - 1 + jnp.where(last, count, 0)
    greeted = greeted + jnp.where(straight_down, count, jnp.where(greeted_below, 1, 0))
    pl.semaphore_wait(pltpu.get_barrier_semaphore(), greeted)

    def beside(side):
        return pltpu.make_async_remote_copy(
            src_ref=stage.at[staged(3 if side == 0 else 0, TEXTURE)],
            dst_ref=tex_h.at[side],
            send_sem=tex_send.at[side],
            recv_sem=tex_recv.at[side],
            device_id={"tile": up if side == 0 else down},
            device_id_type=MESH,
        )

    @pl.when(greeted_below)
    def _():
        beside(1).start()

    @pl.when(last)
    def _():
        beside(0).start()

    def rows_of(segments):
        start = 8 * sum(len(members) for members in SEGMENTS[: segments[0]])
        return pl.ds(start, 8 * sum(len(SEGMENTS[g]) for g in segments))

    def send_copies(copies):
        for g, segments in enumerate(copies):
            rows = rows_of(segments)

            def send_in(k, carry, g=g, rows=rows):
                peer = peer_of(k)
                pltpu.make_async_remote_copy(
                    src_ref=stage.at[rows, pl.ds(pl.multiple_of(peer * LANES, LANES), LANES)],
                    dst_ref=colb.at[me, rows],
                    send_sem=in_send.at[g],
                    recv_sem=in_recv.at[g],
                    device_id={"layer": peer},
                    device_id_type=MESH,
                ).start()
                return carry

            lax.fori_loop(0, count - 1, send_in, 0)

    def others(copies, g, sems):
        part = colb.at[pl.ds(0, count - 1), rows_of(copies[g])]
        pltpu.make_async_copy(part, part, sems.at[g]).wait()

    def in_border(usual, border):
        pl.when(jnp.logical_not(last))(usual)
        pl.when(last)(border)

    in_border(lambda: send_copies(USUAL), lambda: send_copies(BORDER))
    colb[me] = stage[:, my_cols]

    for c in range(CHUNKS):
        params_of(lambda cols, c=c: stage[staged(c, TEXTURE), cols], c + 1)

    loads[5].wait()
    loads[6].wait()
    tab[0:1, 0 : rates.shape[1]] = rate_v[...]
    inflow = jnp.take_along_axis(
        jnp.broadcast_to(tab[0:1, :], (8, LANES)), zone_v[...], axis=1, mode="promise_in_bounds"
    )
    for c in range(CHUNKS):
        ghost[c] = pltpu.roll(inflow, (6 - 2 * c) % 8, 0)

    loads[4].wait()
    inv = inv_v[...]
    inv_hi = inv.astype(jnp.bfloat16)
    inv_lo = (inv - inv_hi.astype(F32)).astype(jnp.bfloat16)
    inv_all = jnp.concatenate([inv_hi, inv_lo, inv_hi], axis=1)

    shape = (count, 8, LANES)
    sub3 = lax.broadcasted_iota(jnp.int32, shape, 1)

    def below(x):
        last = pltpu.roll(x[count - 1 :], 2, 1)
        return pltpu.roll(jnp.where(sub3 < 2, jnp.concatenate([x[1:], last], axis=0), x), 6, 1)

    def field(c, f, at):
        row = 8 * TILES.index((c, f))
        return colb[at, row : row + 8, :]

    def column_params(c):
        group = 4

        def step(i, carry):
            at = pl.ds(i * group, group)
            index = field(c, TEXTURE, at).astype(jnp.int32)
            masks = bits(index, classes)
            values = [lookup(splat, classes, j, index, masks) for j in range(6)]
            for j in range(6):
                par_c[c, j, at] = values[j]
            sat = saturation(field(c, OLD, at), values[0], values[1], values[2])
            mold_c[c, at] = values[4] + values[5] * sat
            return carry

        lax.fori_loop(0, count // group, step, 0)

    def newton(p):
        chunks = PAIRS[p]
        for i, c in enumerate(chunks):
            hcur[p, :, 8 * i : 8 * i + 8, :] = field(c, HEAD, slice(None))

        def step(_, carry):
            for i, c in enumerate(chunks):
                h = hcur[p, :, 8 * i : 8 * i + 8, :]
                sat = saturation(h, par_c[c, 0], par_c[c, 1], par_c[c, 2])
                k = par_c[c, 3] * (sat * sat * sat)
                flux = (0.5 * (k + below(k))) * (h - below(h) + 1.0)
                shifted = jnp.concatenate([ghost[c][None], flux[:-1]], axis=0)
                above_it = pltpu.roll(jnp.where(sub3 >= 6, shifted, flux), 2, 1)
                moisture = par_c[c, 4] + par_c[c, 5] * sat
                misfit = (moisture - mold_c[c]) + (flux - above_it)
                mis_c[i] = misfit.reshape(count * 8, LANES)
            parts = [(i, y) for i in range(len(chunks)) for y in range(2)]
            x = jnp.concatenate([mis_c[i, pl.ds(y, layers, stride=2), :] for i, y in parts], axis=1)
            hi = x.astype(jnp.bfloat16)
            lo = (x - hi.astype(F32)).astype(jnp.bfloat16)
            stacked = jnp.concatenate([hi, hi, lo], axis=0)
            update = jnp.dot(inv_all, stacked, preferred_element_type=F32)
            for j, (i, y) in enumerate(parts):
                upd_c[i, pl.ds(y, layers, stride=2), :] = update[:, j * LANES : (j + 1) * LANES]
            for i in range(len(chunks)):
                rows = slice(8 * i, 8 * i + 8)
                hcur[p, :, rows, :] = hcur[p, :, rows, :] - upd_c[i].reshape(shape)
            return carry

        lax.fori_loop(0, ITERS, step, 0)

    def slot_rows(s):
        return pl.ds(8 * PLACES.index(s), 8)

    def pair_rows(p):
        return pl.ds(8 * PLACES.index(PAIRS[p][0] + 1), 16)

    def send_back(p):
        def send(k, carry):
            peer = peer_of(k)
            pltpu.make_async_remote_copy(
                src_ref=hcur.at[p, peer],
                dst_ref=lay.at[pair_rows(p), my_cols],
                send_sem=back_send.at[p],
                recv_sem=back_recv.at[p],
                device_id={"layer": peer},
                device_id_type=MESH,
            ).start()
            return carry

        lax.fori_loop(0, count - 1, send, 0)
        lay[pair_rows(p), my_cols] = hcur[p, me]

    def landed(p):
        part = lay.at[pair_rows(p), pl.ds(0, (count - 1) * LANES)]
        pltpu.make_async_copy(part, part, back_recv.at[p]).wait()

    def forward(c, slot, side):
        return pltpu.make_async_remote_copy(
            src_ref=lay.at[slot_rows(c + 1)],
            dst_ref=lay.at[slot_rows(slot)],
            send_sem=halo_send.at[side],
            recv_sem=halo_recv.at[side],
            device_id={"tile": up if side == 0 else down},
            device_id_type=MESH,
        )

    heads_up, heads_down = forward(3, 0, 0), forward(0, CHUNKS + 1, 1)
    in_border(lambda: others(USUAL, 0, in_recv), lambda: others(BORDER, 0, in_recv))
    for c in PAIRS[0]:
        column_params(c)

    @pl.when(jnp.logical_not(last))
    def _():
        for c in PAIRS[1]:
            column_params(c)

    pl.when(jnp.logical_not(last))(lambda: others(USUAL, 1, in_recv))
    newton(0)

    def send_straight(row, slot, side, device):
        def send(k, carry):
            peer = peer_of(k)
            pltpu.make_async_remote_copy(
                src_ref=hcur.at[0, peer, pl.ds(row, 8)],
                dst_ref=lay.at[slot_rows(slot), my_cols],
                send_sem=halo_send.at[side],
                recv_sem=halo_recv.at[side],
                device_id={"tile": device, "layer": peer},
                device_id_type=MESH,
            ).start()
            return carry

        lax.fori_loop(0, count, send, 0)

    @pl.when(last)
    def _():
        send_straight(0, 0, 0, up)

    @pl.when(jnp.logical_and(straight_down, jnp.logical_not(last_chip)))
    def _():
        send_straight(8, CHUNKS + 1, 1, down)

    pl.when(jnp.logical_not(last))(lambda: send_back(0))

    @pl.when(jnp.logical_and(straight_down, last_chip))
    def _():
        send_straight(8, CHUNKS + 1, 1, down)

    @pl.when(last)
    def _():
        others(BORDER, 1, in_recv)
        for c in PAIRS[1]:
            column_params(c)
        others(BORDER, 2, in_recv)
        send_back(0)

    newton(1)
    send_back(1)

    @pl.when(greets_up)
    def _():
        beside(1).wait_recv()
        beside(0).start()

    landed(0)

    @pl.when(greets_up)
    def _():
        heads_up.start()


    @pl.when(first)
    def _():
        beside(0).wait_recv()
        beside(1).start()

    @pl.when(jnp.logical_and(beneath, jnp.logical_not(straight_down)))
    def _():
        heads_down.start()

    @pl.when(jnp.logical_not(beneath))
    def _():
        tex_h[0] = jnp.zeros(tex_h.shape[1:], F32)
        lay[slot_rows(0)] = lay[slot_rows(1)]

    @pl.when(jnp.logical_not(above))
    def _():
        tex_h[1] = jnp.zeros(tex_h.shape[1:], F32)
        lay[slot_rows(CHUNKS + 1)] = lay[slot_rows(CHUNKS)]

    def odd_rows(shape):
        return (lax.broadcasted_iota(jnp.int32, shape, 0) & 1) == 1

    def head(src, s, cols):
        return src[slot_rows(s), cols] if src is lay else src[s, :, cols]

    def prepare(src, dst, s):
        h = head(src, s, slice(None))
        sat = saturation(h, par_l[0, s], par_l[1, s], par_l[2, s])
        k = par_l[3, s] * (sat * sat * sat)
        odd = odd_rows(h.shape)
        other_h = jnp.where(odd, pltpu.roll(h, 1, 0), pltpu.roll(h, 7, 0))
        other_k = jnp.where(odd, pltpu.roll(k, 1, 0), pltpu.roll(k, 7, 0))
        dst[0, s] = k
        dst[1, s] = other_h
        dst[2, s] = other_k
        lane = lax.broadcasted_iota(jnp.int32, h.shape, 1)
        flow = (k + pltpu.roll(k, width - 1, 1)) * (pltpu.roll(h, width - 1, 1) - h)
        flow = jnp.where(lane == width - 1, 0.0, flow)
        dst[3, s] = flow - pltpu.roll(flow, 1, 1) + (k + other_k) * (other_h - h)

    def advanced(src, by, s, cols):
        h, k = head(src, s, cols), by[0, s, :, cols]
        odd = odd_rows(h.shape)
        after, before = min(s + 1, CHUNKS + 1), max(s - 1, 0)
        side_h = jnp.where(odd, by[1, after, :, cols], by[1, before, :, cols])
        side_k = jnp.where(odd, by[2, after, :, cols], by[2, before, :, cols])
        side = (k + side_k) * (side_h - h)
        if s == 1:
            side = jnp.where(jnp.logical_and(tile == 0, jnp.logical_not(odd)), 0.0, side)
        if s == CHUNKS:
            side = jnp.where(jnp.logical_and(tile == tiles - 1, odd), 0.0, side)
        return h + (0.5 * OMEGA) * (by[3, s, :, cols] + side)

    def advance(src, by, dst, s):
        dst[s] = advanced(src, by, s, slice(None))

    prepare(lay, ready, 4)
    prepare(lay, ready, 1)

    @pl.when(last)
    def _():
        beside(1).wait_recv()

    params_of(lambda cols: tex_h[1, :, cols], 5)

    def low_side():
        @pl.when(greeted_below)
        def _():
            beside(0).wait_recv()

        params_of(lambda cols: tex_h[0, :, cols], 0)

        @pl.when(beneath)
        def _():
            heads_up.wait_recv()

        prepare(lay, ready, 0)
        advance(lay, ready, lay2, 0)
        prepare(lay2, ready2, 0)

    pl.when(jnp.logical_not(first))(low_side)

    @pl.when(above)
    def _():
        heads_down.wait_recv()

    prepare(lay, ready, 5)
    advance(lay, ready, lay2, 5)
    prepare(lay2, ready2, 5)
    landed(1)
    prepare(lay, ready, 2)
    prepare(lay, ready, 3)
    for s in (2, 3, 4):
        advance(lay, ready, lay2, s)
        prepare(lay2, ready2, s)
    pl.when(first)(low_side)
    advance(lay, ready, lay2, 1)
    prepare(lay2, ready2, 1)
    def finish(b, carry):
        cols = pl.ds(pl.multiple_of(b * wide, wide), wide)
        tops = [advanced(lay2, ready2, c + 1, cols) for c in range(CHUNKS)]
        for l, rows in enumerate(exchange(tops)):
            nat_h[8 * l : 8 * l + 8, cols] = rows
        pltpu.make_async_copy(nat_h.at[:, cols], out.at[:, cols], load_sem.at[7]).start()
        return carry

    lax.fori_loop(0, blocks, finish, 0)
    def sent(copies):
        for g in range(len(copies)):
            others(copies, g, in_send)

    in_border(lambda: sent(USUAL), lambda: sent(BORDER))
    for p in range(len(PAIRS)):
        part = hcur.at[p, pl.ds(0, count - 1)]
        pltpu.make_async_copy(part, part, back_send.at[p]).wait()

    @pl.when(above)
    def _():
        heads_up.wait_send()
        beside(0).wait_send()

    @pl.when(beneath)
    def _():
        heads_down.wait_send()
        beside(1).wait_send()

    pltpu.make_async_copy(nat_h, out, load_sem.at[7]).wait()


def body(pressure, old_pressure, texture, zones, rates, vg_table, approx_inverse):
    count = lax.axis_size("layer")
    tiles = lax.axis_size("tile")
    depth, tall, width = pressure.shape
    rows = depth * tall
    flat = (rows, width)
    slots = (CHUNKS + 2, 2 * depth, width)
    column = (count, 2 * depth, LANES)
    classes = vg_table.shape[1]

    def vmem(*shape, dtype=F32):
        return pltpu.VMEM(shape, dtype)

    result = pl.pallas_call(
        functools.partial(kernel, count, tiles),
        out_shape=jax.ShapeDtypeStruct(flat, F32),
        in_specs=[pl.BlockSpec(memory_space=pltpu.HBM)] * 7,
        out_specs=pl.BlockSpec(memory_space=pltpu.HBM),
        scratch_shapes=[
            vmem(*flat),
            vmem(*flat),
            vmem(*flat, dtype=jnp.int32),
            vmem(CHUNKS * FIELDS * 2 * depth, width),
            vmem(count, len(TILES) * 2 * depth, LANES),
            vmem(len(PAIRS), count, 4 * depth, LANES),
            vmem(CHUNKS, 6, *column),
            vmem(CHUNKS, *column),
            vmem(2, count * 2 * depth, LANES),
            vmem(2, count * 2 * depth, LANES),
            vmem(CHUNKS, 8, LANES),
            vmem((CHUNKS + 2) * 2 * depth, width),
            vmem(*slots),
            vmem(4, *slots),
            vmem(4, *slots),
            vmem(4, *slots),
            vmem(2, 2 * depth, width),
            vmem(tall, LANES, dtype=jnp.int32),
            vmem(1, rates.shape[0]),
            vmem(*vg_table.shape),
            vmem(8, LANES),
            vmem(6, classes, 8, LANES),
            vmem(*approx_inverse.shape),
            pltpu.SemaphoreType.DMA((8,)),
            pltpu.SemaphoreType.DMA((len(BORDER),)),
            pltpu.SemaphoreType.DMA((len(BORDER),)),
            pltpu.SemaphoreType.DMA((len(PAIRS),)),
            pltpu.SemaphoreType.DMA((len(PAIRS),)),
            pltpu.SemaphoreType.DMA((2,)),
            pltpu.SemaphoreType.DMA((2,)),
            pltpu.SemaphoreType.DMA((2,)),
            pltpu.SemaphoreType.DMA((2,)),
        ],
        compiler_params=pltpu.CompilerParams(
            collective_id=0, has_side_effects=True, vmem_limit_bytes=56 * 1024 * 1024
        ),
    )(
        pressure.reshape(flat),
        old_pressure.reshape(flat),
        texture.reshape(flat),
        zones,
        rates.reshape(1, -1),
        vg_table,
        approx_inverse,
    )
    return result.reshape(pressure.shape)


def solution(mesh):
    placed = (
        P("layer", "tile", None),
        P("layer", "tile", None),
        P("layer", "tile", None),
        P("tile", None),
        P(),
        P(),
        P(),
    )
    return jax.shard_map(
        body, mesh=mesh, in_specs=placed, out_specs=P("layer", "tile", None), check_vma=False
    )
```

```python
import functools

import jax
import jax.numpy as jnp
from jax import lax
from jax.experimental import pallas as pl
from jax.experimental.pallas import tpu as pltpu
from jax.sharding import PartitionSpec as P

ITERS = 3
OMEGA = 0.2
LOG2E = 1.4426950408889634
MESH = pl.DeviceIdType.MESH
LANES = 128
CHUNKS = 4
FIELDS = 3
HEAD, OLD, TEXTURE = range(FIELDS)
SEGMENTS = (
    tuple((c, f) for c in (1, 2) for f in (TEXTURE, OLD)),
    tuple((c, f) for c in (3, 0) for f in (TEXTURE, OLD)),
    tuple((c, HEAD) for c in (3, 0)),
    tuple((c, HEAD) for c in (1, 2)),
)
TILES = sum(SEGMENTS, ())
USUAL = ((0, 1), (2,), (3,))
BORDER = ((1, 2), (0,), (3,))
PAIRS = ((3, 0), (1, 2))
PLACES = (0, 4, 1, 2, 3, 5)
SIDE = 4
TURNS = sorted(
    range(1, SIDE * SIDE),
    key=lambda v: (not v & 2, -(v % SIDE) - min(v // SIDE, SIDE - v // SIDE)),
)
F32 = jnp.float32


def words(values):
    packed = [sum(v << (4 * i) for i, v in enumerate(values[j : j + 8])) for j in (0, 8)]
    return [w - (1 << 32) if w >= 1 << 31 else w for w in packed]


TURN_WORDS = words(TURNS + [0])


def turn(k):
    word = jnp.where(k < 8, jnp.int32(TURN_WORDS[0]), jnp.int32(TURN_WORDS[1]))
    return lax.shift_right_logical(word, 4 * lax.rem(k, 8)) & (SIDE * SIDE - 1)


def saturation(head, la, n, negp):
    suction = jnp.log(1.0 + jnp.exp2(jnp.abs(head) * (-LOG2E))) + jnp.maximum(-head, 0.0)
    power = jnp.exp2(n * jnp.log(suction) + la)
    return jnp.exp2(negp * jnp.log(1.0 + power))


def exchange(tiles):
    sub = lax.broadcasted_iota(jnp.int32, tiles[0].shape, 0)
    low, even = sub < 4, (sub & 2) == 0
    a, b, c, d = tiles

    def halves(p, q):
        r = pltpu.roll(jnp.where(low, q, p), 4, 0)
        return jnp.where(low, p, r), jnp.where(low, r, q)

    def pairs(p, q):
        return (
            jnp.where(even, p, pltpu.roll(q, 2, 0)),
            jnp.where(even, pltpu.roll(p, 6, 0), q),
        )

    a, c = halves(a, c)
    b, d = halves(b, d)
    a, b = pairs(a, b)
    c, d = pairs(c, d)
    return a, b, c, d


def lookup(splat, classes, row, index, masks):
    def constant(k):
        tile = splat[row, min(k, classes - 1)]
        if len(index.shape) == 2:
            return jnp.concatenate([tile] * (index.shape[1] // LANES), axis=1)
        return jnp.broadcast_to(tile[None], index.shape)

    level = [constant(k) for k in range(classes)]
    for mask in masks:
        level = [
            jnp.where(mask, level[k + 1], level[k]) if k + 1 < len(level) else level[k]
            for k in range(0, len(level), 2)
        ]
    return level[0]


def bits(index, classes):
    return [(index & (1 << b)) != 0 for b in range((classes - 1).bit_length())]


def kernel(
    count,
    tiles,
    press,
    old,
    tex,
    zones,
    rates,
    table,
    inverse,
    out,
    nat_h,
    nat_o,
    nat_t,
    stage,
    colb,
    hcur,
    par_c,
    mold_c,
    mis_c,
    upd_c,
    ghost,
    lay,
    lay2,
    ready,
    ready2,
    par_l,
    tex_h,
    zone_v,
    rate_v,
    table_v,
    tab,
    splat,
    inv_v,
    load_sem,
    in_send,
    in_recv,
    back_send,
    back_recv,
    halo_send,
    halo_recv,
    tex_send,
    tex_recv,
):
    me = lax.axis_index("layer")
    tile = lax.axis_index("tile")
    width = press.shape[1]
    depth = press.shape[0] // 8
    classes = table.shape[1]
    layers = count * depth
    down = lax.rem(tile + tiles - 1, tiles)
    up = lax.rem(tile + 1, tiles)
    wide = 512
    blocks = width // wide

    def peer_of(k):
        return jnp.bitwise_xor(me, turn(k))

    run = tiles // 2
    my_cols = pl.ds(pl.multiple_of(me * LANES, LANES), LANES)
    loads = [
        pltpu.make_async_copy(table, table_v, load_sem.at[0]),
        pltpu.make_async_copy(press, nat_h, load_sem.at[1]),
        pltpu.make_async_copy(old, nat_o, load_sem.at[2]),
        pltpu.make_async_copy(tex, nat_t, load_sem.at[3]),
        pltpu.make_async_copy(inverse, inv_v, load_sem.at[4]),
        pltpu.make_async_copy(zones.at[:, my_cols], zone_v, load_sem.at[5]),
        pltpu.make_async_copy(rates, rate_v, load_sem.at[6]),
    ]
    for load in loads:
        load.start()

    above, beneath = tile != tiles - 1, tile != 0
    last, first = tile == run - 1, tile == run
    greets_up = jnp.logical_and(above, jnp.logical_not(last))
    greeted_below = jnp.logical_and(beneath, jnp.logical_not(first))
    odd_tile = lax.rem(tile, 2) == 1
    straight_down = jnp.logical_and(greeted_below, jnp.logical_not(odd_tile))

    def hello(device):
        pl.semaphore_signal(
            pltpu.get_barrier_semaphore(), inc=1, device_id=device, device_id_type=MESH
        )

    def greet(k, carry):
        hello({"layer": peer_of(k)})
        return carry

    lax.fori_loop(0, count - 1, greet, 0)

    def greet_above(k, carry):
        hello({"tile": up, "layer": peer_of(k)})
        return carry

    @pl.when(jnp.logical_and(greets_up, odd_tile))
    def _():
        lax.fori_loop(0, count, greet_above, 0)

    @pl.when(jnp.logical_and(greets_up, jnp.logical_not(odd_tile)))
    def _():
        hello({"tile": up})

    def greet_below(k, carry):
        hello({"tile": down, "layer": peer_of(k)})
        return carry

    @pl.when(first)
    def _():
        lax.fori_loop(0, count, greet_below, 0)


    loads[0].wait()
    tab[...] = jnp.ones(tab.shape, F32)
    tab[0:5, 0:classes] = table_v[...]
    t_a, t_n, t_r, t_s, t_k = (tab[j : j + 1, :] for j in range(5))
    derived = (
        t_n * jnp.log(t_a) * LOG2E,
        t_n * LOG2E,
        (1.0 / t_n - 1.0) * LOG2E,
        t_k,
        t_r,
        t_s - t_r,
    )
    for j, row in enumerate(derived):
        for k in range(classes):
            splat[j, k] = jnp.broadcast_to(row[:, k : k + 1], (8, LANES))

    def staged(c, f):
        return pl.ds(8 * TILES.index((c, f)), 8)

    for load in loads[1:4]:
        load.wait()

    def pack(b, carry):
        cols = pl.ds(pl.multiple_of(b * wide, wide), wide)
        for f, nat in enumerate((nat_h, nat_o, nat_t)):
            rows = [nat[8 * l : 8 * l + 8, cols] for l in range(depth)]
            if f == 2:
                rows = [r.astype(F32) for r in rows]
            for c, packed in enumerate(exchange(rows)):
                stage[staged(c, f), cols] = packed
        return carry

    lax.fori_loop(0, blocks, pack, 0)

    def params_of(texture, slot):
        def step(b, carry):
            cols = pl.ds(pl.multiple_of(b * wide, wide), wide)
            index = texture(cols).astype(jnp.int32)
            masks = bits(index, classes)
            for j in range(4):
                par_l[j, slot, :, cols] = lookup(splat, classes, j, index, masks)
            return carry

        lax.fori_loop(0, blocks, step, 0)

    greeted = count - 1 + jnp.where(last, count, 0)
    greeted = greeted + jnp.where(straight_down, count, jnp.where(greeted_below, 1, 0))
    pl.semaphore_wait(pltpu.get_barrier_semaphore(), greeted)

    def beside(side):
        return pltpu.make_async_remote_copy(
            src_ref=stage.at[staged(3 if side == 0 else 0, TEXTURE)],
            dst_ref=tex_h.at[side],
            send_sem=tex_send.at[side],
            recv_sem=tex_recv.at[side],
            device_id={"tile": up if side == 0 else down},
            device_id_type=MESH,
        )

    @pl.when(greeted_below)
    def _():
        beside(1).start()

    @pl.when(last)
    def _():
        beside(0).start()

    def rows_of(segments):
        start = 8 * sum(len(members) for members in SEGMENTS[: segments[0]])
        return pl.ds(start, 8 * sum(len(SEGMENTS[g]) for g in segments))

    def send_copies(copies):
        for g, segments in enumerate(copies):
            rows = rows_of(segments)

            def send_in(k, carry, g=g, rows=rows):
                peer = peer_of(k)
                pltpu.make_async_remote_copy(
                    src_ref=stage.at[rows, pl.ds(pl.multiple_of(peer * LANES, LANES), LANES)],
                    dst_ref=colb.at[me, rows],
                    send_sem=in_send.at[g],
                    recv_sem=in_recv.at[g],
                    device_id={"layer": peer},
                    device_id_type=MESH,
                ).start()
                return carry

            lax.fori_loop(0, count - 1, send_in, 0)

    def others(copies, g, sems):
        part = colb.at[pl.ds(0, count - 1), rows_of(copies[g])]
        pltpu.make_async_copy(part, part, sems.at[g]).wait()

    def in_border(usual, border):
        pl.when(jnp.logical_not(last))(usual)
        pl.when(last)(border)

    in_border(lambda: send_copies(USUAL), lambda: send_copies(BORDER))
    colb[me] = stage[:, my_cols]

    for c in range(CHUNKS):
        params_of(lambda cols, c=c: stage[staged(c, TEXTURE), cols], c + 1)

    loads[5].wait()
    loads[6].wait()
    tab[0:1, 0 : rates.shape[1]] = rate_v[...]
    inflow = jnp.take_along_axis(
        jnp.broadcast_to(tab[0:1, :], (8, LANES)), zone_v[...], axis=1, mode="promise_in_bounds"
    )
    for c in range(CHUNKS):
        ghost[c] = pltpu.roll(inflow, (6 - 2 * c) % 8, 0)

    loads[4].wait()
    inv = inv_v[...]
    inv_hi = inv.astype(jnp.bfloat16)
    inv_lo = (inv - inv_hi.astype(F32)).astype(jnp.bfloat16)
    inv_all = jnp.concatenate([inv_hi, inv_lo, inv_hi], axis=1)

    shape = (count, 8, LANES)
    sub3 = lax.broadcasted_iota(jnp.int32, shape, 1)

    def below(x):
        last = pltpu.roll(x[count - 1 :], 2, 1)
        return pltpu.roll(jnp.where(sub3 < 2, jnp.concatenate([x[1:], last], axis=0), x), 6, 1)

    def field(c, f, at):
        row = 8 * TILES.index((c, f))
        return colb[at, row : row + 8, :]

    def column_params(c):
        group = 4

        def step(i, carry):
            at = pl.ds(i * group, group)
            index = field(c, TEXTURE, at).astype(jnp.int32)
            masks = bits(index, classes)
            values = [lookup(splat, classes, j, index, masks) for j in range(6)]
            for j in range(6):
                par_c[c, j, at] = values[j]
            sat = saturation(field(c, OLD, at), values[0], values[1], values[2])
            mold_c[c, at] = values[4] + values[5] * sat
            return carry

        lax.fori_loop(0, count // group, step, 0)

    def newton(p):
        chunks = PAIRS[p]
        for i, c in enumerate(chunks):
            hcur[p, :, 8 * i : 8 * i + 8, :] = field(c, HEAD, slice(None))

        def step(_, carry):
            for i, c in enumerate(chunks):
                h = hcur[p, :, 8 * i : 8 * i + 8, :]
                sat = saturation(h, par_c[c, 0], par_c[c, 1], par_c[c, 2])
                k = par_c[c, 3] * (sat * sat * sat)
                flux = (0.5 * (k + below(k))) * (h - below(h) + 1.0)
                shifted = jnp.concatenate([ghost[c][None], flux[:-1]], axis=0)
                above_it = pltpu.roll(jnp.where(sub3 >= 6, shifted, flux), 2, 1)
                moisture = par_c[c, 4] + par_c[c, 5] * sat
                misfit = (moisture - mold_c[c]) + (flux - above_it)
                mis_c[i] = misfit.reshape(count * 8, LANES)
            parts = [(i, y) for i in range(len(chunks)) for y in range(2)]
            x = jnp.concatenate([mis_c[i, pl.ds(y, layers, stride=2), :] for i, y in parts], axis=1)
            hi = x.astype(jnp.bfloat16)
            lo = (x - hi.astype(F32)).astype(jnp.bfloat16)
            stacked = jnp.concatenate([hi, hi, lo], axis=0)
            update = jnp.dot(inv_all, stacked, preferred_element_type=F32)
            for j, (i, y) in enumerate(parts):
                upd_c[i, pl.ds(y, layers, stride=2), :] = update[:, j * LANES : (j + 1) * LANES]
            for i in range(len(chunks)):
                rows = slice(8 * i, 8 * i + 8)
                hcur[p, :, rows, :] = hcur[p, :, rows, :] - upd_c[i].reshape(shape)
            return carry

        lax.fori_loop(0, ITERS, step, 0)

    def slot_rows(s):
        return pl.ds(8 * PLACES.index(s), 8)

    def pair_rows(p):
        return pl.ds(8 * PLACES.index(PAIRS[p][0] + 1), 16)

    def send_back(p):
        def send(k, carry):
            peer = peer_of(k)
            pltpu.make_async_remote_copy(
                src_ref=hcur.at[p, peer],
                dst_ref=lay.at[pair_rows(p), my_cols],
                send_sem=back_send.at[p],
                recv_sem=back_recv.at[p],
                device_id={"layer": peer},
                device_id_type=MESH,
            ).start()
            return carry

        lax.fori_loop(0, count - 1, send, 0)
        lay[pair_rows(p), my_cols] = hcur[p, me]

    def landed(p):
        part = lay.at[pair_rows(p), pl.ds(0, (count - 1) * LANES)]
        pltpu.make_async_copy(part, part, back_recv.at[p]).wait()

    def forward(c, slot, side):
        return pltpu.make_async_remote_copy(
            src_ref=lay.at[slot_rows(c + 1)],
            dst_ref=lay.at[slot_rows(slot)],
            send_sem=halo_send.at[side],
            recv_sem=halo_recv.at[side],
            device_id={"tile": up if side == 0 else down},
            device_id_type=MESH,
        )

    heads_up, heads_down = forward(3, 0, 0), forward(0, CHUNKS + 1, 1)
    in_border(lambda: others(USUAL, 0, in_recv), lambda: others(BORDER, 0, in_recv))
    for c in PAIRS[0]:
        column_params(c)

    @pl.when(jnp.logical_not(last))
    def _():
        for c in PAIRS[1]:
            column_params(c)

    pl.when(jnp.logical_not(last))(lambda: others(USUAL, 1, in_recv))
    newton(0)

    def send_straight(row, slot, side, device):
        def send(k, carry):
            peer = peer_of(k)
            pltpu.make_async_remote_copy(
                src_ref=hcur.at[0, peer, pl.ds(row, 8)],
                dst_ref=lay.at[slot_rows(slot), my_cols],
                send_sem=halo_send.at[side],
                recv_sem=halo_recv.at[side],
                device_id={"tile": device, "layer": peer},
                device_id_type=MESH,
            ).start()
            return carry

        lax.fori_loop(0, count, send, 0)

    @pl.when(last)
    def _():
        send_straight(0, 0, 0, up)

    @pl.when(straight_down)
    def _():
        send_straight(8, CHUNKS + 1, 1, down)

    pl.when(jnp.logical_not(last))(lambda: send_back(0))

    @pl.when(last)
    def _():
        others(BORDER, 1, in_recv)
        for c in PAIRS[1]:
            column_params(c)
        send_back(0)
        others(BORDER, 2, in_recv)

    pl.when(jnp.logical_not(last))(lambda: others(USUAL, 2, in_recv))
    newton(1)
    send_back(1)

    @pl.when(greets_up)
    def _():
        beside(1).wait_recv()
        beside(0).start()

    landed(0)

    @pl.when(greets_up)
    def _():
        heads_up.start()


    @pl.when(first)
    def _():
        beside(0).wait_recv()
        beside(1).start()

    @pl.when(jnp.logical_and(beneath, jnp.logical_not(straight_down)))
    def _():
        heads_down.start()

    @pl.when(jnp.logical_not(beneath))
    def _():
        tex_h[0] = jnp.zeros(tex_h.shape[1:], F32)
        lay[slot_rows(0)] = lay[slot_rows(1)]

    @pl.when(jnp.logical_not(above))
    def _():
        tex_h[1] = jnp.zeros(tex_h.shape[1:], F32)
        lay[slot_rows(CHUNKS + 1)] = lay[slot_rows(CHUNKS)]

    def odd_rows(shape):
        return (lax.broadcasted_iota(jnp.int32, shape, 0) & 1) == 1

    def head(src, s, cols):
        return src[slot_rows(s), cols] if src is lay else src[s, :, cols]

    def prepare(src, dst, s):
        h = head(src, s, slice(None))
        sat = saturation(h, par_l[0, s], par_l[1, s], par_l[2, s])
        k = par_l[3, s] * (sat * sat * sat)
        odd = odd_rows(h.shape)
        other_h = jnp.where(odd, pltpu.roll(h, 1, 0), pltpu.roll(h, 7, 0))
        other_k = jnp.where(odd, pltpu.roll(k, 1, 0), pltpu.roll(k, 7, 0))
        dst[0, s] = k
        dst[1, s] = other_h
        dst[2, s] = other_k
        if src is lay2 and s in (0, CHUNKS + 1):
            return
        lane = lax.broadcasted_iota(jnp.int32, h.shape, 1)
        flow = (k + pltpu.roll(k, width - 1, 1)) * (pltpu.roll(h, width - 1, 1) - h)
        flow = jnp.where(lane == width - 1, 0.0, flow)
        dst[3, s] = flow - pltpu.roll(flow, 1, 1) + (k + other_k) * (other_h - h)

    def advanced(src, by, s, cols):
        h, k = head(src, s, cols), by[0, s, :, cols]
        odd = odd_rows(h.shape)
        after, before = min(s + 1, CHUNKS + 1), max(s - 1, 0)
        side_h = jnp.where(odd, by[1, after, :, cols], by[1, before, :, cols])
        side_k = jnp.where(odd, by[2, after, :, cols], by[2, before, :, cols])
        side = (k + side_k) * (side_h - h)
        if s == 1:
            side = jnp.where(jnp.logical_and(tile == 0, jnp.logical_not(odd)), 0.0, side)
        if s == CHUNKS:
            side = jnp.where(jnp.logical_and(tile == tiles - 1, odd), 0.0, side)
        return h + (0.5 * OMEGA) * (by[3, s, :, cols] + side)

    def advance(src, by, dst, s):
        dst[s] = advanced(src, by, s, slice(None))

    prepare(lay, ready, 4)
    prepare(lay, ready, 1)

    @pl.when(last)
    def _():
        beside(1).wait_recv()

    params_of(lambda cols: tex_h[1, :, cols], 5)

    @pl.when(greeted_below)
    def _():
        beside(0).wait_recv()

    params_of(lambda cols: tex_h[0, :, cols], 0)
    landed(1)
    prepare(lay, ready, 2)
    prepare(lay, ready, 3)
    for s in (2, 3):
        advance(lay, ready, lay2, s)
        prepare(lay2, ready2, s)

    @pl.when(above)
    def _():
        heads_down.wait_recv()

    prepare(lay, ready, 5)
    for s in (4, 5):
        advance(lay, ready, lay2, s)
        prepare(lay2, ready2, s)

    @pl.when(beneath)
    def _():
        heads_up.wait_recv()

    prepare(lay, ready, 0)
    for s in (0, 1):
        advance(lay, ready, lay2, s)
        prepare(lay2, ready2, s)

    def finish(b, carry):
        cols = pl.ds(pl.multiple_of(b * wide, wide), wide)
        tops = [advanced(lay2, ready2, c + 1, cols) for c in range(CHUNKS)]
        for l, rows in enumerate(exchange(tops)):
            nat_h[8 * l : 8 * l + 8, cols] = rows
        pltpu.make_async_copy(nat_h.at[:, cols], out.at[:, cols], load_sem.at[7]).start()
        return carry

    lax.fori_loop(0, blocks, finish, 0)
    def sent(copies):
        for g in range(len(copies)):
            others(copies, g, in_send)

    in_border(lambda: sent(USUAL), lambda: sent(BORDER))
    for p in range(len(PAIRS)):
        part = hcur.at[p, pl.ds(0, count - 1)]
        pltpu.make_async_copy(part, part, back_send.at[p]).wait()

    @pl.when(above)
    def _():
        heads_up.wait_send()
        beside(0).wait_send()

    @pl.when(beneath)
    def _():
        heads_down.wait_send()
        beside(1).wait_send()

    pltpu.make_async_copy(nat_h, out, load_sem.at[7]).wait()


def body(pressure, old_pressure, texture, zones, rates, vg_table, approx_inverse):
    count = lax.axis_size("layer")
    tiles = lax.axis_size("tile")
    depth, tall, width = pressure.shape
    rows = depth * tall
    flat = (rows, width)
    slots = (CHUNKS + 2, 2 * depth, width)
    column = (count, 2 * depth, LANES)
    classes = vg_table.shape[1]

    def vmem(*shape, dtype=F32):
        return pltpu.VMEM(shape, dtype)

    result = pl.pallas_call(
        functools.partial(kernel, count, tiles),
        out_shape=jax.ShapeDtypeStruct(flat, F32),
        in_specs=[pl.BlockSpec(memory_space=pltpu.HBM)] * 7,
        out_specs=pl.BlockSpec(memory_space=pltpu.HBM),
        scratch_shapes=[
            vmem(*flat),
            vmem(*flat),
            vmem(*flat, dtype=jnp.int32),
            vmem(CHUNKS * FIELDS * 2 * depth, width),
            vmem(count, len(TILES) * 2 * depth, LANES),
            vmem(len(PAIRS), count, 4 * depth, LANES),
            vmem(CHUNKS, 6, *column),
            vmem(CHUNKS, *column),
            vmem(2, count * 2 * depth, LANES),
            vmem(2, count * 2 * depth, LANES),
            vmem(CHUNKS, 8, LANES),
            vmem((CHUNKS + 2) * 2 * depth, width),
            vmem(*slots),
            vmem(4, *slots),
            vmem(4, *slots),
            vmem(4, *slots),
            vmem(2, 2 * depth, width),
            vmem(tall, LANES, dtype=jnp.int32),
            vmem(1, rates.shape[0]),
            vmem(*vg_table.shape),
            vmem(8, LANES),
            vmem(6, classes, 8, LANES),
            vmem(*approx_inverse.shape),
            pltpu.SemaphoreType.DMA((8,)),
            pltpu.SemaphoreType.DMA((len(BORDER),)),
            pltpu.SemaphoreType.DMA((len(BORDER),)),
            pltpu.SemaphoreType.DMA((len(PAIRS),)),
            pltpu.SemaphoreType.DMA((len(PAIRS),)),
            pltpu.SemaphoreType.DMA((2,)),
            pltpu.SemaphoreType.DMA((2,)),
            pltpu.SemaphoreType.DMA((2,)),
            pltpu.SemaphoreType.DMA((2,)),
        ],
        compiler_params=pltpu.CompilerParams(
            collective_id=0, has_side_effects=True, vmem_limit_bytes=56 * 1024 * 1024
        ),
    )(
        pressure.reshape(flat),
        old_pressure.reshape(flat),
        texture.reshape(flat),
        zones,
        rates.reshape(1, -1),
        vg_table,
        approx_inverse,
    )
    return result.reshape(pressure.shape)


def solution(mesh):
    placed = (
        P("layer", "tile", None),
        P("layer", "tile", None),
        P("layer", "tile", None),
        P("tile", None),
        P(),
        P(),
        P(),
    )
    return jax.shard_map(
        body, mesh=mesh, in_specs=placed, out_specs=P("layer", "tile", None), check_vma=False
    )
```

```python
import functools

import jax
import jax.numpy as jnp
from jax import lax
from jax.experimental import pallas as pl
from jax.experimental.pallas import tpu as pltpu
from jax.sharding import PartitionSpec as P

ITERS = 3
OMEGA = 0.2
LOG2E = 1.4426950408889634
MESH = pl.DeviceIdType.MESH
LANES = 128
CHUNKS = 4
FIELDS = 3
HEAD, OLD, TEXTURE = range(FIELDS)
SEGMENTS = (
    tuple((c, f) for c in (1, 2) for f in (TEXTURE, OLD)),
    tuple((c, f) for c in (3, 0) for f in (TEXTURE, OLD)),
    tuple((c, HEAD) for c in (3, 0)),
    tuple((c, HEAD) for c in (1, 2)),
)
TILES = sum(SEGMENTS, ())
COPIES = ((1, 2), (0,), (3,))
PAIRS = ((3, 0), (1, 2))
PLACES = (0, 4, 1, 2, 3, 5)
SIDE = 4
TURNS = sorted(
    range(1, SIDE * SIDE),
    key=lambda v: (not v & 2, -(v % SIDE) - min(v // SIDE, SIDE - v // SIDE)),
)
F32 = jnp.float32


def words(values):
    packed = [sum(v << (4 * i) for i, v in enumerate(values[j : j + 8])) for j in (0, 8)]
    return [w - (1 << 32) if w >= 1 << 31 else w for w in packed]


TURN_WORDS = words(TURNS + [0])


def turn(k):
    word = jnp.where(k < 8, jnp.int32(TURN_WORDS[0]), jnp.int32(TURN_WORDS[1]))
    return lax.shift_right_logical(word, 4 * lax.rem(k, 8)) & (SIDE * SIDE - 1)


def saturation(head, la, n, negp):
    suction = jnp.log(1.0 + jnp.exp2(jnp.abs(head) * (-LOG2E))) + jnp.maximum(-head, 0.0)
    power = jnp.exp2(n * jnp.log(suction) + la)
    return jnp.exp2(negp * jnp.log(1.0 + power))


def exchange(tiles):
    sub = lax.broadcasted_iota(jnp.int32, tiles[0].shape, 0)
    low, even = sub < 4, (sub & 2) == 0
    a, b, c, d = tiles

    def halves(p, q):
        r = pltpu.roll(jnp.where(low, q, p), 4, 0)
        return jnp.where(low, p, r), jnp.where(low, r, q)

    def pairs(p, q):
        return (
            jnp.where(even, p, pltpu.roll(q, 2, 0)),
            jnp.where(even, pltpu.roll(p, 6, 0), q),
        )

    a, c = halves(a, c)
    b, d = halves(b, d)
    a, b = pairs(a, b)
    c, d = pairs(c, d)
    return a, b, c, d


def lookup(splat, classes, row, index, masks):
    def constant(k):
        tile = splat[row, min(k, classes - 1)]
        if len(index.shape) == 2:
            return jnp.concatenate([tile] * (index.shape[1] // LANES), axis=1)
        return jnp.broadcast_to(tile[None], index.shape)

    level = [constant(k) for k in range(classes)]
    for mask in masks:
        level = [
            jnp.where(mask, level[k + 1], level[k]) if k + 1 < len(level) else level[k]
            for k in range(0, len(level), 2)
        ]
    return level[0]


def bits(index, classes):
    return [(index & (1 << b)) != 0 for b in range((classes - 1).bit_length())]


def kernel(
    count,
    tiles,
    press,
    old,
    tex,
    zones,
    rates,
    table,
    inverse,
    out,
    nat_h,
    nat_o,
    nat_t,
    stage,
    colb,
    hcur,
    par_c,
    mold_c,
    mis_c,
    upd_c,
    ghost,
    lay,
    lay2,
    ready,
    ready2,
    par_l,
    tex_h,
    zone_v,
    rate_v,
    table_v,
    tab,
    splat,
    inv_v,
    load_sem,
    in_send,
    in_recv,
    back_send,
    back_recv,
    halo_send,
    halo_recv,
    tex_send,
    tex_recv,
):
    me = lax.axis_index("layer")
    tile = lax.axis_index("tile")
    width = press.shape[1]
    depth = press.shape[0] // 8
    classes = table.shape[1]
    layers = count * depth
    down = lax.rem(tile + tiles - 1, tiles)
    up = lax.rem(tile + 1, tiles)
    wide = 512
    blocks = width // wide

    def peer_of(k):
        return jnp.bitwise_xor(me, turn(k))

    run = tiles // 2
    my_cols = pl.ds(pl.multiple_of(me * LANES, LANES), LANES)
    loads = [
        pltpu.make_async_copy(table, table_v, load_sem.at[0]),
        pltpu.make_async_copy(press, nat_h, load_sem.at[1]),
        pltpu.make_async_copy(old, nat_o, load_sem.at[2]),
        pltpu.make_async_copy(tex, nat_t, load_sem.at[3]),
        pltpu.make_async_copy(inverse, inv_v, load_sem.at[4]),
        pltpu.make_async_copy(zones.at[:, my_cols], zone_v, load_sem.at[5]),
        pltpu.make_async_copy(rates, rate_v, load_sem.at[6]),
    ]
    for load in loads:
        load.start()

    above, beneath = tile != tiles - 1, tile != 0
    last, first = tile == run - 1, tile == run
    greets_up = jnp.logical_and(above, jnp.logical_not(last))
    greeted_below = jnp.logical_and(beneath, jnp.logical_not(first))
    odd_tile = lax.rem(tile, 2) == 1
    straight_down = jnp.logical_and(greeted_below, jnp.logical_not(odd_tile))

    def hello(device):
        pl.semaphore_signal(
            pltpu.get_barrier_semaphore(), inc=1, device_id=device, device_id_type=MESH
        )

    def greet(k, carry):
        hello({"layer": peer_of(k)})
        return carry

    lax.fori_loop(0, count - 1, greet, 0)

    def greet_above(k, carry):
        hello({"tile": up, "layer": peer_of(k)})
        return carry

    @pl.when(jnp.logical_and(greets_up, odd_tile))
    def _():
        lax.fori_loop(0, count, greet_above, 0)

    @pl.when(jnp.logical_and(greets_up, jnp.logical_not(odd_tile)))
    def _():
        hello({"tile": up})

    def greet_below(k, carry):
        hello({"tile": down, "layer": peer_of(k)})
        return carry

    @pl.when(first)
    def _():
        lax.fori_loop(0, count, greet_below, 0)


    loads[0].wait()
    tab[...] = jnp.ones(tab.shape, F32)
    tab[0:5, 0:classes] = table_v[...]
    t_a, t_n, t_r, t_s, t_k = (tab[j : j + 1, :] for j in range(5))
    derived = (
        t_n * jnp.log(t_a) * LOG2E,
        t_n * LOG2E,
        (1.0 / t_n - 1.0) * LOG2E,
        t_k,
        t_r,
        t_s - t_r,
    )
    for j, row in enumerate(derived):
        for k in range(classes):
            splat[j, k] = jnp.broadcast_to(row[:, k : k + 1], (8, LANES))

    def staged(c, f):
        return pl.ds(8 * TILES.index((c, f)), 8)

    for load in loads[1:4]:
        load.wait()

    def pack(b, carry):
        cols = pl.ds(pl.multiple_of(b * wide, wide), wide)
        for f, nat in enumerate((nat_h, nat_o, nat_t)):
            rows = [nat[8 * l : 8 * l + 8, cols] for l in range(depth)]
            if f == 2:
                rows = [r.astype(F32) for r in rows]
            for c, packed in enumerate(exchange(rows)):
                stage[staged(c, f), cols] = packed
        return carry

    lax.fori_loop(0, blocks, pack, 0)

    def params_of(texture, slot):
        def step(b, carry):
            cols = pl.ds(pl.multiple_of(b * wide, wide), wide)
            index = texture(cols).astype(jnp.int32)
            masks = bits(index, classes)
            for j in range(4):
                par_l[j, slot, :, cols] = lookup(splat, classes, j, index, masks)
            return carry

        lax.fori_loop(0, blocks, step, 0)

    greeted = count - 1 + jnp.where(last, count, 0)
    greeted = greeted + jnp.where(straight_down, count, jnp.where(greeted_below, 1, 0))
    pl.semaphore_wait(pltpu.get_barrier_semaphore(), greeted)

    def beside(side):
        return pltpu.make_async_remote_copy(
            src_ref=stage.at[staged(3 if side == 0 else 0, TEXTURE)],
            dst_ref=tex_h.at[side],
            send_sem=tex_send.at[side],
            recv_sem=tex_recv.at[side],
            device_id={"tile": up if side == 0 else down},
            device_id_type=MESH,
        )

    @pl.when(greeted_below)
    def _():
        beside(1).start()

    @pl.when(last)
    def _():
        beside(0).start()

    def rows_of(segments):
        start = 8 * sum(len(members) for members in SEGMENTS[: segments[0]])
        return pl.ds(start, 8 * sum(len(SEGMENTS[g]) for g in segments))

    for g, segments in enumerate(COPIES):
        rows = rows_of(segments)

        def send_in(k, carry, g=g, rows=rows):
            peer = peer_of(k)
            pltpu.make_async_remote_copy(
                src_ref=stage.at[rows, pl.ds(pl.multiple_of(peer * LANES, LANES), LANES)],
                dst_ref=colb.at[me, rows],
                send_sem=in_send.at[g],
                recv_sem=in_recv.at[g],
                device_id={"layer": peer},
                device_id_type=MESH,
            ).start()
            return carry

        lax.fori_loop(0, count - 1, send_in, 0)

    def others(g, sems):
        part = colb.at[pl.ds(0, count - 1), rows_of(COPIES[g])]
        pltpu.make_async_copy(part, part, sems.at[g]).wait()

    colb[me] = stage[:, my_cols]

    for c in range(CHUNKS):
        params_of(lambda cols, c=c: stage[staged(c, TEXTURE), cols], c + 1)

    loads[5].wait()
    loads[6].wait()
    tab[0:1, 0 : rates.shape[1]] = rate_v[...]
    inflow = jnp.take_along_axis(
        jnp.broadcast_to(tab[0:1, :], (8, LANES)), zone_v[...], axis=1, mode="promise_in_bounds"
    )
    for c in range(CHUNKS):
        ghost[c] = pltpu.roll(inflow, (6 - 2 * c) % 8, 0)

    loads[4].wait()
    inv = inv_v[...]
    inv_hi = inv.astype(jnp.bfloat16)
    inv_lo = (inv - inv_hi.astype(F32)).astype(jnp.bfloat16)
    inv_all = jnp.concatenate([inv_hi, inv_lo, inv_hi], axis=1)

    shape = (count, 8, LANES)
    sub3 = lax.broadcasted_iota(jnp.int32, shape, 1)

    def below(x):
        last = pltpu.roll(x[count - 1 :], 2, 1)
        return pltpu.roll(jnp.where(sub3 < 2, jnp.concatenate([x[1:], last], axis=0), x), 6, 1)

    def field(c, f, at):
        row = 8 * TILES.index((c, f))
        return colb[at, row : row + 8, :]

    def column_params(c):
        group = 4

        def step(i, carry):
            at = pl.ds(i * group, group)
            index = field(c, TEXTURE, at).astype(jnp.int32)
            masks = bits(index, classes)
            values = [lookup(splat, classes, j, index, masks) for j in range(6)]
            for j in range(6):
                par_c[c, j, at] = values[j]
            sat = saturation(field(c, OLD, at), values[0], values[1], values[2])
            mold_c[c, at] = values[4] + values[5] * sat
            return carry

        lax.fori_loop(0, count // group, step, 0)

    def newton(p):
        chunks = PAIRS[p]
        for i, c in enumerate(chunks):
            hcur[p, :, 8 * i : 8 * i + 8, :] = field(c, HEAD, slice(None))

        def step(_, carry):
            for i, c in enumerate(chunks):
                h = hcur[p, :, 8 * i : 8 * i + 8, :]
                sat = saturation(h, par_c[c, 0], par_c[c, 1], par_c[c, 2])
                k = par_c[c, 3] * (sat * sat * sat)
                flux = (0.5 * (k + below(k))) * (h - below(h) + 1.0)
                shifted = jnp.concatenate([ghost[c][None], flux[:-1]], axis=0)
                above_it = pltpu.roll(jnp.where(sub3 >= 6, shifted, flux), 2, 1)
                moisture = par_c[c, 4] + par_c[c, 5] * sat
                misfit = (moisture - mold_c[c]) + (flux - above_it)
                mis_c[i] = misfit.reshape(count * 8, LANES)
            parts = [(i, y) for i in range(len(chunks)) for y in range(2)]
            x = jnp.concatenate([mis_c[i, pl.ds(y, layers, stride=2), :] for i, y in parts], axis=1)
            hi = x.astype(jnp.bfloat16)
            lo = (x - hi.astype(F32)).astype(jnp.bfloat16)
            stacked = jnp.concatenate([hi, hi, lo], axis=0)
            update = jnp.dot(inv_all, stacked, preferred_element_type=F32)
            for j, (i, y) in enumerate(parts):
                upd_c[i, pl.ds(y, layers, stride=2), :] = update[:, j * LANES : (j + 1) * LANES]
            for i in range(len(chunks)):
                rows = slice(8 * i, 8 * i + 8)
                hcur[p, :, rows, :] = hcur[p, :, rows, :] - upd_c[i].reshape(shape)
            return carry

        lax.fori_loop(0, ITERS, step, 0)

    def slot_rows(s):
        return pl.ds(8 * PLACES.index(s), 8)

    def pair_rows(p):
        return pl.ds(8 * PLACES.index(PAIRS[p][0] + 1), 16)

    def send_back(p):
        def send(k, carry):
            peer = peer_of(k)
            pltpu.make_async_remote_copy(
                src_ref=hcur.at[p, peer],
                dst_ref=lay.at[pair_rows(p), my_cols],
                send_sem=back_send.at[p],
                recv_sem=back_recv.at[p],
                device_id={"layer": peer},
                device_id_type=MESH,
            ).start()
            return carry

        lax.fori_loop(0, count - 1, send, 0)
        lay[pair_rows(p), my_cols] = hcur[p, me]

    def landed(p):
        part = lay.at[pair_rows(p), pl.ds(0, (count - 1) * LANES)]
        pltpu.make_async_copy(part, part, back_recv.at[p]).wait()

    def forward(c, slot, side):
        return pltpu.make_async_remote_copy(
            src_ref=lay.at[slot_rows(c + 1)],
            dst_ref=lay.at[slot_rows(slot)],
            send_sem=halo_send.at[side],
            recv_sem=halo_recv.at[side],
            device_id={"tile": up if side == 0 else down},
            device_id_type=MESH,
        )

    heads_up, heads_down = forward(3, 0, 0), forward(0, CHUNKS + 1, 1)
    others(0, in_recv)
    for c in PAIRS[0]:
        column_params(c)

    newton(0)

    def send_straight(row, slot, side, device):
        def send(k, carry):
            peer = peer_of(k)
            pltpu.make_async_remote_copy(
                src_ref=hcur.at[0, peer, pl.ds(row, 8)],
                dst_ref=lay.at[slot_rows(slot), my_cols],
                send_sem=halo_send.at[side],
                recv_sem=halo_recv.at[side],
                device_id={"tile": device, "layer": peer},
                device_id_type=MESH,
            ).start()
            return carry

        lax.fori_loop(0, count, send, 0)

    @pl.when(last)
    def _():
        send_straight(0, 0, 0, up)

    @pl.when(straight_down)
    def _():
        send_straight(8, CHUNKS + 1, 1, down)


    others(1, in_recv)
    for c in PAIRS[1]:
        column_params(c)
    send_back(0)
    others(2, in_recv)

    newton(1)
    send_back(1)

    @pl.when(greets_up)
    def _():
        beside(1).wait_recv()
        beside(0).start()

    landed(0)

    @pl.when(greets_up)
    def _():
        heads_up.start()


    @pl.when(first)
    def _():
        beside(0).wait_recv()
        beside(1).start()

    @pl.when(jnp.logical_and(beneath, jnp.logical_not(straight_down)))
    def _():
        heads_down.start()

    @pl.when(jnp.logical_not(beneath))
    def _():
        tex_h[0] = jnp.zeros(tex_h.shape[1:], F32)
        lay[slot_rows(0)] = lay[slot_rows(1)]

    @pl.when(jnp.logical_not(above))
    def _():
        tex_h[1] = jnp.zeros(tex_h.shape[1:], F32)
        lay[slot_rows(CHUNKS + 1)] = lay[slot_rows(CHUNKS)]

    def odd_rows(shape):
        return (lax.broadcasted_iota(jnp.int32, shape, 0) & 1) == 1

    def head(src, s, cols):
        return src[slot_rows(s), cols] if src is lay else src[s, :, cols]

    def prepare(src, dst, s):
        h = head(src, s, slice(None))
        sat = saturation(h, par_l[0, s], par_l[1, s], par_l[2, s])
        k = par_l[3, s] * (sat * sat * sat)
        odd = odd_rows(h.shape)
        other_h = jnp.where(odd, pltpu.roll(h, 1, 0), pltpu.roll(h, 7, 0))
        other_k = jnp.where(odd, pltpu.roll(k, 1, 0), pltpu.roll(k, 7, 0))
        dst[0, s] = k
        dst[1, s] = other_h
        dst[2, s] = other_k
        if src is lay2 and s in (0, CHUNKS + 1):
            return
        lane = lax.broadcasted_iota(jnp.int32, h.shape, 1)
        flow = (k + pltpu.roll(k, width - 1, 1)) * (pltpu.roll(h, width - 1, 1) - h)
        flow = jnp.where(lane == width - 1, 0.0, flow)
        dst[3, s] = flow - pltpu.roll(flow, 1, 1) + (k + other_k) * (other_h - h)

    def advanced(src, by, s, cols):
        h, k = head(src, s, cols), by[0, s, :, cols]
        odd = odd_rows(h.shape)
        after, before = min(s + 1, CHUNKS + 1), max(s - 1, 0)
        side_h = jnp.where(odd, by[1, after, :, cols], by[1, before, :, cols])
        side_k = jnp.where(odd, by[2, after, :, cols], by[2, before, :, cols])
        side = (k + side_k) * (side_h - h)
        if s == 1:
            side = jnp.where(jnp.logical_and(tile == 0, jnp.logical_not(odd)), 0.0, side)
        if s == CHUNKS:
            side = jnp.where(jnp.logical_and(tile == tiles - 1, odd), 0.0, side)
        return h + (0.5 * OMEGA) * (by[3, s, :, cols] + side)

    def advance(src, by, dst, s):
        dst[s] = advanced(src, by, s, slice(None))

    prepare(lay, ready, 4)
    prepare(lay, ready, 1)

    @pl.when(last)
    def _():
        beside(1).wait_recv()

    params_of(lambda cols: tex_h[1, :, cols], 5)

    @pl.when(greeted_below)
    def _():
        beside(0).wait_recv()

    params_of(lambda cols: tex_h[0, :, cols], 0)
    landed(1)
    prepare(lay, ready, 2)
    prepare(lay, ready, 3)
    for s in (2, 3):
        advance(lay, ready, lay2, s)
        prepare(lay2, ready2, s)

    @pl.when(above)
    def _():
        heads_down.wait_recv()

    prepare(lay, ready, 5)
    for s in (4, 5):
        advance(lay, ready, lay2, s)
        prepare(lay2, ready2, s)

    @pl.when(beneath)
    def _():
        heads_up.wait_recv()

    prepare(lay, ready, 0)
    for s in (0, 1):
        advance(lay, ready, lay2, s)
        prepare(lay2, ready2, s)

    def finish(b, carry):
        cols = pl.ds(pl.multiple_of(b * wide, wide), wide)
        tops = [advanced(lay2, ready2, c + 1, cols) for c in range(CHUNKS)]
        for l, rows in enumerate(exchange(tops)):
            nat_h[8 * l : 8 * l + 8, cols] = rows
        pltpu.make_async_copy(nat_h.at[:, cols], out.at[:, cols], load_sem.at[7]).start()
        return carry

    lax.fori_loop(0, blocks, finish, 0)
    for g in range(len(COPIES)):
        others(g, in_send)
    for p in range(len(PAIRS)):
        part = hcur.at[p, pl.ds(0, count - 1)]
        pltpu.make_async_copy(part, part, back_send.at[p]).wait()

    @pl.when(above)
    def _():
        heads_up.wait_send()
        beside(0).wait_send()

    @pl.when(beneath)
    def _():
        heads_down.wait_send()
        beside(1).wait_send()

    pltpu.make_async_copy(nat_h, out, load_sem.at[7]).wait()


def body(pressure, old_pressure, texture, zones, rates, vg_table, approx_inverse):
    count = lax.axis_size("layer")
    tiles = lax.axis_size("tile")
    depth, tall, width = pressure.shape
    rows = depth * tall
    flat = (rows, width)
    slots = (CHUNKS + 2, 2 * depth, width)
    column = (count, 2 * depth, LANES)
    classes = vg_table.shape[1]

    def vmem(*shape, dtype=F32):
        return pltpu.VMEM(shape, dtype)

    result = pl.pallas_call(
        functools.partial(kernel, count, tiles),
        out_shape=jax.ShapeDtypeStruct(flat, F32),
        in_specs=[pl.BlockSpec(memory_space=pltpu.HBM)] * 7,
        out_specs=pl.BlockSpec(memory_space=pltpu.HBM),
        scratch_shapes=[
            vmem(*flat),
            vmem(*flat),
            vmem(*flat, dtype=jnp.int32),
            vmem(CHUNKS * FIELDS * 2 * depth, width),
            vmem(count, len(TILES) * 2 * depth, LANES),
            vmem(len(PAIRS), count, 4 * depth, LANES),
            vmem(CHUNKS, 6, *column),
            vmem(CHUNKS, *column),
            vmem(2, count * 2 * depth, LANES),
            vmem(2, count * 2 * depth, LANES),
            vmem(CHUNKS, 8, LANES),
            vmem((CHUNKS + 2) * 2 * depth, width),
            vmem(*slots),
            vmem(4, *slots),
            vmem(4, *slots),
            vmem(4, *slots),
            vmem(2, 2 * depth, width),
            vmem(tall, LANES, dtype=jnp.int32),
            vmem(1, rates.shape[0]),
            vmem(*vg_table.shape),
            vmem(8, LANES),
            vmem(6, classes, 8, LANES),
            vmem(*approx_inverse.shape),
            pltpu.SemaphoreType.DMA((8,)),
            pltpu.SemaphoreType.DMA((len(COPIES),)),
            pltpu.SemaphoreType.DMA((len(COPIES),)),
            pltpu.SemaphoreType.DMA((len(PAIRS),)),
            pltpu.SemaphoreType.DMA((len(PAIRS),)),
            pltpu.SemaphoreType.DMA((2,)),
            pltpu.SemaphoreType.DMA((2,)),
            pltpu.SemaphoreType.DMA((2,)),
            pltpu.SemaphoreType.DMA((2,)),
        ],
        compiler_params=pltpu.CompilerParams(
            collective_id=0, has_side_effects=True, vmem_limit_bytes=56 * 1024 * 1024
        ),
    )(
        pressure.reshape(flat),
        old_pressure.reshape(flat),
        texture.reshape(flat),
        zones,
        rates.reshape(1, -1),
        vg_table,
        approx_inverse,
    )
    return result.reshape(pressure.shape)


def solution(mesh):
    placed = (
        P("layer", "tile", None),
        P("layer", "tile", None),
        P("layer", "tile", None),
        P("tile", None),
        P(),
        P(),
        P(),
    )
    return jax.shard_map(
        body, mesh=mesh, in_specs=placed, out_specs=P("layer", "tile", None), check_vma=False
    )
```

```python
import functools

import jax
import jax.numpy as jnp
from jax import lax
from jax.experimental import pallas as pl
from jax.experimental.pallas import tpu as pltpu
from jax.sharding import PartitionSpec as P

ITERS = 3
OMEGA = 0.2
LOG2E = 1.4426950408889634
MESH = pl.DeviceIdType.MESH
LANES = 128
CHUNKS = 4
FIELDS = 3
HEAD, OLD, TEXTURE = range(FIELDS)
SEGMENTS = (
    tuple((c, f) for c in (1, 2) for f in (TEXTURE, OLD)),
    tuple((c, f) for c in (3, 0) for f in (TEXTURE, OLD)),
    tuple((c, HEAD) for c in (3, 0)),
    tuple((c, HEAD) for c in (1, 2)),
)
TILES = sum(SEGMENTS, ())
COPIES = ((1, 2), (0,), (3,))
PAIRS = ((3, 0), (1, 2))
PLACES = (0, 4, 1, 2, 3, 5)
SIDE = 4
TURNS = sorted(
    range(1, SIDE * SIDE),
    key=lambda v: (not v & 2, -(v % SIDE) - min(v // SIDE, SIDE - v // SIDE)),
)
F32 = jnp.float32


def words(values):
    packed = [sum(v << (4 * i) for i, v in enumerate(values[j : j + 8])) for j in (0, 8)]
    return [w - (1 << 32) if w >= 1 << 31 else w for w in packed]


TURN_WORDS = words(TURNS + [0])


def turn(k):
    word = jnp.where(k < 8, jnp.int32(TURN_WORDS[0]), jnp.int32(TURN_WORDS[1]))
    return lax.shift_right_logical(word, 4 * lax.rem(k, 8)) & (SIDE * SIDE - 1)


def saturation(head, la, n, negp):
    suction = jnp.log(1.0 + jnp.exp2(jnp.abs(head) * (-LOG2E))) + jnp.maximum(-head, 0.0)
    power = jnp.exp2(n * jnp.log(suction) + la)
    return jnp.exp2(negp * jnp.log(1.0 + power))


def exchange(tiles):
    sub = lax.broadcasted_iota(jnp.int32, tiles[0].shape, 0)
    low, even = sub < 4, (sub & 2) == 0
    a, b, c, d = tiles

    def halves(p, q):
        r = pltpu.roll(jnp.where(low, q, p), 4, 0)
        return jnp.where(low, p, r), jnp.where(low, r, q)

    def pairs(p, q):
        return (
            jnp.where(even, p, pltpu.roll(q, 2, 0)),
            jnp.where(even, pltpu.roll(p, 6, 0), q),
        )

    a, c = halves(a, c)
    b, d = halves(b, d)
    a, b = pairs(a, b)
    c, d = pairs(c, d)
    return a, b, c, d


def lookup(splat, classes, row, index, masks):
    def constant(k):
        tile = splat[row, min(k, classes - 1)]
        if len(index.shape) == 2:
            return jnp.concatenate([tile] * (index.shape[1] // LANES), axis=1)
        return jnp.broadcast_to(tile[None], index.shape)

    level = [constant(k) for k in range(classes)]
    for mask in masks:
        level = [
            jnp.where(mask, level[k + 1], level[k]) if k + 1 < len(level) else level[k]
            for k in range(0, len(level), 2)
        ]
    return level[0]


def bits(index, classes):
    return [(index & (1 << b)) != 0 for b in range((classes - 1).bit_length())]


def kernel(
    count,
    tiles,
    press,
    old,
    tex,
    zones,
    rates,
    table,
    inverse,
    out,
    nat_h,
    nat_o,
    nat_t,
    stage,
    colb,
    hcur,
    par_c,
    mold_c,
    mis_c,
    upd_c,
    ghost,
    lay,
    lay2,
    ready,
    ready2,
    par_l,
    tex_h,
    zone_v,
    rate_v,
    table_v,
    tab,
    splat,
    inv_v,
    load_sem,
    in_send,
    in_recv,
    back_send,
    back_recv,
    halo_send,
    halo_recv,
    tex_send,
    tex_recv,
):
    me = lax.axis_index("layer")
    tile = lax.axis_index("tile")
    width = press.shape[1]
    depth = press.shape[0] // 8
    classes = table.shape[1]
    layers = count * depth
    down = lax.rem(tile + tiles - 1, tiles)
    up = lax.rem(tile + 1, tiles)
    wide = 1024
    blocks = width // wide

    def peer_of(k):
        return jnp.bitwise_xor(me, turn(k))

    run = tiles // 2
    my_cols = pl.ds(pl.multiple_of(me * LANES, LANES), LANES)
    loads = [
        pltpu.make_async_copy(table, table_v, load_sem.at[0]),
        pltpu.make_async_copy(press, nat_h, load_sem.at[1]),
        pltpu.make_async_copy(old, nat_o, load_sem.at[2]),
        pltpu.make_async_copy(tex, nat_t, load_sem.at[3]),
        pltpu.make_async_copy(inverse, inv_v, load_sem.at[4]),
        pltpu.make_async_copy(zones.at[:, my_cols], zone_v, load_sem.at[5]),
        pltpu.make_async_copy(rates, rate_v, load_sem.at[6]),
    ]
    for load in loads:
        load.start()

    above, beneath = tile != tiles - 1, tile != 0
    last, first = tile == run - 1, tile == run
    greets_up = jnp.logical_and(above, jnp.logical_not(last))
    greeted_below = jnp.logical_and(beneath, jnp.logical_not(first))
    odd_tile = lax.rem(tile, 2) == 1
    straight_down = jnp.logical_and(greeted_below, jnp.logical_not(odd_tile))

    def hello(device):
        pl.semaphore_signal(
            pltpu.get_barrier_semaphore(), inc=1, device_id=device, device_id_type=MESH
        )

    def greet(k, carry):
        hello({"layer": peer_of(k)})
        return carry

    lax.fori_loop(0, count - 1, greet, 0)

    def greet_above(k, carry):
        hello({"tile": up, "layer": peer_of(k)})
        return carry

    @pl.when(jnp.logical_and(greets_up, odd_tile))
    def _():
        lax.fori_loop(0, count, greet_above, 0)

    @pl.when(jnp.logical_and(greets_up, jnp.logical_not(odd_tile)))
    def _():
        hello({"tile": up})

    def greet_below(k, carry):
        hello({"tile": down, "layer": peer_of(k)})
        return carry

    @pl.when(first)
    def _():
        lax.fori_loop(0, count, greet_below, 0)


    loads[0].wait()
    tab[...] = jnp.ones(tab.shape, F32)
    tab[0:5, 0:classes] = table_v[...]
    t_a, t_n, t_r, t_s, t_k = (tab[j : j + 1, :] for j in range(5))
    derived = (
        t_n * jnp.log(t_a) * LOG2E,
        t_n * LOG2E,
        (1.0 / t_n - 1.0) * LOG2E,
        t_k,
        t_r,
        t_s - t_r,
    )
    for j, row in enumerate(derived):
        for k in range(classes):
            splat[j, k] = jnp.broadcast_to(row[:, k : k + 1], (8, LANES))

    def staged(c, f):
        return pl.ds(8 * TILES.index((c, f)), 8)

    for load in loads[1:4]:
        load.wait()

    def pack(b, carry):
        cols = pl.ds(pl.multiple_of(b * wide, wide), wide)
        for f, nat in enumerate((nat_h, nat_o, nat_t)):
            rows = [nat[8 * l : 8 * l + 8, cols] for l in range(depth)]
            if f == 2:
                rows = [r.astype(F32) for r in rows]
            for c, packed in enumerate(exchange(rows)):
                stage[staged(c, f), cols] = packed
        return carry

    lax.fori_loop(0, blocks, pack, 0)

    def params_of(texture, slot):
        def step(b, carry):
            cols = pl.ds(pl.multiple_of(b * wide, wide), wide)
            index = texture(cols).astype(jnp.int32)
            masks = bits(index, classes)
            for j in range(4):
                par_l[j, slot, :, cols] = lookup(splat, classes, j, index, masks)
            return carry

        lax.fori_loop(0, blocks, step, 0)

    greeted = count - 1 + jnp.where(last, count, 0)
    greeted = greeted + jnp.where(straight_down, count, jnp.where(greeted_below, 1, 0))
    pl.semaphore_wait(pltpu.get_barrier_semaphore(), greeted)

    def beside(side):
        return pltpu.make_async_remote_copy(
            src_ref=stage.at[staged(3 if side == 0 else 0, TEXTURE)],
            dst_ref=tex_h.at[side],
            send_sem=tex_send.at[side],
            recv_sem=tex_recv.at[side],
            device_id={"tile": up if side == 0 else down},
            device_id_type=MESH,
        )

    @pl.when(greeted_below)
    def _():
        beside(1).start()

    @pl.when(last)
    def _():
        beside(0).start()

    def rows_of(segments):
        start = 8 * sum(len(members) for members in SEGMENTS[: segments[0]])
        return pl.ds(start, 8 * sum(len(SEGMENTS[g]) for g in segments))

    for g, segments in enumerate(COPIES):
        rows = rows_of(segments)

        def send_in(k, carry, g=g, rows=rows):
            peer = peer_of(k)
            pltpu.make_async_remote_copy(
                src_ref=stage.at[rows, pl.ds(pl.multiple_of(peer * LANES, LANES), LANES)],
                dst_ref=colb.at[me, rows],
                send_sem=in_send.at[g],
                recv_sem=in_recv.at[g],
                device_id={"layer": peer},
                device_id_type=MESH,
            ).start()
            return carry

        lax.fori_loop(0, count - 1, send_in, 0)

    def others(g, sems):
        part = colb.at[pl.ds(0, count - 1), rows_of(COPIES[g])]
        pltpu.make_async_copy(part, part, sems.at[g]).wait()

    colb[me] = stage[:, my_cols]

    for c in range(CHUNKS):
        params_of(lambda cols, c=c: stage[staged(c, TEXTURE), cols], c + 1)

    loads[5].wait()
    loads[6].wait()
    tab[0:1, 0 : rates.shape[1]] = rate_v[...]
    inflow = jnp.take_along_axis(
        jnp.broadcast_to(tab[0:1, :], (8, LANES)), zone_v[...], axis=1, mode="promise_in_bounds"
    )
    for c in range(CHUNKS):
        ghost[c] = pltpu.roll(inflow, (6 - 2 * c) % 8, 0)

    loads[4].wait()
    inv = inv_v[...]
    inv_hi = inv.astype(jnp.bfloat16)
    inv_lo = (inv - inv_hi.astype(F32)).astype(jnp.bfloat16)
    inv_all = jnp.concatenate([inv_hi, inv_lo, inv_hi], axis=1)

    shape = (count, 8, LANES)
    sub3 = lax.broadcasted_iota(jnp.int32, shape, 1)

    def below(x):
        last = pltpu.roll(x[count - 1 :], 2, 1)
        return pltpu.roll(jnp.where(sub3 < 2, jnp.concatenate([x[1:], last], axis=0), x), 6, 1)

    def field(c, f, at):
        row = 8 * TILES.index((c, f))
        return colb[at, row : row + 8, :]

    def column_params(c):
        group = 4

        def step(i, carry):
            at = pl.ds(i * group, group)
            index = field(c, TEXTURE, at).astype(jnp.int32)
            masks = bits(index, classes)
            values = [lookup(splat, classes, j, index, masks) for j in range(6)]
            for j in range(6):
                par_c[c, j, at] = values[j]
            sat = saturation(field(c, OLD, at), values[0], values[1], values[2])
            mold_c[c, at] = values[4] + values[5] * sat
            return carry

        lax.fori_loop(0, count // group, step, 0)

    def newton(p):
        chunks = PAIRS[p]
        for i, c in enumerate(chunks):
            hcur[p, :, 8 * i : 8 * i + 8, :] = field(c, HEAD, slice(None))

        def step(_, carry):
            for i, c in enumerate(chunks):
                h = hcur[p, :, 8 * i : 8 * i + 8, :]
                sat = saturation(h, par_c[c, 0], par_c[c, 1], par_c[c, 2])
                k = par_c[c, 3] * (sat * sat * sat)
                flux = (0.5 * (k + below(k))) * (h - below(h) + 1.0)
                shifted = jnp.concatenate([ghost[c][None], flux[:-1]], axis=0)
                above_it = pltpu.roll(jnp.where(sub3 >= 6, shifted, flux), 2, 1)
                moisture = par_c[c, 4] + par_c[c, 5] * sat
                misfit = (moisture - mold_c[c]) + (flux - above_it)
                mis_c[i] = misfit.reshape(count * 8, LANES)
            parts = [(i, y) for i in range(len(chunks)) for y in range(2)]
            x = jnp.concatenate([mis_c[i, pl.ds(y, layers, stride=2), :] for i, y in parts], axis=1)
            hi = x.astype(jnp.bfloat16)
            lo = (x - hi.astype(F32)).astype(jnp.bfloat16)
            stacked = jnp.concatenate([hi, hi, lo], axis=0)
            update = jnp.dot(inv_all, stacked, preferred_element_type=F32)
            for j, (i, y) in enumerate(parts):
                upd_c[i, pl.ds(y, layers, stride=2), :] = update[:, j * LANES : (j + 1) * LANES]
            for i in range(len(chunks)):
                rows = slice(8 * i, 8 * i + 8)
                hcur[p, :, rows, :] = hcur[p, :, rows, :] - upd_c[i].reshape(shape)
            return carry

        lax.fori_loop(0, ITERS, step, 0)

    def slot_rows(s):
        return pl.ds(8 * PLACES.index(s), 8)

    def pair_rows(p):
        return pl.ds(8 * PLACES.index(PAIRS[p][0] + 1), 16)

    def send_back(p):
        def send(k, carry):
            peer = peer_of(k)
            pltpu.make_async_remote_copy(
                src_ref=hcur.at[p, peer],
                dst_ref=lay.at[pair_rows(p), my_cols],
                send_sem=back_send.at[p],
                recv_sem=back_recv.at[p],
                device_id={"layer": peer},
                device_id_type=MESH,
            ).start()
            return carry

        lax.fori_loop(0, count - 1, send, 0)
        lay[pair_rows(p), my_cols] = hcur[p, me]

    def landed(p):
        part = lay.at[pair_rows(p), pl.ds(0, (count - 1) * LANES)]
        pltpu.make_async_copy(part, part, back_recv.at[p]).wait()

    def forward(c, slot, side):
        return pltpu.make_async_remote_copy(
            src_ref=lay.at[slot_rows(c + 1)],
            dst_ref=lay.at[slot_rows(slot)],
            send_sem=halo_send.at[side],
            recv_sem=halo_recv.at[side],
            device_id={"tile": up if side == 0 else down},
            device_id_type=MESH,
        )

    heads_up, heads_down = forward(3, 0, 0), forward(0, CHUNKS + 1, 1)
    others(0, in_recv)
    for c in PAIRS[0]:
        column_params(c)

    newton(0)

    def send_straight(row, slot, side, device):
        def send(k, carry):
            peer = peer_of(k)
            pltpu.make_async_remote_copy(
                src_ref=hcur.at[0, peer, pl.ds(row, 8)],
                dst_ref=lay.at[slot_rows(slot), my_cols],
                send_sem=halo_send.at[side],
                recv_sem=halo_recv.at[side],
                device_id={"tile": device, "layer": peer},
                device_id_type=MESH,
            ).start()
            return carry

        lax.fori_loop(0, count, send, 0)

    @pl.when(last)
    def _():
        send_straight(0, 0, 0, up)

    @pl.when(straight_down)
    def _():
        send_straight(8, CHUNKS + 1, 1, down)


    others(1, in_recv)
    for c in PAIRS[1]:
        column_params(c)
    send_back(0)
    others(2, in_recv)

    newton(1)
    send_back(1)

    @pl.when(greets_up)
    def _():
        beside(1).wait_recv()
        beside(0).start()

    landed(0)

    @pl.when(greets_up)
    def _():
        heads_up.start()


    @pl.when(first)
    def _():
        beside(0).wait_recv()
        beside(1).start()

    @pl.when(jnp.logical_and(beneath, jnp.logical_not(straight_down)))
    def _():
        heads_down.start()

    @pl.when(jnp.logical_not(beneath))
    def _():
        tex_h[0] = jnp.zeros(tex_h.shape[1:], F32)
        lay[slot_rows(0)] = lay[slot_rows(1)]

    @pl.when(jnp.logical_not(above))
    def _():
        tex_h[1] = jnp.zeros(tex_h.shape[1:], F32)
        lay[slot_rows(CHUNKS + 1)] = lay[slot_rows(CHUNKS)]

    def odd_rows(shape):
        return (lax.broadcasted_iota(jnp.int32, shape, 0) & 1) == 1

    def head(src, s, cols):
        return src[slot_rows(s), cols] if src is lay else src[s, :, cols]

    def prepare(src, dst, s):
        h = head(src, s, slice(None))
        sat = saturation(h, par_l[0, s], par_l[1, s], par_l[2, s])
        k = par_l[3, s] * (sat * sat * sat)
        odd = odd_rows(h.shape)
        other_h = jnp.where(odd, pltpu.roll(h, 1, 0), pltpu.roll(h, 7, 0))
        other_k = jnp.where(odd, pltpu.roll(k, 1, 0), pltpu.roll(k, 7, 0))
        dst[0, s] = k
        dst[1, s] = other_h
        dst[2, s] = other_k
        if src is lay2 and s in (0, CHUNKS + 1):
            return
        lane = lax.broadcasted_iota(jnp.int32, h.shape, 1)
        flow = (k + pltpu.roll(k, width - 1, 1)) * (pltpu.roll(h, width - 1, 1) - h)
        flow = jnp.where(lane == width - 1, 0.0, flow)
        dst[3, s] = flow - pltpu.roll(flow, 1, 1) + (k + other_k) * (other_h - h)

    def advanced(src, by, s, cols):
        h, k = head(src, s, cols), by[0, s, :, cols]
        odd = odd_rows(h.shape)
        after, before = min(s + 1, CHUNKS + 1), max(s - 1, 0)
        side_h = jnp.where(odd, by[1, after, :, cols], by[1, before, :, cols])
        side_k = jnp.where(odd, by[2, after, :, cols], by[2, before, :, cols])
        side = (k + side_k) * (side_h - h)
        if s == 1:
            side = jnp.where(jnp.logical_and(tile == 0, jnp.logical_not(odd)), 0.0, side)
        if s == CHUNKS:
            side = jnp.where(jnp.logical_and(tile == tiles - 1, odd), 0.0, side)
        return h + (0.5 * OMEGA) * (by[3, s, :, cols] + side)

    def advance(src, by, dst, s):
        dst[s] = advanced(src, by, s, slice(None))

    prepare(lay, ready, 4)
    prepare(lay, ready, 1)

    @pl.when(last)
    def _():
        beside(1).wait_recv()

    params_of(lambda cols: tex_h[1, :, cols], 5)

    @pl.when(greeted_below)
    def _():
        beside(0).wait_recv()

    params_of(lambda cols: tex_h[0, :, cols], 0)
    landed(1)
    prepare(lay, ready, 2)
    prepare(lay, ready, 3)
    for s in (2, 3):
        advance(lay, ready, lay2, s)
        prepare(lay2, ready2, s)

    @pl.when(above)
    def _():
        heads_down.wait_recv()

    prepare(lay, ready, 5)
    for s in (4, 5):
        advance(lay, ready, lay2, s)
        prepare(lay2, ready2, s)

    @pl.when(beneath)
    def _():
        heads_up.wait_recv()

    prepare(lay, ready, 0)
    for s in (0, 1):
        advance(lay, ready, lay2, s)
        prepare(lay2, ready2, s)

    def finish(b, carry):
        cols = pl.ds(pl.multiple_of(b * wide, wide), wide)
        tops = [advanced(lay2, ready2, c + 1, cols) for c in range(CHUNKS)]
        for l, rows in enumerate(exchange(tops)):
            nat_h[8 * l : 8 * l + 8, cols] = rows
        pltpu.make_async_copy(nat_h.at[:, cols], out.at[:, cols], load_sem.at[7]).start()
        return carry

    lax.fori_loop(0, blocks, finish, 0)
    for g in range(len(COPIES)):
        others(g, in_send)
    for p in range(len(PAIRS)):
        part = hcur.at[p, pl.ds(0, count - 1)]
        pltpu.make_async_copy(part, part, back_send.at[p]).wait()

    @pl.when(above)
    def _():
        heads_up.wait_send()
        beside(0).wait_send()

    @pl.when(beneath)
    def _():
        heads_down.wait_send()
        beside(1).wait_send()

    pltpu.make_async_copy(nat_h, out, load_sem.at[7]).wait()


def body(pressure, old_pressure, texture, zones, rates, vg_table, approx_inverse):
    count = lax.axis_size("layer")
    tiles = lax.axis_size("tile")
    depth, tall, width = pressure.shape
    rows = depth * tall
    flat = (rows, width)
    slots = (CHUNKS + 2, 2 * depth, width)
    column = (count, 2 * depth, LANES)
    classes = vg_table.shape[1]

    def vmem(*shape, dtype=F32):
        return pltpu.VMEM(shape, dtype)

    result = pl.pallas_call(
        functools.partial(kernel, count, tiles),
        out_shape=jax.ShapeDtypeStruct(flat, F32),
        in_specs=[pl.BlockSpec(memory_space=pltpu.HBM)] * 7,
        out_specs=pl.BlockSpec(memory_space=pltpu.HBM),
        scratch_shapes=[
            vmem(*flat),
            vmem(*flat),
            vmem(*flat, dtype=jnp.int32),
            vmem(CHUNKS * FIELDS * 2 * depth, width),
            vmem(count, len(TILES) * 2 * depth, LANES),
            vmem(len(PAIRS), count, 4 * depth, LANES),
            vmem(CHUNKS, 6, *column),
            vmem(CHUNKS, *column),
            vmem(2, count * 2 * depth, LANES),
            vmem(2, count * 2 * depth, LANES),
            vmem(CHUNKS, 8, LANES),
            vmem((CHUNKS + 2) * 2 * depth, width),
            vmem(*slots),
            vmem(4, *slots),
            vmem(4, *slots),
            vmem(4, *slots),
            vmem(2, 2 * depth, width),
            vmem(tall, LANES, dtype=jnp.int32),
            vmem(1, rates.shape[0]),
            vmem(*vg_table.shape),
            vmem(8, LANES),
            vmem(6, classes, 8, LANES),
            vmem(*approx_inverse.shape),
            pltpu.SemaphoreType.DMA((8,)),
            pltpu.SemaphoreType.DMA((len(COPIES),)),
            pltpu.SemaphoreType.DMA((len(COPIES),)),
            pltpu.SemaphoreType.DMA((len(PAIRS),)),
            pltpu.SemaphoreType.DMA((len(PAIRS),)),
            pltpu.SemaphoreType.DMA((2,)),
            pltpu.SemaphoreType.DMA((2,)),
            pltpu.SemaphoreType.DMA((2,)),
            pltpu.SemaphoreType.DMA((2,)),
        ],
        compiler_params=pltpu.CompilerParams(
            collective_id=0, has_side_effects=True, vmem_limit_bytes=56 * 1024 * 1024
        ),
    )(
        pressure.reshape(flat),
        old_pressure.reshape(flat),
        texture.reshape(flat),
        zones,
        rates.reshape(1, -1),
        vg_table,
        approx_inverse,
    )
    return result.reshape(pressure.shape)


def solution(mesh):
    placed = (
        P("layer", "tile", None),
        P("layer", "tile", None),
        P("layer", "tile", None),
        P("tile", None),
        P(),
        P(),
        P(),
    )
    return jax.shard_map(
        body, mesh=mesh, in_specs=placed, out_specs=P("layer", "tile", None), check_vma=False
    )
```
